32 devices in a mesh: row: 4 (over y, x), seq: 8 (over z, core).
Axes of the slice: x: 2, y: 2, z: 4, core: 2. Of those that a mesh axis runs over, the one named last changes fastest.
Arguments:
- signal: bfloat16 [4, 16384, 512], P('row', 'seq'), may hold values from -6 to 6
- condition: bfloat16 [4, 16384, 80], P('row', 'seq'), may hold values from -6 to 6
- lengths: int32 [4, 4], P('row'), may hold values from 1 to 15360, 16384 in all within a row
- owner: int32 [256], replicated, may hold values from 0 to 255, each once
- grad_out: bfloat16 [4, 16384, 512], P('row', 'seq'), may hold values from -6 to 6
- grad_skip: bfloat16 [4, 16384, 512], P('row', 'seq'), may hold values from -6 to 6
- w_in: float32 [256, 69, 128], P(('row', 'seq')), may hold values from -0.1875 to 0.1875
- w_out: float32 [256, 64, 64], P(('row', 'seq')), may hold values from -0.75 to 0.75
- left_in: float32 [256, 69, 69], P(('row', 'seq')), as said below
- right_in: float32 [256, 128, 128], P(('row', 'seq')), as said below
- root_left_in: float32 [256, 69, 69], P(('row', 'seq')), as said below
- root_right_in: float32 [256, 128, 128], P(('row', 'seq')), as said below
- left_out: float32 [256, 64, 64], P(('row', 'seq')), as said below
- right_out: float32 [256, 64, 64], P(('row', 'seq')), as said below
- root_left_out: float32 [256, 64, 64], P(('row', 'seq')), as said below
- root_right_out: float32 [256, 64, 64], P(('row', 'seq')), as said below
Outputs:
- out_x: float32 [4, 16384, 512], P('row', 'seq')
- skip_sum: float32 [4, 16384, 512], P('row', 'seq')
- grad_x: float32 [4, 16384, 512], P('row', 'seq')
- grad_cond: float32 [4, 16384, 80], P('row', 'seq')
- grad_in_blocks: float32 [256, 69, 128], P(('row', 'seq'))
- grad_out_blocks: float32 [256, 64, 64], P(('row', 'seq'))
- new_left_in: float32 [256, 69, 69], P(('row', 'seq'))
- new_right_in: float32 [256, 128, 128], P(('row', 'seq'))
- new_left_out: float32 [256, 64, 64], P(('row', 'seq'))
- new_right_out: float32 [256, 64, 64], P(('row', 'seq'))
- new_w_in: float32 [256, 69, 128], P(('row', 'seq'))
- new_w_out: float32 [256, 64, 64], P(('row', 'seq'))
The draws below stay inside these ranges and needn't reach their ends.
Inputs may be any that keep to these rules, and one draw needn't show every extreme that they name: `lengths`: each packed row is filled exactly; its longest utterance has exactly 15360 samples. `owner`: a permutation of the block numbers. `left_in`: symmetric matrices. `right_in`: symmetric matrices. `root_left_in`: symmetric matrices. `root_right_in`: symmetric matrices. `left_out`: symmetric matrices. `right_out`: symmetric matrices. `root_left_out`: symmetric matrices. `root_right_out`: symmetric matrices.
All inputs are finite; a program needn't handle non-finite values.
Results may differ from the reference program's by a relative error of at most 0.0086.
Values may be sent and summed in bfloat16 or wider, within the bound.
A program may use at most 256 MiB of HBM per device.

```python
import math
import jax
import jax.numpy as jnp
import numpy as np
from jax import lax

R = 512
S = 512
M = 80
FIRST_DILATION = 512
UTTS = 4
NBLK = 256
TOK_DEV = 2048
KIN = 1104
H = 512
BIR = 69
BIC = 128
BOR = 64
BOC = 64
SPAN = 16384
PACKS = 4
TOKENS = 65536


def statistic(key, size, factor, low_end, high_end):
    diag_key, off_key = jax.random.split(key)
    log_values = jax.random.uniform(diag_key, (NBLK, size), jnp.float32, math.log(low_end), math.log(high_end))
    spread = jax.random.normal(off_key, (NBLK, size, size), jnp.float32)
    off_part = (spread + jnp.swapaxes(spread, 1, 2)) * (0.42 * factor / math.sqrt(size))
    identity = jnp.eye(size, dtype=jnp.float32)
    return off_part * (1.0 - identity) + (jnp.exp(log_values) * factor)[:, :, None] * identity


def entry_in():
    return 2.25 * TOKENS


def entry_out():
    return 0.16 * TOKENS


def draw_left_in(key, part):
    key = jax.random.fold_in(key, 11)
    return statistic(key, BIR, BIC * entry_in(), 1.0, 4.0)


def draw_right_in(key, part):
    key = jax.random.fold_in(key, 12)
    return statistic(key, BIC, BIR * entry_in(), 1.0, 4.0)


def draw_root_left_in(key, part):
    key = jax.random.fold_in(key, 13)
    return statistic(key, BIR, (BIC * entry_in()) ** (-0.25), 0.5, 1.0)


def draw_root_right_in(key, part):
    key = jax.random.fold_in(key, 14)
    return statistic(key, BIC, (BIR * entry_in()) ** (-0.25), 0.5, 1.0)


def draw_left_out(key, part):
    key = jax.random.fold_in(key, 15)
    return statistic(key, BOR, BOC * entry_out(), 1.0, 4.0)


def draw_right_out(key, part):
    key = jax.random.fold_in(key, 16)
    return statistic(key, BOC, BOR * entry_out(), 1.0, 4.0)


def draw_root_left_out(key, part):
    key = jax.random.fold_in(key, 17)
    return statistic(key, BOR, (BOC * entry_out()) ** (-0.25), 0.5, 1.0)


def draw_root_right_out(key, part):
    key = jax.random.fold_in(key, 18)
    return statistic(key, BOC, (BOR * entry_out()) ** (-0.25), 0.5, 1.0)


def level_of(stream_key, dims, pieces, low, largest):
    loudness, own = 1.0, jax.random.fold_in(stream_key, 6)
    for axis_at, parts in pieces:
        draws = jnp.exp(jax.random.uniform(jax.random.fold_in(own, axis_at), (parts,), jnp.float32, low / len(pieces), largest / len(pieces)))
        loudness = loudness * jnp.repeat(draws, dims[axis_at] // parts).reshape([-1 if axis == axis_at else 1 for axis in range(len(dims))])
    return loudness


def length_profile(count, total, bound, slope):
    loads = [(1 << 20) // math.isqrt(standing ** slope) + 1 for standing in range(2, count + 1)]
    spare, counts = total - bound - (count - 1), [1] * (count - 1)
    while spare > 0:
        free = [i for i in range(count - 1) if counts[i] < bound]
        pool, remaining = sum([loads[i] for i in free]), spare
        for i in free:
            addition = min(bound - counts[i], max(1, remaining * loads[i] // pool), spare)
            counts[i] = counts[i] + addition
            spare = spare - addition
    return np.array([bound] + counts)


def uneven(rng, number_of, total, reach, lean):
    if number_of == 2:
        one = jax.random.randint(rng, (), max(1, total - reach), min(reach, total - 1) + 1)
        return jnp.stack([one, total - one])
    tallies = jnp.asarray(length_profile(number_of, total, reach, lean), jnp.int32)
    pairs = (number_of - 1) // 2
    giver, taker = tallies[1:1 + 2 * pairs:2], tallies[2:2 + 2 * pairs:2]
    margin = jnp.minimum(giver - 1, reach - taker)
    shifted = jax.random.randint(jax.random.fold_in(rng, 1), (pairs,), 0, 1 << 20) % (margin + 1)
    tallies = tallies.at[1:1 + 2 * pairs:2].set(giver - shifted).at[2:2 + 2 * pairs:2].set(taker + shifted)
    return tallies[jax.random.permutation(jax.random.fold_in(rng, 2), number_of)]


def gaussian(stream_key, shape, scale, most, pieces=(), held_as=jnp.bfloat16):
    level = level_of(stream_key, shape, pieces, -0.22, 0.18) if pieces else 1.0
    array = jax.random.normal(stream_key, shape, jnp.float32) * scale * level
    return jnp.minimum(jnp.maximum(array, -most), most).astype(held_as)


def setup_inputs(seed: int = 0) -> dict:
    splits = jax.random.split(jax.random.key(seed), 17)
    signal = gaussian(splits[0], (PACKS, SPAN, R), 1.0, 6.0, ((0, 4), (1, 8)))
    condition = gaussian(splits[1], (PACKS, SPAN, M), 1.0, 6.0, ((0, 4), (1, 8)))
    lengths = jax.vmap(lambda own: uneven(own, UTTS, SPAN, SPAN - TOK_DEV // 2, 2))(jax.random.split(splits[2], PACKS)).reshape((PACKS, UTTS)).astype(jnp.int32)
    owner = jax.random.permutation(splits[3], NBLK).astype(jnp.int32)
    grad_out = gaussian(splits[4], (PACKS, SPAN, R), 1.0, 6.0, ((0, 4), (1, 8)))
    grad_skip = gaussian(splits[5], (PACKS, SPAN, S), 1.0, 6.0, ((0, 4), (1, 8)))
    w_in = gaussian(splits[6], (NBLK, BIR, BIC), KIN ** -0.5, 0.1875, ((0, 32),), jnp.float32)
    w_out = gaussian(splits[7], (NBLK, BOR, BOC), (H // 8) ** -0.5, 0.75, ((0, 32),), jnp.float32)
    left_in = draw_left_in(jax.random.fold_in(splits[16], 71), 0)
    right_in = draw_right_in(jax.random.fold_in(splits[16], 71), 0)
    root_left_in = draw_root_left_in(jax.random.fold_in(splits[16], 71), 0)
    root_right_in = draw_root_right_in(jax.random.fold_in(splits[16], 71), 0)
    left_out = draw_left_out(jax.random.fold_in(splits[16], 71), 0)
    right_out = draw_right_out(jax.random.fold_in(splits[16], 71), 0)
    root_left_out = draw_root_left_out(jax.random.fold_in(splits[16], 71), 0)
    root_right_out = draw_root_right_out(jax.random.fold_in(splits[16], 71), 0)
    return dict(signal=signal, condition=condition, lengths=lengths, owner=owner, grad_out=grad_out, grad_skip=grad_skip, w_in=w_in, w_out=w_out, left_in=left_in, right_in=right_in, root_left_in=root_left_in, root_right_in=root_right_in, left_out=left_out, right_out=right_out, root_left_out=root_left_out, root_right_out=root_right_out)


@jax.custom_vjp
def low(v):
    return lax.optimization_barrier(v.astype(jnp.bfloat16)).astype(jnp.float32)

@jax.custom_vjp
def low_back(v):
    return v

def low_keep(v):
    return (low(v), None)

def low_pass(kept, grad):
    return (grad,)

def back_keep(v):
    return (v, None)

def back_low(kept, grad):
    return (low(grad),)
low.defvjp(low_keep, low_pass)
low_back.defvjp(back_keep, back_low)
highest = lax.Precision.HIGHEST
rate_in = 0.3
rate_out = 1.0

def to_blocks(full, row_parts, col_parts):
    layers, rows, cols = full.shape
    shaped = full.reshape(layers, row_parts, rows // row_parts, col_parts, cols // col_parts)
    return shaped.transpose(0, 1, 3, 2, 4).reshape(layers * row_parts * col_parts, rows // row_parts, cols // col_parts)

def from_blocks(blocks, row_parts, col_parts):
    count, block_rows, block_cols = blocks.shape
    layers = count // (row_parts * col_parts)
    shaped = blocks.reshape(layers, row_parts, col_parts, block_rows, block_cols)
    return shaped.transpose(0, 1, 3, 2, 4).reshape(layers, row_parts * block_rows, col_parts * block_cols)

def receptive_mask(utterance_lengths_row, sample_positions, dilation):
    ends = jnp.cumsum(utterance_lengths_row).astype(jnp.int32)
    starts = lax.optimization_barrier(jnp.sum(jnp.where(ends[None, :] <= sample_positions[:, None], utterance_lengths_row[None, :], 0), axis=1)).astype(jnp.int32)
    return (sample_positions - dilation >= starts).astype(jnp.float32)

def gated_wavenet_layer(optimizer_state, conditioning_row, input_weight, output_weight, valid, dilation):
    width = optimizer_state.shape[1]
    rounded = low(optimizer_state)
    delayed = jnp.concatenate([jnp.zeros((dilation, width), jnp.float32), rounded[:-dilation]], axis=0) * valid[:, None]
    units = jnp.concatenate([delayed, rounded, conditioning_row], axis=1)
    pre = low_back(jnp.dot(units, input_weight, precision=highest))
    half = pre.shape[1] // 2
    hidden = low(jnp.tanh(pre[:, :half]) * jax.nn.sigmoid(pre[:, half:]))
    proj = low_back(jnp.dot(hidden, output_weight, precision=highest))
    return (optimizer_state + proj[:, :width], proj[:, width:])

def network(optimizer_state, conditioning_row, full_in, full_out, longer_mask, mask_short):
    input_weight = low(full_in)
    output_weight = low(full_out)
    first_layer_state, first_skip_output = gated_wavenet_layer(optimizer_state, conditioning_row, input_weight[0], output_weight[0], longer_mask, FIRST_DILATION)
    state_two, skip_two = gated_wavenet_layer(first_layer_state, conditioning_row, input_weight[1], output_weight[1], mask_short, 1)
    return (state_two, first_skip_output + skip_two)

def shampoo(grad, left, right, root_left, root_right, weight, rate):
    new_left = 0.5 * left + 0.5 * jnp.einsum('bij,bkj->bik', grad, grad, precision=highest)
    new_right = 0.5 * right + 0.5 * jnp.einsum('bji,bjk->bik', grad, grad, precision=highest)
    step = jnp.einsum('bij,bjk->bik', root_left, grad, precision=highest)
    step = jnp.einsum('bij,bjk->bik', step, root_right, precision=highest)
    return (new_left, new_right, weight - rate * step)

def reference(signal, condition, lengths, owner, grad_out, grad_skip, w_in, w_out, left_in, right_in, root_left_in, root_right_in, left_out, right_out, root_left_out, root_right_out):
    inverse = jnp.argsort(owner).astype(jnp.int32)
    full_in = from_blocks(jnp.take(w_in, inverse, axis=0), 16, 8)
    full_out = from_blocks(jnp.take(w_out, inverse, axis=0), 8, 16)
    sample_positions = jnp.arange(SPAN, dtype=jnp.int32)

    def per_pack(carry, items):
        signal_row, conditioning_row, utterance_lengths_row, out_cot, skip_cot = items
        longer_mask = receptive_mask(utterance_lengths_row, sample_positions, FIRST_DILATION)
        mask_short = receptive_mask(utterance_lengths_row, sample_positions, 1)

        def forward(optimizer_state, cond_value, input_weight, output_weight):
            return network(optimizer_state, cond_value, input_weight, output_weight, longer_mask, mask_short)
        primal, pullback = jax.vjp(forward, signal_row.astype(jnp.float32), conditioning_row.astype(jnp.float32), full_in, full_out)
        grad_state, grad_cond_row, grad_win, grad_wout = pullback((out_cot.astype(jnp.float32), skip_cot.astype(jnp.float32)))
        return ((carry[0] + grad_win, carry[1] + grad_wout), (primal[0], primal[1], grad_state, grad_cond_row))
    start_carry = (jnp.zeros(full_in.shape, jnp.float32), jnp.zeros(full_out.shape, jnp.float32))
    (grad_win, grad_wout), (out_x, skip_sum, grad_x, grad_cond) = lax.scan(per_pack, start_carry, (signal, condition, lengths, grad_out, grad_skip))
    grad_in_blocks = jnp.take(to_blocks(grad_win, 16, 8), owner, axis=0)
    grad_out_blocks = jnp.take(to_blocks(grad_wout, 8, 16), owner, axis=0)
    new_left_in, new_right_in, new_w_in = shampoo(grad_in_blocks, left_in, right_in, root_left_in, root_right_in, w_in, rate_in)
    new_left_out, new_right_out, new_w_out = shampoo(grad_out_blocks, left_out, right_out, root_left_out, root_right_out, w_out, rate_out)
    return (out_x, skip_sum, grad_x, grad_cond, grad_in_blocks, grad_out_blocks, new_left_in, new_right_in, new_left_out, new_right_out, new_w_in, new_w_out)
```

```python
import jax
import jax.numpy as jnp
from jax import lax
from jax.experimental import pallas as pl
from jax.experimental.pallas import tpu as pltpu
from jax.sharding import PartitionSpec as P

FIRST_DILATION = 512
MESH = pl.DeviceIdType.MESH
bf16, f32, i32 = jnp.bfloat16, jnp.float32, jnp.int32

highest = lax.Precision.HIGHEST
rate_in = 0.3
rate_out = 1.0

ROWS_IN = 576
ROWS_OUT = 256


def shifted(block, axis, distance):
    devices = range(lax.axis_size(axis))
    route = [(i - distance, i) for i in devices if i - distance in devices]
    return lax.ppermute(block, axis, route)


def to_blocks(full, row_parts, col_parts):
    layers, rows, cols = full.shape
    shaped = full.reshape(layers, row_parts, rows // row_parts, col_parts, cols // col_parts)
    return shaped.transpose(0, 1, 3, 2, 4).reshape(
        layers * row_parts * col_parts, rows // row_parts, cols // col_parts
    )


def from_blocks(blocks, row_parts, col_parts):
    count, block_rows, block_cols = blocks.shape
    layers = count // (row_parts * col_parts)
    shaped = blocks.reshape(layers, row_parts, col_parts, block_rows, block_cols)
    return shaped.transpose(0, 1, 3, 2, 4).reshape(
        layers, row_parts * block_rows, col_parts * block_cols
    )


def receptive_mask(lengths, sample_positions, dilation):
    ends = jnp.cumsum(lengths, axis=1)
    starts = jnp.sum(
        jnp.where(ends[:, None, :] <= sample_positions[None, :, None], lengths[:, None, :], 0),
        axis=2,
    )
    return sample_positions[None, :] - dilation >= starts


def gate_forward(units, input_weight, output_weight):
    pre = jnp.einsum("ptk,kg->ptg", units, input_weight, preferred_element_type=jnp.float32)
    half = pre.shape[2] // 2
    tanh_part = jnp.tanh(pre[..., :half])
    sigm_part = jax.nn.sigmoid(pre[..., half:])
    hidden = (tanh_part * sigm_part).astype(jnp.bfloat16)
    projected = jnp.einsum("ptg,gk->ptk", hidden, output_weight, preferred_element_type=jnp.float32)
    return (tanh_part, sigm_part, hidden, projected)


def gate_backward(
    units, tanh_part, sigm_part, hidden, input_weight, output_weight, grad_state, grad_skip
):
    grad_proj = jnp.concatenate([grad_state, grad_skip.astype(jnp.float32)], axis=2).astype(
        jnp.bfloat16
    )
    grad_wout = jnp.einsum("ptg,ptk->gk", hidden, grad_proj, preferred_element_type=jnp.float32)
    grad_hidden = jnp.einsum(
        "ptk,gk->ptg", grad_proj, output_weight, preferred_element_type=jnp.float32
    )
    grad_tanh = grad_hidden * sigm_part * (1.0 - tanh_part * tanh_part)
    grad_sigm = grad_hidden * tanh_part * sigm_part * (1.0 - sigm_part)
    grad_pre = jnp.concatenate([grad_tanh, grad_sigm], axis=2).astype(jnp.bfloat16)
    grad_win = jnp.einsum("ptk,ptg->kg", units, grad_pre, preferred_element_type=jnp.float32)
    grad_units = jnp.einsum(
        "ptg,kg->ptk", grad_pre, input_weight, preferred_element_type=jnp.float32
    )
    return (grad_win, grad_wout, grad_units)


def shampoo(grad, left, right, root_left, root_right, weight, rate):
    new_left = 0.5 * left + 0.5 * jnp.einsum("bij,bkj->bik", grad, grad, precision=highest)
    new_right = 0.5 * right + 0.5 * jnp.einsum("bji,bjk->bik", grad, grad, precision=highest)
    step = jnp.einsum("bij,bjk->bik", root_left, grad, precision=highest)
    step = jnp.einsum("bij,bjk->bik", step, root_right, precision=highest)
    return (new_left, new_right, weight - rate * step)


class Place:
    def __init__(self):
        self.row, self.seq = lax.axis_index("row"), lax.axis_index("seq")
        self.z, self.core = self.seq // 2, self.seq % 2
        x, y = self.row % 2, self.row // 2
        self.rows = (
            self.row,
            self.row + 1 - 2 * x,
            self.row + 2 - 4 * y,
            self.row + 3 - 2 * x - 4 * y,
        )
        self.x_peer = (self.rows[1], self.seq)
        self.y_peer = (self.rows[2], self.seq)
        self.sibling = (self.row, self.seq + 1 - 2 * self.core)
        low = self.z // 2
        near = self.z + low * (3 - 2 * self.z)
        self.others = [t + low * (3 - 2 * t) for t in (1 - near, 2, 3)]

    def z_peer(self, z):
        return (self.row, 2 * z + self.core)

    def owner(self, rel, z, core=None):
        core = self.core if core is None else core
        return self.rows[rel] * 8 + 2 * z + core

    def barrier(self, more=()):
        sem = pltpu.get_barrier_semaphore()
        peers = [self.x_peer, self.y_peer, self.sibling] + [self.z_peer(z) for z in self.others]
        for peer in peers + list(more):
            pl.semaphore_signal(sem, inc=1, device_id=peer, device_id_type=MESH)
        pl.semaphore_wait(sem, len(peers) + len(more))


def remote(src, dst, sems, index, peer):
    send, recv = sems
    return pltpu.make_async_remote_copy(
        src_ref=src, dst_ref=dst, send_sem=send.at[index], recv_sem=recv.at[index],
        device_id=peer, device_id_type=MESH,
    )


class Gather:
    def __init__(self, place, stack, sems):
        self.p, self.stack = place, stack
        self.z_sems, self.x_sems, self.y_sems, self.s_sems = sems
        self.sent = []

    def at(self, rel, z, half=None, core=None):
        start = self.p.owner(rel, z, core) * 4
        if half is None:
            return self.stack.at[pl.ds(start, 4)]
        return self.stack.at[pl.ds(start + half * 2, 2)]

    def send(self, ref, sems, index, peer):
        copy = remote(ref, ref, sems, index, peer)
        copy.start()
        self.sent.append(copy)

    def arrived(self, ref, sems, index, peer):
        remote(ref, ref, sems, index, peer).wait_recv()

    def to_x(self, kind, rel, z, half):
        self.send(self.at(rel, z, half), self.x_sems, kind * 4 + z, self.p.x_peer)

    def to_y(self, kind, rel, z, half):
        self.send(self.at(rel, z, half), self.y_sems, kind * 4 + z, self.p.y_peer)

    def to_sibling(self, rel, z, half):
        if half is None:
            self.send(self.at(rel, z), self.s_sems, z, self.p.sibling)
        else:
            self.send(self.at(rel, z, half), self.s_sems, (rel * 2 + half - 1) * 4 + z, self.p.sibling)

    def spread(self, z):
        self.to_x(0, 0, z, 0)
        self.to_y(0, 0, z, 1)
        self.to_y(1, 0, z, 0)
        self.to_x(1, 0, z, 1)
        self.to_sibling(0, z, None)

    def start(self):
        p = self.p
        self.to_x(0, 0, p.z, 0)
        self.to_y(0, 0, p.z, 1)
        for z in reversed(p.others):
            copy = pltpu.make_async_remote_copy(
                src_ref=self.at(0, p.z), dst_ref=self.at(0, p.z), send_sem=self.z_sems[0].at[z],
                recv_sem=self.z_sems[1].at[p.z], device_id=p.z_peer(z), device_id_type=MESH)
            copy.start()
            self.sent.append(copy)
        self.to_y(1, 0, p.z, 0)
        self.to_x(1, 0, p.z, 1)
        self.to_sibling(0, p.z, None)

    def from_z(self, z):
        self.arrived(self.at(0, z), self.z_sems, z, self.p.z_peer(z))
        self.spread(z)

    def first(self, z):
        p = self.p
        self.arrived(self.at(1, z, 0), self.x_sems, z, p.x_peer)
        self.to_y(2, 1, z, 0)
        self.to_sibling(1, z, 0)
        self.arrived(self.at(2, z, 1), self.y_sems, z, p.y_peer)
        self.to_x(2, 2, z, 1)
        self.to_sibling(2, z, 1)

    def second(self, z):
        p = self.p
        self.arrived(self.at(1, z, 1), self.x_sems, 4 + z, p.x_peer)
        self.to_sibling(1, z, 1)
        self.arrived(self.at(2, z, 0), self.y_sems, 4 + z, p.y_peer)
        self.to_sibling(2, z, 0)

    def third(self, z):
        p = self.p
        self.arrived(self.at(3, z, 1), self.x_sems, 8 + z, p.x_peer)
        self.to_sibling(3, z, 1)
        self.arrived(self.at(3, z, 0), self.y_sems, 8 + z, p.y_peer)
        self.to_sibling(3, z, 0)

    def finish(self):
        p = self.p
        other = 1 - p.core
        for z in range(4):
            self.arrived(self.at(0, z, None, other), self.s_sems, z, p.sibling)
            for rel in (1, 2, 3):
                for half in (0, 1):
                    self.arrived(self.at(rel, z, half, other), self.s_sems, (rel * 2 + half - 1) * 4 + z, p.sibling)
        for copy in self.sent:
            copy.wait_send()

    def events(self):
        p = self.p
        order = [p.z] + p.others
        todo = [self.start]
        todo.append(lambda: self.from_z(order[1]))
        todo.append(lambda: self.first(order[0]))
        todo.append(lambda: self.from_z(order[2]))
        todo.append(lambda: self.first(order[1]))
        todo.append(lambda: self.from_z(order[3]))
        todo.append(lambda: self.first(order[2]))
        todo.append(lambda: self.second(order[0]))
        todo.append(lambda: self.third(order[0]))
        todo.append(lambda: self.first(order[3]))
        for n in (1, 2, 3):
            todo.append(lambda n=n: self.second(order[n]))
            todo.append(lambda n=n: self.third(order[n]))
        todo.append(self.finish)
        return todo


GATHER_SEMS = [pltpu.SemaphoreType.DMA((n,)) for n in (4, 4, 12, 12, 12, 12, 28, 28)]


def pairs(sems):
    return [(sems[i], sems[i + 1]) for i in range(0, len(sems), 2)]


def pick(which, zero, one):
    return jnp.where(jnp.full(zero.shape, which, i32) == 0, zero, one)


def assemble_in(inverse, stack, spread, weight, layer):
    def column(j, _):
        for i in range(16):
            q = inverse[layer * 128 + i * 8 + j]
            pair = stack[lax.div(q, 2)].astype(f32)
            spread[j, pl.ds(69 * i, 72), :] = pick(lax.rem(q, 2), pair[:72], pair[72:])
        weight[layer, :, pl.ds(pl.multiple_of(j * 128, 128), 128)] = spread[j, :1104, :].astype(bf16)
        return 0

    lax.fori_loop(0, 8, column, 0)


def assemble_out(inverse, stack, weight, layer):
    lane = lax.broadcasted_iota(i32, (64, 128), 1)

    def line(i, _):
        for m in range(8):
            halves = []
            for h in range(2):
                q = inverse[layer * 128 + i * 16 + 2 * m + h]
                pair = stack[lax.div(q, 2)].astype(f32)
                turned = pltpu.roll(pair, 64, 1)
                halves.append(pick(lax.rem(q, 2), *((turned, pair) if h else (pair, turned))))
            weight[layer, pl.ds(pl.multiple_of(i * 64, 64), 64), 128 * m : 128 * m + 128] = jnp.where(
                lane < 64, halves[0], halves[1]
            ).astype(bf16)
        return 0

    lax.fori_loop(0, 8, line, 0)


def own_share_in(w_ref, spread, stack, start):
    for k in range(8):
        spread[0, pl.ds(72 * k, 69), :] = w_ref[k]
    for m in range(4):
        stack[start + m] = spread[0, 144 * m : 144 * m + 144, :].astype(bf16)


def own_share_out(w_ref, stack, start):
    for m in range(4):
        stack[start + m] = jnp.concatenate(
            [w_ref[2 * m], w_ref[2 * m + 1]], axis=1
        ).astype(bf16)


def gather_kernel(inverse, w_in, w_out, full_in, full_out, stack_in, stack_out, spread, *sems):
    place = Place()
    spread[...] = jnp.zeros_like(spread)
    me = place.row * 8 + place.seq
    own_share_in(w_in, spread, stack_in, me * 4)
    own_share_out(w_out, stack_out, me * 4)
    place.barrier()
    for event in Gather(place, stack_in, pairs(sems[:8])).events():
        event()
    out = Gather(place, stack_out, pairs(sems[8:])).events()
    out[0]()
    for layer in range(2):
        assemble_in(inverse, stack_in, spread, full_in, layer)
    for event in out[1:]:
        event()
    for layer in range(2):
        assemble_out(inverse, stack_out, full_out, layer)


VMEM = pl.BlockSpec(memory_space=pltpu.VMEM)
SMEM = pl.BlockSpec(memory_space=pltpu.SMEM)


def gather_weights(inverse, w_in, w_out):
    return pl.pallas_call(
        gather_kernel,
        out_shape=[
            jax.ShapeDtypeStruct((2, 1104, 1024), bf16),
            jax.ShapeDtypeStruct((2, 512, 1024), bf16),
        ],
        in_specs=[SMEM, VMEM, VMEM],
        out_specs=[VMEM, VMEM],
        scratch_shapes=[
            pltpu.VMEM((128, 144, 128), bf16),
            pltpu.VMEM((128, 64, 128), bf16),
            pltpu.VMEM((8, 1112, 128), f32),
        ]
        + GATHER_SEMS
        + GATHER_SEMS,
        name="gather",
        compiler_params=pltpu.CompilerParams(
            collective_id=0, has_side_effects=True, vmem_limit_bytes=48 << 20
        ),
    )(inverse, w_in, w_out)


class Reduce:
    def __init__(self, place, pack, rows, bufs, sems):
        self.p, self.pack, self.rows, self.half, self.pair = place, pack, rows, rows // 2, rows // 4
        (self.s_out, self.s_in, self.x1_out, self.x1_in, self.y1_out, self.y1_in,
         self.x2_out, self.x2_in, self.y2_out, self.y2_in, self.z_out, self.z_in) = bufs
        self.s_sems, self.x1_sems, self.y1_sems, self.x2_sems, self.y2_sems, self.z_sems = sems
        self.sent = []

    def rows_at(self, start, count):
        return pl.ds(pl.multiple_of(start, 16), count)

    def move(self, out, into, sems, index, count, peer):
        where = self.rows_at(index * count, count)
        return remote(out.at[where], into.at[where], sems, index, peer)

    def send(self, copy):
        copy.start()
        self.sent.append(copy)

    def sibling_copy(self, z):
        return self.move(self.s_out, self.s_in, self.s_sems, z, 4 * self.rows, self.p.sibling)

    def first_copies(self, z):
        return (
            self.move(self.x1_out, self.x1_in, self.x1_sems, z, 2 * self.half, self.p.x_peer),
            self.move(self.y1_out, self.y1_in, self.y1_sems, z, 2 * self.half, self.p.y_peer),
        )

    def second_copies(self, z):
        return (
            self.move(self.x2_out, self.x2_in, self.x2_sems, z, self.half, self.p.x_peer),
            self.move(self.y2_out, self.y2_in, self.y2_sems, z, self.half, self.p.y_peer),
        )

    def z_copy(self, src, dst, peer_z):
        p = self.p
        return pltpu.make_async_remote_copy(
            src_ref=self.z_out.at[self.rows_at(dst * self.rows, self.rows)],
            dst_ref=self.z_in.at[self.rows_at(src * self.rows, self.rows)],
            send_sem=self.z_sems[0].at[dst],
            recv_sem=self.z_sems[1].at[src],
            device_id=p.z_peer(peer_z),
            device_id_type=MESH,
        )

    def to_sibling(self, z):
        p = self.p
        for rel in range(4):
            owner = p.owner(rel, z, 1 - p.core)

            def put(m, _, rel=rel, owner=owner):
                start = (z * 4 + rel) * self.rows + m * self.pair
                self.s_out[self.rows_at(start, self.pair), :] = self.pack(owner, m).astype(bf16)
                return 0

            lax.fori_loop(0, 4, put, 0)
        self.send(self.sibling_copy(z))

    def term(self, rel, z, half, m):
        start = (z * 4 + rel) * self.rows + half * self.half + m * self.pair
        other = self.s_in[self.rows_at(start, self.pair), :].astype(f32)
        return self.pack(self.p.owner(rel, z), half * 2 + m) + other

    def read(self, ref, start, m):
        return ref[self.rows_at(start + m * self.pair, self.pair), :].astype(f32)

    def first(self, z):
        self.sibling_copy(z).wait_recv()
        for out, half, rels in ((self.x1_out, 0, (1, 3)), (self.y1_out, 1, (2, 3))):
            for n, rel in enumerate(rels):

                def put(m, _, out=out, half=half, rel=rel, n=n):
                    start = (z * 2 + n) * self.half + m * self.pair
                    out[self.rows_at(start, self.pair), :] = self.term(rel, z, half, m).astype(bf16)
                    return 0

                lax.fori_loop(0, 2, put, 0)
        for copy in self.first_copies(z):
            self.send(copy)

    def second(self, z):
        for copy in self.first_copies(z):
            copy.wait_recv()
        for out, into, half, rel in ((self.y2_out, self.x1_in, 0, 2), (self.x2_out, self.y1_in, 1, 1)):

            def put(m, _, out=out, into=into, half=half, rel=rel):
                total = self.term(rel, z, half, m) + self.read(into, (z * 2 + 1) * self.half, m)
                out[self.rows_at(z * self.half + m * self.pair, self.pair), :] = total.astype(bf16)
                return 0

            lax.fori_loop(0, 2, put, 0)
        for copy in self.second_copies(z):
            self.send(copy)

    def column(self, z, half, m):
        first, second = ((self.x1_in, self.y2_in), (self.y1_in, self.x2_in))[half]
        return (
            self.term(0, z, half, m)
            + self.read(first, z * 2 * self.half, m)
            + self.read(second, z * self.half, m)
        )

    def third(self, z):
        for copy in self.second_copies(z):
            copy.wait_recv()
        for half in range(2):

            def put(m, _, half=half):
                start = z * self.rows + half * self.half + m * self.pair
                self.z_out[self.rows_at(start, self.pair), :] = self.column(z, half, m).astype(bf16)
                return 0

            lax.fori_loop(0, 2, put, 0)
        self.send(self.z_copy(self.p.z, z, z))

    def last(self, out):
        p = self.p
        for copy in self.second_copies(p.z):
            copy.wait_recv()
        for z in p.others:
            self.z_copy(z, p.z, z).wait_recv()
        for half in range(2):

            def put(m, _, half=half):
                total = self.column(p.z, half, m)
                start = half * self.half + m * self.pair
                for z in p.others:
                    total = total + self.read(self.z_in, z * self.rows + start, m * 0)
                out[pl.ds(pl.multiple_of(start, 8), self.pair), :] = total
                return 0

            lax.fori_loop(0, 2, put, 0)

    def finish(self):
        for copy in self.sent:
            copy.wait_send()

    def events(self, out):
        p = self.p
        order = p.others[::-1] + [p.z]
        todo = [lambda z=z: self.to_sibling(z) for z in order[:2]]
        todo.append(lambda: self.first(order[0]))
        todo.append(lambda: self.to_sibling(order[2]))
        todo.append(lambda: self.first(order[1]))
        todo.append(lambda: self.second(order[0]))
        todo.append(lambda: self.to_sibling(order[3]))
        todo.append(lambda: self.first(order[2]))
        todo.append(lambda: self.second(order[1]))
        todo.append(lambda: self.third(order[0]))
        todo.append(lambda: self.first(order[3]))
        todo.append(lambda: self.second(order[2]))
        todo.append(lambda: self.third(order[1]))
        todo.append(lambda: self.second(order[3]))
        todo.append(lambda: self.third(order[2]))
        todo.append(lambda: self.last(out))
        todo.append(self.finish)
        return todo


def reduce_bufs(rows):
    counts = (16, 16, 4, 4, 4, 4, 2, 2, 2, 2, 4, 4)
    return [pltpu.VMEM((n * rows, 128), bf16) for n in counts]


REDUCE_SEMS = [pltpu.SemaphoreType.DMA((4,)) for _ in range(12)]


def pack_in(owner, grad):
    def pack(device, m):
        halves = []
        for h in range(2):
            b = owner[device * 8 + m * 2 + h]
            layer, i, j = lax.div(b, 128), lax.div(lax.rem(b, 128), 8), lax.rem(b, 8)
            halves.append(grad[layer * 8 + j, pl.ds(69 * i, 72), :])
        return jnp.concatenate(halves, axis=0)

    return pack


def pack_out(owner, grad):
    def pack(device, m):
        lane = lax.broadcasted_iota(i32, (64, 128), 1)
        halves = []
        for h in range(2):
            b = owner[device * 8 + m * 2 + h]
            layer, i, j = lax.div(b, 128), lax.div(lax.rem(b, 128), 16), lax.rem(b, 16)
            pair = grad[layer * 64 + i * 8 + lax.div(j, 2)]
            turned = pltpu.roll(pair, 64, 1)
            halves.append(pick(lax.rem(j, 2), *((turned, pair) if h else (pair, turned))))
        return jnp.where(lane < 64, halves[0], halves[1])

    return pack


def dot(a, b, ca, cb, precision=None):
    return lax.dot_general(
        a, b, (((ca,), (cb,)), ((), ())), precision=precision, preferred_element_type=f32
    )


def shampoo_block(grad, left, right, root_left, root_right, weight, rate):
    new_left = 0.5 * left + 0.5 * dot(grad, grad, 1, 1, highest)
    new_right = 0.5 * right + 0.5 * dot(grad, grad, 0, 0, highest)
    step = dot(dot(root_left, grad, 1, 0, highest), root_right, 1, 0, highest)
    return new_left, new_right, weight - rate * step


def reduce_kernel(
    owner, gin, gout, w_in, w_out, left_in, right_in, root_left_in, root_right_in,
    left_out, right_out, root_left_out, root_right_out,
    grad_in, grad_out, new_left_in, new_right_in, new_left_out, new_right_out, new_w_in, new_w_out,
    sum_in, sum_out, *rest,
):
    place = Place()
    place.barrier()
    bufs_in, bufs_out, sems = rest[:12], rest[12:24], rest[24:]
    out = Reduce(place, pack_out(owner, gout), ROWS_OUT, bufs_out, pairs(sems[:12]))
    for event in out.events(sum_out):
        event()
    into = Reduce(place, pack_in(owner, gin), ROWS_IN, bufs_in, pairs(sems[12:]))
    for event in into.events(sum_in):
        event()
    for k in range(8):
        grad = sum_in[72 * k : 72 * k + 69, :]
        grad_in[k] = grad
        new_left_in[k], new_right_in[k], new_w_in[k] = shampoo_block(
            grad, left_in[k], right_in[k], root_left_in[k], root_right_in[k], w_in[k], rate_in
        )
        grad = sum_out[64 * (k // 2) : 64 * (k // 2) + 64, 64 * (k % 2) : 64 * (k % 2) + 64]
        grad_out[k] = grad
        new_left_out[k], new_right_out[k], new_w_out[k] = shampoo_block(
            grad, left_out[k], right_out[k], root_left_out[k], root_right_out[k], w_out[k], rate_out
        )


def reduce_and_update(owner, gin, gout, *blocks):
    shapes = [(8, 69, 128), (8, 64, 64), (8, 69, 69), (8, 128, 128), (8, 64, 64), (8, 64, 64), (8, 69, 128), (8, 64, 64)]
    return pl.pallas_call(
        reduce_kernel,
        out_shape=[jax.ShapeDtypeStruct(s, f32) for s in shapes],
        in_specs=[SMEM] + [VMEM] * 12,
        out_specs=[VMEM] * 8,
        scratch_shapes=[pltpu.VMEM((ROWS_IN, 128), f32), pltpu.VMEM((ROWS_OUT, 128), f32)]
        + reduce_bufs(ROWS_IN)
        + reduce_bufs(ROWS_OUT)
        + REDUCE_SEMS
        + REDUCE_SEMS,
        name="reduce",
        compiler_params=pltpu.CompilerParams(
            collective_id=1, has_side_effects=True, vmem_limit_bytes=58 << 20
        ),
    )(owner, gin, gout, *blocks)


def local(
    signal,
    condition,
    lengths,
    owner,
    grad_out,
    grad_skip,
    w_in,
    w_out,
    left_in,
    right_in,
    root_left_in,
    root_right_in,
    left_out,
    right_out,
    root_left_out,
    root_right_out,
):
    fused = lax.axis_size("row") == 4 and lax.axis_size("seq") == 8
    audio_samples = signal.shape[1]
    width = signal.shape[2]
    if fused:
        at = jnp.arange(256, dtype=i32)
        inverse = jnp.sum(jnp.where(owner[None, :] == at[:, None], at[None, :], 0), axis=1)
        input_weight, output_weight = gather_weights(inverse, w_in, w_out)
    else:
        stack_in = lax.all_gather(w_in.astype(bf16), ("row", "seq"), axis=0, tiled=True)
        stack_out = lax.all_gather(w_out.astype(bf16), ("row", "seq"), axis=0, tiled=True)
        inverse = jnp.argsort(owner)
        input_weight = from_blocks(jnp.take(stack_in, inverse, axis=0), 16, 8)
        output_weight = from_blocks(jnp.take(stack_out, inverse, axis=0), 8, 16)
    sample_positions = lax.axis_index("seq") * audio_samples + jnp.arange(
        audio_samples, dtype=jnp.int32
    )
    longer_mask = receptive_mask(lengths, sample_positions, FIRST_DILATION)[:, :, None]
    mask_short = receptive_mask(lengths, sample_positions, 1)[:, :, None]
    preceding_longer = shifted(signal[:, audio_samples - FIRST_DILATION :, :], "seq", 1)
    delayed_one = jnp.concatenate([preceding_longer, signal], axis=1)[:, :audio_samples, :]
    delayed_one = jnp.where(longer_mask, delayed_one, jnp.zeros_like(delayed_one))
    units_one = jnp.concatenate([delayed_one, signal, condition], axis=2)
    tanh_one, sigm_one, hidden_one, proj_one = gate_forward(
        units_one, input_weight[0], output_weight[0]
    )
    first_layer_state = signal.astype(jnp.float32) + proj_one[..., :width]
    rounded_one = first_layer_state.astype(jnp.bfloat16)
    before_short = shifted(rounded_one[:, audio_samples - 1 :, :], "seq", 1)
    delayed_two = jnp.concatenate([before_short, rounded_one[:, : audio_samples - 1, :]], axis=1)
    delayed_two = jnp.where(mask_short, delayed_two, jnp.zeros_like(delayed_two))
    units_two = jnp.concatenate([delayed_two, rounded_one, condition], axis=2)
    tanh_two, sigm_two, hidden_two, proj_two = gate_forward(
        units_two, input_weight[1], output_weight[1]
    )
    out_x = first_layer_state + proj_two[..., :width]
    skip_sum = proj_one[..., width:] + proj_two[..., width:]
    grad_next = grad_out.astype(jnp.float32)
    gin_two, gout_two, units_grad_two = gate_backward(
        units_two,
        tanh_two,
        sigm_two,
        hidden_two,
        input_weight[1],
        output_weight[1],
        grad_next,
        grad_skip,
    )
    early_two = jnp.where(mask_short, units_grad_two[..., :width], 0.0)
    from_short = shifted(early_two[:, :1, :], "seq", -1)
    grad_state = (
        grad_next
        + units_grad_two[..., width : 2 * width]
        + jnp.concatenate([early_two[:, 1:, :], from_short], axis=1)
    )
    gin_one, gout_one, units_grad_one = gate_backward(
        units_one,
        tanh_one,
        sigm_one,
        hidden_one,
        input_weight[0],
        output_weight[0],
        grad_state,
        grad_skip,
    )
    earlier_first = jnp.where(longer_mask, units_grad_one[..., :width], 0.0)
    taken_longer = shifted(earlier_first[:, :FIRST_DILATION, :], "seq", -1)
    grad_x = (
        grad_state
        + units_grad_one[..., width : 2 * width]
        + jnp.concatenate([earlier_first[:, FIRST_DILATION:, :], taken_longer], axis=1)
    )
    grad_cond = units_grad_one[..., 2 * width :] + units_grad_two[..., 2 * width :]
    if fused:
        gin = jnp.stack([gin_one, gin_two]).reshape(2, 1104, 8, 128).transpose(0, 2, 1, 3)
        gin = jnp.pad(gin.reshape(16, 1104, 128), ((0, 0), (0, 8), (0, 0)))
        gout = jnp.stack([gout_one, gout_two]).reshape(2, 8, 64, 8, 128).transpose(0, 1, 3, 2, 4)
        gout = gout.reshape(128, 64, 128)
        updated = reduce_and_update(
            owner, gin, gout, w_in, w_out,
            left_in, right_in, root_left_in, root_right_in,
            left_out, right_out, root_left_out, root_right_out,
        )
        return (out_x, skip_sum, grad_x, grad_cond, *updated)
    local_in = jnp.take(to_blocks(jnp.stack([gin_one, gin_two]), 16, 8), owner, axis=0)
    local_out = jnp.take(to_blocks(jnp.stack([gout_one, gout_two]), 8, 16), owner, axis=0)
    grad_in_blocks, grad_out_blocks = (
        lax.psum_scatter(local_in, ("row", "seq"), scatter_dimension=0, tiled=True),
        lax.psum_scatter(local_out, ("row", "seq"), scatter_dimension=0, tiled=True),
    )
    new_left_in, new_right_in, new_w_in = shampoo(
        grad_in_blocks, left_in, right_in, root_left_in, root_right_in, w_in, rate_in
    )
    new_left_out, new_right_out, new_w_out = shampoo(
        grad_out_blocks, left_out, right_out, root_left_out, root_right_out, w_out, rate_out
    )
    return (
        out_x,
        skip_sum,
        grad_x,
        grad_cond,
        grad_in_blocks,
        grad_out_blocks,
        new_left_in,
        new_right_in,
        new_left_out,
        new_right_out,
        new_w_in,
        new_w_out,
    )


def solution(mesh):
    tokens, blocks = P("row", "seq", None), P(("row", "seq"), None, None)
    in_specs = (tokens, tokens, P("row", None), P(), tokens, tokens) + (blocks,) * 10
    out_specs = (tokens,) * 4 + (blocks,) * 8
    return jax.shard_map(local, mesh=mesh, in_specs=in_specs, out_specs=out_specs, check_vma=False)
```

```python
import jax
import jax.numpy as jnp
from jax import lax
from jax.experimental import pallas as pl
from jax.experimental.pallas import tpu as pltpu
from jax.sharding import PartitionSpec as P

FIRST_DILATION = 512
MESH = pl.DeviceIdType.MESH
bf16, f32, i32 = jnp.bfloat16, jnp.float32, jnp.int32

highest = lax.Precision.HIGHEST
rate_in = 0.3
rate_out = 1.0

TILE = 512
ROWS_IN = 576
ROWS_OUT = 256


def shifted(block, axis, distance):
    devices = range(lax.axis_size(axis))
    route = [(i - distance, i) for i in devices if i - distance in devices]
    return lax.ppermute(block, axis, route)


def to_blocks(full, row_parts, col_parts):
    layers, rows, cols = full.shape
    shaped = full.reshape(layers, row_parts, rows // row_parts, col_parts, cols // col_parts)
    return shaped.transpose(0, 1, 3, 2, 4).reshape(
        layers * row_parts * col_parts, rows // row_parts, cols // col_parts
    )


def from_blocks(blocks, row_parts, col_parts):
    count, block_rows, block_cols = blocks.shape
    layers = count // (row_parts * col_parts)
    shaped = blocks.reshape(layers, row_parts, col_parts, block_rows, block_cols)
    return shaped.transpose(0, 1, 3, 2, 4).reshape(
        layers, row_parts * block_rows, col_parts * block_cols
    )


def receptive_mask(lengths, sample_positions, dilation):
    ends = jnp.cumsum(lengths, axis=1)
    starts = jnp.sum(
        jnp.where(ends[:, None, :] <= sample_positions[None, :, None], lengths[:, None, :], 0),
        axis=2,
    )
    return sample_positions[None, :] - dilation >= starts


def gate_forward(units, input_weight, output_weight):
    pre = jnp.einsum("ptk,kg->ptg", units, input_weight, preferred_element_type=jnp.float32)
    half = pre.shape[2] // 2
    tanh_part = jnp.tanh(pre[..., :half])
    sigm_part = jax.nn.sigmoid(pre[..., half:])
    hidden = (tanh_part * sigm_part).astype(jnp.bfloat16)
    projected = jnp.einsum("ptg,gk->ptk", hidden, output_weight, preferred_element_type=jnp.float32)
    return (tanh_part, sigm_part, hidden, projected)


def gate_backward(
    units, tanh_part, sigm_part, hidden, input_weight, output_weight, grad_state, grad_skip
):
    grad_proj = jnp.concatenate([grad_state, grad_skip.astype(jnp.float32)], axis=2).astype(
        jnp.bfloat16
    )
    grad_wout = jnp.einsum("ptg,ptk->gk", hidden, grad_proj, preferred_element_type=jnp.float32)
    grad_hidden = jnp.einsum(
        "ptk,gk->ptg", grad_proj, output_weight, preferred_element_type=jnp.float32
    )
    grad_tanh = grad_hidden * sigm_part * (1.0 - tanh_part * tanh_part)
    grad_sigm = grad_hidden * tanh_part * sigm_part * (1.0 - sigm_part)
    grad_pre = jnp.concatenate([grad_tanh, grad_sigm], axis=2).astype(jnp.bfloat16)
    grad_win = jnp.einsum("ptk,ptg->kg", units, grad_pre, preferred_element_type=jnp.float32)
    grad_units = jnp.einsum(
        "ptg,kg->ptk", grad_pre, input_weight, preferred_element_type=jnp.float32
    )
    return (grad_win, grad_wout, grad_units)


def shampoo(grad, left, right, root_left, root_right, weight, rate):
    new_left = 0.5 * left + 0.5 * jnp.einsum("bij,bkj->bik", grad, grad, precision=highest)
    new_right = 0.5 * right + 0.5 * jnp.einsum("bji,bjk->bik", grad, grad, precision=highest)
    step = jnp.einsum("bij,bjk->bik", root_left, grad, precision=highest)
    step = jnp.einsum("bij,bjk->bik", step, root_right, precision=highest)
    return (new_left, new_right, weight - rate * step)


class Place:
    def __init__(self):
        self.row, self.seq = lax.axis_index("row"), lax.axis_index("seq")
        self.z, self.core = self.seq // 2, self.seq % 2
        x, y = self.row % 2, self.row // 2
        self.rows = (
            self.row,
            self.row + 1 - 2 * x,
            self.row + 2 - 4 * y,
            self.row + 3 - 2 * x - 4 * y,
        )
        self.x_peer = (self.rows[1], self.seq)
        self.y_peer = (self.rows[2], self.seq)
        self.sibling = (self.row, self.seq + 1 - 2 * self.core)
        self.near = self.mirrored(self.z)
        self.others = [self.mirrored(t) for t in (1 - self.near, 2, 3)]

    def mirrored(self, z):
        return z + self.z // 2 * (3 - 2 * z)

    def z_peer(self, z):
        return (self.row, 2 * z + self.core)

    def owner(self, rel, z, core=None):
        core = self.core if core is None else core
        return self.rows[rel] * 8 + 2 * z + core

    def announce(self):
        peers = [self.x_peer, self.y_peer, self.sibling] + [self.z_peer(z) for z in self.others]
        for peer in peers:
            pl.semaphore_signal(
                pltpu.get_barrier_semaphore(), inc=1, device_id=peer, device_id_type=MESH
            )

    def all_here(self):
        pl.semaphore_wait(pltpu.get_barrier_semaphore(), 6)


class Gather:
    def __init__(self, place, stack, count, sems):
        self.p, self.stack, self.count = place, stack, count
        self.send_sem, self.z_sems, self.x_sems, self.y_sems, self.s_sem = sems
        self.sent = 0

    def at(self, rel, z, half=None, core=None):
        start = self.p.owner(rel, z, core) * self.count
        if half is None:
            return self.stack.at[pl.ds(start, self.count)]
        part = self.count // 2
        return self.stack.at[pl.ds(start + half * part, part)]

    def copy(self, ref, sem, peer):
        return pltpu.make_async_remote_copy(
            src_ref=ref, dst_ref=ref, send_sem=self.send_sem.at[0], recv_sem=sem, device_id=peer, device_id_type=MESH
        )

    def send(self, ref, sem, peer):
        self.copy(ref, sem, peer).start()
        self.sent += 1

    def arrived(self, ref, sem, peer):
        self.copy(ref, sem, peer).wait_recv()

    def to_x(self, kind, rel, z, half):
        self.send(self.at(rel, z, half), self.x_sems.at[kind * 4 + z], self.p.x_peer)

    def to_y(self, kind, rel, z, half):
        self.send(self.at(rel, z, half), self.y_sems.at[kind * 4 + z], self.p.y_peer)

    def to_sibling(self, rel, z, half):
        self.send(self.at(rel, z, half), self.s_sem.at[0], self.p.sibling)

    def sides(self, z, half):
        if half == 0:
            self.to_x(0, 0, z, 0)
            self.to_y(1, 0, z, 0)
        else:
            self.to_y(0, 0, z, 1)
            self.to_x(1, 0, z, 1)
        self.to_sibling(0, z, half)

    def z_copy(self, src, half, z):
        return self.copy(self.at(0, src, half), self.z_sems.at[2 * src + half], self.p.z_peer(z))

    def z_passed(self, n, half):
        p = self.p
        outer, inner = p.mirrored(0), p.mirrored(2)
        near, far, farthest = p.others
        src, z = ((p.z, inner), (near, inner), (far, outer), (farthest, outer))[n]
        return self.z_copy(src, half, z)

    def pass_on(self, n, half):
        pl.when(self.p.near == 1)(lambda: self.z_passed(n, half).start())

    def start(self):
        p = self.p
        for half in range(2):
            self.z_copy(p.z, half, p.mirrored(1 - p.near)).start()
            self.sent += 1
            self.pass_on(0, half)

    def start_sides(self):
        for half in range(2):
            self.sides(self.p.z, half)

    def relay(self, n, half):
        z = self.p.others[n]
        self.arrived(self.at(0, z, half), self.z_sems.at[2 * z + half], self.p.z_peer(z))
        self.pass_on(n + 1, half)

    def spread(self, n, half):
        self.sides(self.p.others[n], half)

    def along_z(self, n):
        for half in range(2):
            self.relay(n, half)
            self.spread(n, half)

    def first(self, z):
        p = self.p
        self.arrived(self.at(1, z, 0), self.x_sems.at[z], p.x_peer)
        self.to_y(2, 1, z, 0)
        self.to_sibling(1, z, 0)
        self.arrived(self.at(2, z, 1), self.y_sems.at[z], p.y_peer)
        self.to_x(2, 2, z, 1)
        self.to_sibling(2, z, 1)

    def second(self, z):
        p = self.p
        self.arrived(self.at(1, z, 1), self.x_sems.at[4 + z], p.x_peer)
        self.to_sibling(1, z, 1)
        self.arrived(self.at(2, z, 0), self.y_sems.at[4 + z], p.y_peer)
        self.to_sibling(2, z, 0)

    def third(self, z):
        p = self.p
        self.arrived(self.at(3, z, 1), self.x_sems.at[8 + z], p.x_peer)
        self.to_sibling(3, z, 1)
        self.arrived(self.at(3, z, 0), self.y_sems.at[8 + z], p.y_peer)
        self.to_sibling(3, z, 0)

    def rest(self, z):
        self.second(z)
        self.third(z)

    def bytes_of(self, halves):
        return self.stack.at[pl.ds(0, halves * self.count // 2)]

    def finish(self):
        self.arrived(self.bytes_of(32), self.s_sem.at[0], self.p.sibling)
        self.copy(self.bytes_of(self.sent), self.s_sem.at[0], self.p.sibling).wait_send()

        @pl.when(self.p.near == 1)
        def _():
            self.copy(self.bytes_of(8), self.s_sem.at[0], self.p.sibling).wait_send()


GATHER_SEMS = [pltpu.SemaphoreType.DMA((n,)) for n in (1, 8, 12, 12, 1)]


def pick(which, zero, one):
    return jnp.where(jnp.full(zero.shape, which, i32) == 0, zero, one)


def assemble_in(inverse, stack, spread, weight, layer):
    def column(j, _):
        for i in range(16):
            q = inverse[layer, i * 8 + j]
            pair = stack[lax.div(q, 2)].astype(f32)
            spread[j, pl.ds(69 * i, 72), :] = pick(lax.rem(q, 2), pair[:72], pair[72:])
        weight[layer, :1104, pl.ds(pl.multiple_of(j * 128, 128), 128)] = spread[j, :1104, :].astype(bf16)
        return 0

    lax.fori_loop(0, 8, column, 0)


def across(top, bottom):
    left = lax.broadcasted_iota(i32, top.shape, 1) < 64
    return (
        jnp.where(left, top, pltpu.roll(bottom, 64, 1)),
        jnp.where(left, pltpu.roll(top, 64, 1), bottom),
    )


def assemble_out(inverse, stack, weight, layer):
    def line(i, _):
        for m in range(8):
            two = [stack[inverse[layer, i * 16 + 2 * m + h]].astype(f32) for h in range(2)]
            for k, rows in enumerate(across(*two)):
                first = pl.multiple_of(layer * 512 + i * 64 + 32 * k, 32)
                weight[pl.ds(first, 32), 128 * m : 128 * m + 128] = rows.astype(bf16)
        return 0

    lax.fori_loop(0, 8, line, 0)


VMEM = pl.BlockSpec(memory_space=pltpu.VMEM)
SMEM = pl.BlockSpec(memory_space=pltpu.SMEM)


class Reduce:
    def __init__(self, place, pack, rows, bufs, sems):
        self.p, self.pack, self.rows, self.half, self.pair = place, pack, rows, rows // 2, rows // 4
        (self.s_out, self.s_in, self.x1_out, self.x1_in, self.y1_out, self.y1_in,
         self.x2_out, self.x2_in, self.y2_out, self.y2_in, self.z_out, self.z_in) = bufs
        self.send_sem, self.s_sems, self.x1_sems, self.y1_sems, self.x2_sems, self.y2_sems, self.z_sems = sems
        self.sent = 0

    def rows_at(self, start, count):
        return pl.ds(pl.multiple_of(start, 16), count)

    def at(self, buf, start, count):
        ref, first = buf
        return ref.at[self.rows_at(first + start, count)]

    def put(self, buf, start, value):
        ref, first = buf
        ref[self.rows_at(first + start, self.pair), :] = value.astype(bf16)

    def read(self, buf, start):
        ref, first = buf
        return ref[self.rows_at(first + start, self.pair), :].astype(f32)

    def move(self, out, into, sems, index, count, peer):
        start = index * count
        return self.copy(self.at(out, start, count), self.at(into, start, count), sems.at[index], peer)

    def copy(self, src, dst, sem, peer):
        return pltpu.make_async_remote_copy(
            src_ref=src, dst_ref=dst, send_sem=self.send_sem.at[0], recv_sem=sem, device_id=peer, device_id_type=MESH
        )

    def sibling_copy(self, z):
        return self.move(self.s_out, self.s_in, self.s_sems, z, 4 * self.rows, self.p.sibling)

    def first_copies(self, z):
        return (
            self.move(self.x1_out, self.x1_in, self.x1_sems, z, 2 * self.half, self.p.x_peer),
            self.move(self.y1_out, self.y1_in, self.y1_sems, z, 2 * self.half, self.p.y_peer),
        )

    def second_copies(self, z):
        return (
            self.move(self.x2_out, self.x2_in, self.x2_sems, z, self.half, self.p.x_peer),
            self.move(self.y2_out, self.y2_in, self.y2_sems, z, self.half, self.p.y_peer),
        )

    def z_copy(self, src, dst, peer_z):
        return self.copy(
            self.at(self.z_out, dst * self.rows, self.rows), self.at(self.z_in, src * self.rows, self.rows),
            self.z_sems.at[src], self.p.z_peer(peer_z),
        )

    def to_sibling(self, z):
        p = self.p
        for rel in range(4):
            owner = p.owner(rel, z, 1 - p.core)

            def put(m, _, rel=rel, owner=owner):
                start = (z * 4 + rel) * self.rows + m * self.pair
                self.put(self.s_out, start, self.pack(owner, m))
                return 0

            lax.fori_loop(0, 4, put, 0)
        self.sibling_copy(z).start()

    def term(self, rel, z, half, m):
        start = (z * 4 + rel) * self.rows + half * self.half + m * self.pair
        return self.pack(self.p.owner(rel, z), half * 2 + m).astype(f32) + self.read(self.s_in, start)

    def first(self, z):
        self.sibling_copy(z).wait_recv()
        for out, half, rels in ((self.x1_out, 0, (1, 3)), (self.y1_out, 1, (2, 3))):
            for n, rel in enumerate(rels):

                def put(m, _, out=out, half=half, rel=rel, n=n):
                    start = (z * 2 + n) * self.half + m * self.pair
                    self.put(out, start, self.term(rel, z, half, m))
                    return 0

                lax.fori_loop(0, 2, put, 0)
        for copy in self.first_copies(z):
            copy.start()

    def second(self, z):
        for copy in self.first_copies(z):
            copy.wait_recv()
        for out, into, half, rel in ((self.y2_out, self.x1_in, 0, 2), (self.x2_out, self.y1_in, 1, 1)):

            def put(m, _, out=out, into=into, half=half, rel=rel):
                there = (z * 2 + 1) * self.half + m * self.pair
                total = self.term(rel, z, half, m) + self.read(into, there)
                self.put(out, z * self.half + m * self.pair, total)
                return 0

            lax.fori_loop(0, 2, put, 0)
        for copy in self.second_copies(z):
            copy.start()

    def column(self, z, half, m):
        first, second = ((self.x1_in, self.y2_in), (self.y1_in, self.x2_in))[half]
        return (
            self.term(0, z, half, m)
            + self.read(first, z * 2 * self.half + m * self.pair)
            + self.read(second, z * self.half + m * self.pair)
        )

    def third(self, z):
        for copy in self.second_copies(z):
            copy.wait_recv()
        for half in range(2):

            def put(m, _, half=half):
                start = z * self.rows + half * self.half + m * self.pair
                self.put(self.z_out, start, self.column(z, half, m))
                return 0

            lax.fori_loop(0, 2, put, 0)
        self.z_copy(self.p.z, z, z).start()

    def last(self, out):
        p = self.p
        for copy in self.second_copies(p.z):
            copy.wait_recv()
        for z in p.others:
            self.z_copy(z, p.z, z).wait_recv()
        for half in range(2):

            def put(m, _, half=half):
                total = self.column(p.z, half, m)
                start = half * self.half + m * self.pair
                for z in p.others:
                    total = total + self.read(self.z_in, z * self.rows + start)
                out[pl.ds(pl.multiple_of(start, 8), self.pair), :] = total
                return 0

            lax.fori_loop(0, 2, put, 0)

    def finish(self):
        whole = self.at((self.s_out[0], 0), 0, 31 * self.rows)
        self.copy(whole, whole, self.z_sems.at[0], self.p.sibling).wait_send()

    def events(self, out, steps):
        order = self.p.others[::-1] + [self.p.z]

        def event(step):
            kind, k = step
            if kind == "last":
                return lambda: self.last(out)
            return lambda: getattr(self, kind)(order[k])

        return [event(step) for step in steps]


def steps_of(*kinds):
    seen = {}
    for kind in kinds:
        seen[kind] = seen.get(kind, -1) + 1
        yield kind, seen[kind]


TO, ONE, TWO, THREE, LAST = "to_sibling", "first", "second", "third", "last"
REDUCE_ORDER = tuple(
    steps_of(TO, TO, ONE, TO, ONE, TO, TWO, ONE, TWO, THREE, TWO, ONE, THREE, THREE, TWO, LAST)
)
REDUCE_ORDER_OUT = tuple(
    steps_of(TO, TO, ONE, TO, ONE, TWO, TO, ONE, TWO, THREE, ONE, TWO, THREE, TWO, THREE, LAST)
)


REDUCE_COUNTS = (16, 4, 4, 2, 2, 4)
REDUCE_SEMS = [pltpu.SemaphoreType.DMA((n,)) for n in (1, 4, 4, 4, 4, 4, 4)]


def reduce_bufs(out, into, rows):
    bufs, first = [], 0
    for count in REDUCE_COUNTS:
        bufs += [(out, first), (into, first)]
        first += count * rows
    return bufs


def pack_in(owner, grad):
    def pack(device, m):
        halves = []
        for h in range(2):
            b = owner[device * 8 + m * 2 + h]
            layer, i, j = lax.div(b, 128), lax.div(lax.rem(b, 128), 8), lax.rem(b, 8)
            halves.append(grad[layer * 8 + j, pl.ds(69 * i, 72), :])
        return jnp.concatenate(halves, axis=0)

    return pack


def pack_out(owner, grad):
    def pack(device, m):
        return jnp.concatenate([grad[owner[device * 8 + m * 2 + h]] for h in range(2)], axis=0)

    return pack


def dot(a, b, ca, cb, precision=None):
    return lax.dot_general(
        a, b, (((ca,), (cb,)), ((), ())), precision=precision, preferred_element_type=f32
    )


def shampoo_block(grad, left, right, root_left, root_right, weight, rate):
    new_left = 0.5 * left + 0.5 * dot(grad, grad, 1, 1, highest)
    new_right = 0.5 * right + 0.5 * dot(grad, grad, 0, 0, highest)
    step = dot(dot(root_left, grad, 1, 0, highest), root_right, 1, 0, highest)
    return new_left, new_right, weight - rate * step


def dot(a, b, ca, cb, precision=None):
    return lax.dot_general(
        a, b, (((ca,), (cb,)), ((), ())), precision=precision, preferred_element_type=f32
    )


def tile(t, size=TILE):
    return pl.ds(pl.multiple_of(t * size, size), size)


def wide(mask):
    return jnp.concatenate([mask, mask], axis=1)


def gate_of(left, right):
    tau = jnp.tanh(left)
    sigma = 0.5 * jnp.tanh(0.5 * right) + 0.5
    hidden = tau * sigma
    return hidden, sigma - hidden * tau, hidden * (1.0 - sigma)


class Planes:
    def __init__(self, ref, samples, count):
        self.ref, self.samples, self.count = ref, samples, count

    def rows(self, plane, start, size):
        return pl.ds(pl.multiple_of(plane * self.samples + start, size), size)

    def get(self, t, planes, size=TILE):
        return jnp.concatenate([self.ref[self.rows(c, t * size, size), :] for c in planes], axis=1)

    def put(self, t, planes, value, size=TILE):
        for n, c in enumerate(planes):
            self.ref[self.rows(c, t * size, size), :] = value[:, 128 * n : 128 * n + 128]


class Layers:
    def __init__(self, refs, place):
        self.__dict__.update(refs)
        self.place = place
        self.samples = self.hidden.shape[0]
        self.tiles = self.samples // TILE
        self.gate = Planes(self.stack_in, self.samples, 8)
        self.early_at = 8 * self.samples


    def make_masks(self):
        def step(t, _):
            pos = self.place.seq * self.samples + t * TILE + lax.broadcasted_iota(i32, (TILE, 128), 0)
            end, start = 0, jnp.zeros((TILE, 128), i32)
            for k in range(self.lengths.shape[1]):
                end = end + self.lengths[0, k]
                start = start + jnp.where(end <= pos, self.lengths[0, k], 0)
            for ref, dilation in ((self.mask_long, FIRST_DILATION), (self.mask_short, 1)):
                ref[tile(t), :] = jnp.where(pos - dilation >= start, 1.0, 0.0).astype(bf16)
            return 0

        lax.fori_loop(0, self.tiles, step, 0)

    def make_inverse(self):
        block = lax.broadcasted_iota(i32, (2, 128), 0) * 128 + lax.broadcasted_iota(i32, (2, 128), 1)

        def step(q, found):
            return jnp.maximum(found, jnp.where(block == self.owner[q], q, 0))

        found = lax.fori_loop(0, 256, step, jnp.zeros((2, 128), i32), unroll=8)
        self.inverse_vmem[pl.ds(0, 2), :] = found
        copy = pltpu.make_async_copy(self.inverse_vmem, self.inverse, self.inverse_sem)
        copy.start()
        copy.wait()

    def make_condition(self):
        def step(t, _):
            lanes = tile(t)
            part = self.cond_t[:, lanes].astype(f32)
            padded = jnp.concatenate([part, jnp.zeros((128 - part.shape[0], TILE), f32)], axis=0)
            turned = padded.T.astype(bf16)
            self.units1[tile(t), 1024:] = turned
            self.units2[tile(t), 1024:] = turned
            return 0

        lax.fori_loop(0, self.tiles, step, 0)

    def make_delayed(self):
        def step(t, _):
            mask = self.mask_long[tile(t), :]
            for c in range(4):
                before = self.units1[tile(t - 1), 512 + 128 * c : 640 + 128 * c]
                self.units1[tile(t), 128 * c : 128 * c + 128] = before * mask
            return 0

        lax.fori_loop(1, self.tiles, step, 0)

    def make_first_delayed(self):
        mask = self.mask_long[pl.ds(0, TILE), :]
        for c in range(4):
            lanes = slice(128 * c, 128 * c + 128)
            self.units1[pl.ds(0, TILE), lanes] = self.halo_signal[:, lanes] * mask


    def forward_one(self, t):
        for c in range(2):
            left, right = self.halves(self.units1[tile(t), :], self.full_in[0], c)
            hidden, by_tanh, by_sigmoid = gate_of(left, right)
            self.hidden[tile(t), 256 * c : 256 * c + 256] = hidden.astype(bf16)
            self.gate.put(t, range(2 * c, 2 * c + 2), by_tanh.astype(bf16))
            self.gate.put(t, range(4 + 2 * c, 6 + 2 * c), by_sigmoid.astype(bf16))

    def halves(self, units, weight, c):
        return [dot(units, weight[:, first : first + 256], 1, 0) for first in (256 * c, 512 + 256 * c)]

    def state_one(self, t):
        mask = self.mask_short[tile(t), :].astype(f32)
        for c in range(2):
            lanes = slice(256 * c, 256 * c + 256)
            out = dot(self.hidden[tile(t), :512], self.full_out[:512, lanes], 1, 0)
            state = self.units1[tile(t), 512 + 256 * c : 768 + 256 * c].astype(f32) + out
            rounded = state.astype(bf16)
            self.units2[tile(t), 512 + 256 * c : 768 + 256 * c] = rounded
            delayed = pltpu.roll(rounded.astype(f32), 1, 0)
            self.last_rows[t, :, lanes] = delayed[:8]
            self.units2[tile(t), lanes] = (delayed * wide(mask)).astype(bf16)

    def mend_delayed(self, t):
        source = self.halo_state if t == 0 else self.last_rows.at[t - 1]
        first = lax.broadcasted_iota(i32, (16, 128), 0) == 0
        mask = self.mask_short[pl.ds(t * TILE, 16), :].astype(f32)
        rows = pl.ds(t * TILE, 16)
        for c in range(4):
            lanes = slice(128 * c, 128 * c + 128)
            row = jnp.broadcast_to(source[0:1, lanes], (16, 128)) * mask
            self.units2[rows, lanes] = jnp.where(first, row, self.units2[rows, lanes].astype(f32)).astype(bf16)

    def layer_two(self, t):
        for c in range(2):
            left, right = self.halves(self.units2[tile(t), :], self.full_in[1], c)
            hidden, by_tanh, by_sigmoid = gate_of(left, right)
            self.hidden[tile(t), 512 + 256 * c : 768 + 256 * c] = hidden.astype(bf16)
            gh = dot(self.go[tile(t), :], self.full_out[512 + 256 * c : 768 + 256 * c, :], 1, 1)
            self.gz[tile(t), 256 * c : 256 * c + 256] = (gh * by_tanh).astype(bf16)
            self.gz[tile(t), 512 + 256 * c : 768 + 256 * c] = (gh * by_sigmoid).astype(bf16)

    def units_two(self, t):
        mask = wide(self.mask_short[tile(t), :].astype(f32))
        last = lax.broadcasted_iota(i32, (TILE, 256), 0) == TILE - 1
        gz = self.gz[tile(t), :]
        for c in range(2):
            lanes = slice(256 * c, 256 * c + 256)
            early = dot(gz, self.full_in[1, lanes, :], 1, 1) * mask
            self.first_rows[t, :, lanes] = early[:8]
            moved = jnp.where(last, 0.0, pltpu.roll(early, TILE - 1, 0))
            here = dot(gz, self.full_in[1, 512 + 256 * c : 768 + 256 * c, :], 1, 1)
            self.gx[tile(t), lanes] = self.go[tile(t), lanes].astype(f32) + here + moved
        self.cond_grad[:, tile(t)] = self.condition_part(gz, 1)

    def condition_part(self, gz, layer):
        part = dot(gz, self.full_in[layer, 1024:, :], 1, 1).T
        return part[: self.cond_grad.shape[0], :]

    def mend_gx(self, t):
        source = self.halo_grad if t == self.tiles - 1 else self.first_rows.at[t + 1]
        last = lax.broadcasted_iota(i32, (8, 512), 0) == 7
        rows = pl.ds((t + 1) * TILE - 8, 8)
        row = jnp.broadcast_to(source[0:1, :], (8, 512))
        self.gx[rows, :] = self.gx[rows, :] + jnp.where(last, row, 0.0)

    def round_gx(self, t):
        self.go[tile(t), :512] = self.gx[tile(t), :].astype(bf16)

    def layer_one_back(self, t):
        for c in range(2):
            gh = dot(self.go[tile(t), :], self.full_out[256 * c : 256 * c + 256, :], 1, 1)
            for part in range(2):
                gate = self.gate.get(t, range(4 * part + 2 * c, 4 * part + 2 * c + 2)).astype(f32)
                first = 512 * part + 256 * c
                self.gz[tile(t), first : first + 256] = (gh * gate).astype(bf16)


    def weight_out(self, layer):
        def step(m, _):
            lanes = pl.ds(pl.multiple_of(layer * 512 + m * 256, 256), 256)
            grad = dot(self.hidden[:, lanes], self.go[...], 0, 0)
            for i in range(4):
                for j in range(8):
                    pair = grad[64 * i : 64 * i + 64, 128 * j : 128 * j + 128]
                    first = layer * 128 + (m * 4 + i) * 16 + 2 * j
                    for k, block in enumerate(across(pair[:32], pair[32:])):
                        self.grad_out[first + k] = block.astype(bf16)
            return 0

        lax.fori_loop(0, 2, step, 0)

    def weight_in(self, layer, units, m):
        rows = pl.ds(pl.multiple_of(384 * m, 384), 384)
        grad = dot(units[:, rows], self.gz[...], 0, 0)
        for j in range(8):
            self.grad_in[layer * 8 + j, rows, :] = grad[:, 128 * j : 128 * j + 128]


    def early_units_one(self):
        mask = wide(self.mask_long[pl.ds(0, TILE), :].astype(f32))
        for c in range(2):
            lanes = slice(256 * c, 256 * c + 256)
            early = dot(self.gz[pl.ds(0, TILE), :], self.full_in[0, lanes, :], 1, 1) * mask
            for k in range(2):
                rows = pl.ds(self.early_at + TILE * (2 * c + k), TILE)
                self.stack_in[rows, :] = early[:, 128 * k : 128 * k + 128].astype(bf16)

    def units_one(self, t):
        gz = self.gz[tile(t), :]
        mask = wide(self.mask_long[tile(t), :].astype(f32))
        for c in range(2):
            lanes = slice(256 * c, 256 * c + 256)
            if t > 0:
                early = dot(gz, self.full_in[0, lanes, :], 1, 1)
                self.gx[tile(t - 1), lanes] = self.gx[tile(t - 1), lanes] + early * mask
            here = dot(gz, self.full_in[0, 512 + 256 * c : 768 + 256 * c, :], 1, 1)
            self.gx[tile(t), lanes] = self.gx[tile(t), lanes] + here
        self.cond_grad[:, tile(t)] = self.cond_grad[:, tile(t)] + self.condition_part(gz, 0)

    def put_out(self, src, dst, sem):
        copy = pltpu.make_async_copy(src, dst, sem)
        copy.start()
        self.pending.append(copy)

    def send_gx(self, t):
        self.units2[tile(t), :512] = self.gx[tile(t), :].astype(bf16)
        self.put_out(self.units2.at[tile(t), pl.ds(0, 512)], self.grad_x.at[tile(t)], self.gx_sems.at[t])

    def outputs(self, n):
        rows = tile(n, 256)
        for c in range(4):
            lanes = slice(256 * c, 256 * c + 256)
            out = dot(self.hidden[rows, :], self.full_out[:, lanes], 1, 0)
            if c < 2:
                out = out + self.units1[rows, 512 + 256 * c : 768 + 256 * c].astype(f32)
            self.go[rows, lanes] = out.astype(bf16)
        self.output_copy(n).start()

    def output_copy(self, n):
        rows = tile(n, 256)
        return pltpu.make_async_copy(self.go.at[rows], self.both.at[rows], self.stage_sems.at[n])

    def drain(self, copies):
        for copy in copies:
            copy.wait()

    def end_gx(self, near, early_halo):
        t = self.tiles - 1
        near.arrived(*early_halo)
        for c in range(4):
            lanes = slice(128 * c, 128 * c + 128)
            late = self.halo_early[pl.ds(TILE * c, TILE), :].astype(f32)
            self.gx[tile(t), lanes] = self.gx[tile(t), lanes] + late
        self.send_gx(t)

    def tail(self, near, early_halo, small, rest_out):
        work = {}
        work[TO, 3] = [lambda: self.units_one(0)]
        work[ONE, 2] = [lambda: self.units_one(1), lambda: self.send_gx(0), lambda: near.sent(*early_halo)]
        work[THREE, 0] = [lambda: self.units_one(2), lambda: self.send_gx(1), lambda: self.outputs(0)]
        work[ONE, 3] = [lambda: self.outputs(1)]
        work[THREE, 1] = [lambda: self.outputs(2), *rest_out, lambda: small[1].start()]
        work[THREE, 2] = [
            lambda: self.units_one(3),
            lambda: self.send_gx(2),
            lambda: self.end_gx(near, early_halo),
            lambda: small[0].start(),
            lambda: self.outputs(3),
        ]
        work[TWO, 3] = [lambda: loop(4, self.samples // 256, self.outputs)]
        return [work.get(step, []) for step in REDUCE_ORDER]


def loop(first, last, body):
    lax.fori_loop(first, last, lambda t, _: (body(t), 0)[1], 0)


class Neighbours:
    def __init__(self, place):
        self.p = place
        self.has = {1: place.seq < 7, -1: place.seq > 0}

    def copy(self, src, dst, sems, way):
        return pltpu.make_async_remote_copy(
            src_ref=src, dst_ref=dst, send_sem=sems[0], recv_sem=sems[1],
            device_id=(self.p.row, self.p.seq + way), device_id_type=MESH)

    def start(self, src, dst, sems, way):
        pl.when(self.has[way])(lambda: self.copy(src, dst, sems, way).start())

    def sent(self, src, dst, sems, way):
        pl.when(self.has[way])(lambda: self.copy(src, dst, sems, way).wait_send())

    def arrived(self, src, dst, sems, way):
        pl.when(self.has[-way])(lambda: self.copy(src, dst, sems, way).wait_recv())


INPUTS = ("owner", "lengths", "signal", "cot_x", "cot_skip", "cond_t", "w_in", "w_out")
OUTPUTS = ("both", "grad_x", "grad_cond_t", "sum_in", "sum_out")
SCRATCH = dict(
    stack_in=pltpu.VMEM((32 * ROWS_IN, 128), bf16),
    stack_out=pltpu.VMEM((32 * ROWS_OUT, 128), bf16),
    full_in=pltpu.VMEM((2, 1152, 1024), bf16),
    full_out=pltpu.VMEM((1024, 1024), bf16),
    units1=pltpu.VMEM((2048, 1152), bf16),
    units2=pltpu.VMEM((2048, 1152), bf16),
    hidden=pltpu.VMEM((2048, 1024), bf16),
    gz=pltpu.VMEM((2048, 1024), bf16),
    go=pltpu.VMEM((2048, 1024), bf16),
    gx=pltpu.VMEM((2048, 512), f32),
    grad_in=pltpu.VMEM((16, 1152, 128), f32),
    grad_out=pltpu.VMEM((256, 32, 128), bf16),
    mask_long=pltpu.VMEM((2048, 128), bf16),
    mask_short=pltpu.VMEM((2048, 128), bf16),
    halo_signal=pltpu.VMEM((TILE, 512), bf16),
    halo_early=pltpu.VMEM((4 * TILE, 128), bf16),
    last_rows=pltpu.VMEM((4, 8, 512), f32),
    first_rows=pltpu.VMEM((4, 8, 512), f32),
    halo_state=pltpu.VMEM((8, 512), f32),
    halo_grad=pltpu.VMEM((8, 512), f32),
    reduce_in=pltpu.VMEM((32 * ROWS_IN, 128), bf16),
    reduce_out=pltpu.VMEM((32 * ROWS_OUT, 128), bf16),
    cond_grad=pltpu.VMEM((80, 2048), f32),
    share_in=pltpu.VMEM((ROWS_IN, 128), f32),
    share_out=pltpu.VMEM((ROWS_OUT, 128), f32),
    small_sems=pltpu.SemaphoreType.DMA((3,)),
    inverse_vmem=pltpu.VMEM((8, 128), i32),
    inverse=pltpu.SMEM((8, 128), i32),
    inverse_sem=pltpu.SemaphoreType.DMA,
    load_sems=pltpu.SemaphoreType.DMA((3,)),
    gx_sems=pltpu.SemaphoreType.DMA((4,)),
    stage_sems=pltpu.SemaphoreType.DMA((8,)),
    halo_sems=pltpu.SemaphoreType.DMA((8,)),
)


def network_kernel(*refs):
    names = INPUTS + OUTPUTS + tuple(SCRATCH)
    sems = refs[len(names) :]
    gather_sems, reduce_sems = len(GATHER_SEMS), len(REDUCE_SEMS)
    sems_in, sems = sems[:gather_sems], sems[gather_sems:]
    sems_out, sems = sems[:gather_sems], sems[gather_sems:]
    sum_sems_out, sum_sems_in = sems[:reduce_sems], sems[reduce_sems:]
    place = Place()
    n = Layers(dict(zip(names, refs)), place)
    n.pending = []
    near = Neighbours(place)
    samples, tiles = n.samples, n.tiles

    targets = ((n.signal, n.units1, 512), (n.cot_x, n.go, 0), (n.cot_skip, n.go, 512))
    loads = [
        pltpu.make_async_copy(src, dst.at[:, pl.ds(lane, 512)], n.load_sems.at[k])
        for k, (src, dst, lane) in enumerate(targets)
    ]
    for copy in loads:
        copy.start()
    place.announce()
    me = place.row * 8 + place.seq
    pairs_in, blocks_out = n.stack_in.reshape(128, 144, 128), n.stack_out.reshape(256, 32, 128)
    spread = n.grad_in
    spread[0, :ROWS_IN, :] = jnp.zeros((ROWS_IN, 128), f32)
    spread[1, : 8 * 69, :] = n.w_in[...]
    for k in range(8):
        spread[0, pl.ds(72 * k, 69), :] = spread[1, pl.ds(k, 72, 8), :][:69]
    for m in range(4):
        pairs_in[me * 4 + m] = spread[0, 144 * m : 144 * m + 144, :].astype(bf16)

    for k in range(8):
        block = n.w_out[k]
        blocks_out[me * 8 + k] = jnp.concatenate([block[:32], block[32:]], axis=1).astype(bf16)

    def cleared(refs, when):
        @pl.when(when)
        def _():
            for ref in refs:
                ref[...] = jnp.zeros_like(ref)

    cleared([n.halo_signal, n.halo_state], place.seq == 0)
    cleared([n.halo_early, n.halo_grad], place.seq == 7)
    n.make_masks()
    n.make_inverse()
    n.make_condition()
    n.full_in[0, 1104:, :] = jnp.zeros((48, 1024), bf16)
    n.full_in[1, 1104:, :] = jnp.zeros((48, 1024), bf16)
    place.all_here()

    halo = [(n.halo_sems.at[2 * k], n.halo_sems.at[2 * k + 1]) for k in range(4)]
    signal_halo = (n.signal.at[pl.ds(samples - TILE, TILE)], n.halo_signal, halo[0], 1)
    state_halo = (n.last_rows.at[tiles - 1], n.halo_state, halo[1], 1)
    grad_halo = (n.first_rows.at[0], n.halo_grad, halo[2], -1)
    early_halo = (n.stack_in.at[pl.ds(n.early_at, 4 * TILE)], n.halo_early, halo[3], -1)
    into = Gather(place, pairs_in, 4, sems_in)
    out = Gather(place, blocks_out, 8, sems_out)
    order = [place.z] + place.others
    into.start()
    into.start_sides()
    out.start()
    for k in range(3):
        into.along_z(k)
        out.relay(k, 0)
        out.relay(k, 1)
        into.first(order[k])
    into.rest(order[0])
    into.first(order[3])
    near.start(*signal_halo)
    out.start_sides()
    for k in range(3):
        out.spread(k, 0)
        out.spread(k, 1)
    for copy in loads:
        copy.wait()
    n.make_delayed()
    for k in range(1, tiles):
        into.rest(order[k])
    into.finish()
    assemble_in(n.inverse, pairs_in, spread, n.full_in, 0)
    assemble_in(n.inverse, pairs_in, spread, n.full_in, 1)

    near.arrived(*signal_halo)
    n.make_first_delayed()
    out.first(order[0])
    out.first(order[1])
    loop(0, 2, n.forward_one)
    out.first(order[2])
    out.first(order[3])
    out.rest(order[0])
    out.rest(order[1])
    loop(2, tiles, n.forward_one)
    out.rest(order[2])
    out.rest(order[3])
    out.finish()
    assemble_out(n.inverse, blocks_out, n.full_out, 0)
    assemble_out(n.inverse, blocks_out, n.full_out, 1)
    n.state_one(tiles - 1)
    near.start(*state_halo)
    loop(0, tiles - 1, n.state_one)
    for t in range(1, tiles):
        n.mend_delayed(t)
    near.arrived(*state_halo)
    n.mend_delayed(0)

    loop(0, tiles, n.layer_two)
    n.units_two(0)
    near.start(*grad_halo)
    loop(1, tiles, n.units_two)
    n.weight_out(1)
    for t in range(tiles - 1):
        n.mend_gx(t)
    near.arrived(*grad_halo)
    n.mend_gx(tiles - 1)
    loop(0, tiles, n.round_gx)
    n.weight_out(0)

    reduce_out = Reduce(
        place, pack_out(n.owner, n.grad_out), ROWS_OUT,
        reduce_bufs(n.stack_out, n.reduce_out, ROWS_OUT), sum_sems_out,
    )
    reduce_in = Reduce(
        place, pack_in(n.owner, n.grad_in), ROWS_IN,
        reduce_bufs(n.stack_in, n.reduce_in, ROWS_IN), sum_sems_in,
    )
    sum_out = reduce_out.events(n.share_out, REDUCE_ORDER_OUT)
    sum_in = reduce_in.events(n.share_in, REDUCE_ORDER)

    def run(*events):
        for event in events:
            event()

    small = [
        pltpu.make_async_copy(a, b, n.small_sems.at[k])
        for k, (a, b) in enumerate(
            ((n.cond_grad, n.grad_cond_t), (n.share_out, n.sum_out), (n.share_in, n.sum_in))
        )
    ]
    run(*sum_out[:2])
    n.weight_in(1, n.units2, 0)
    run(*sum_out[2:5], sum_out[6])
    n.weight_in(1, n.units2, 1)
    run(sum_out[5], sum_out[7])
    n.weight_in(1, n.units2, 2)
    run(*sum_out[8:10])
    loop(0, 2, n.layer_one_back)
    run(*sum_out[10:12])
    loop(2, tiles, n.layer_one_back)
    run(*sum_out[12:14])
    n.early_units_one()
    near.start(*early_halo)
    n.weight_in(0, n.units1, 0)
    run(sum_out[14])
    n.weight_in(0, n.units1, 1)
    n.weight_in(0, n.units1, 2)
    for event, work in zip(sum_in, n.tail(near, early_halo, small, [sum_out[15], reduce_out.finish])):
        event()
        for part in work:
            part()
    reduce_in.finish()
    small[2].start()
    for halo in (signal_halo, state_halo, grad_halo):
        near.sent(*halo)
    n.drain(n.pending)
    loop(0, samples // 256, lambda k: n.output_copy(k).wait())
    n.drain(small)


ANY = pl.BlockSpec(memory_space=pl.ANY)


def shampoo_block(grad, left, right, root_left, root_right, weight, rate):
    low = grad.astype(bf16)
    new_left = 0.5 * left + 0.5 * dot(low, low, 1, 1)
    new_right = 0.5 * right + 0.5 * dot(low, low, 0, 0)
    step = dot(dot(root_left.astype(bf16), low, 1, 0).astype(bf16), root_right.astype(bf16), 1, 0)
    return new_left, new_right, weight - rate * step


BLOCKS_IN = ("w_in", "left_in", "root_left_in", "right_in", "root_right_in")
BLOCKS_OUT = ("w_out", "left_out", "root_left_out", "right_out", "root_right_out")
SUMS = ("sum_in", "sum_out")
LARGE = ("out_x", "skip_sum", "grad_x")
LOW = ("both", "grad_x")


def finish_kernel(*refs):
    taken = SUMS + BLOCKS_IN + BLOCKS_OUT
    names = ["from_" + a for a in taken + LOW + ("cond",)]
    names += ["to_" + a for a in LARGE + ("cond", "grad_in", "grad_out")]
    names += ["to_" + a for kind in ("in", "out") for a in ("w_" + kind, "left_" + kind, "right_" + kind)]
    names += list(taken) + ["grad_in", "grad_out", "large", "both", "low", "cond", "load_sems", "store_sems"]
    r = dict(zip(names, refs))
    loads, stores, sems = {}, {}, iter(range(64))

    def move(table, key, src, dst, sem):
        table[key] = pltpu.make_async_copy(src, dst, r[sem].at[next(sems)])

    for a in taken:
        there = r[a].at[pl.ds(0, 552)] if a in BLOCKS_IN[:3] else r[a]
        move(loads, a, r["from_" + a], there, "load_sems")
    for m in range(4):
        move(loads, ("both", m), r["from_both"].at[tile(m)], r["both"].at[tile(m)], "load_sems")
        move(loads, ("low", m), r["from_grad_x"].at[tile(m)], r["low"].at[tile(m)], "load_sems")
    move(loads, "cond", r["from_cond"], r["cond"], "load_sems")
    sems = iter(range(64))
    for m in range(4):
        for k in range(3):
            move(stores, (k, m), r["large"].at[k, tile(m)], r["to_" + LARGE[k]].at[tile(m)], "store_sems")
    for a in ("cond", "grad_in", "w_in", "left_in", "right_in", "grad_out", "w_out", "left_out", "right_out"):
        here = r[a].at[pl.ds(0, 552)] if a in ("grad_in", "w_in", "left_in") else r[a]
        move(stores, a, here, r["to_" + a], "store_sems")
    for copy in loads.values():
        copy.start()

    def widen(m, name):
        loads[name, m].wait()
        for k in (0, 1) if name == "both" else (2,):
            lanes = slice(512 * (k % 2), 512 * (k % 2) + 512)
            r["large"][k, tile(m), :] = r[name][tile(m), lanes].astype(f32)
            stores[k, m].start()

    for a in ("sum_in",) + BLOCKS_IN:
        loads[a].wait()
    for k in range(8):
        at, put = pl.ds(k, 72, 8), pl.ds(k, 69, 8)
        grad = r["sum_in"][72 * k : 72 * k + 72, :]
        r["grad_in"][at, :] = grad
        r["left_in"][put, :], r["right_in"][k], r["w_in"][put, :] = shampoo_block(
            grad[:69], r["left_in"][at, :][:69], r["right_in"][k], r["root_left_in"][at, :][:69],
            r["root_right_in"][k], r["w_in"][at, :][:69], rate_in,
        )
        if k % 2 == 0:
            widen(k // 2, "both")
    for a in ("grad_in", "w_in", "left_in", "right_in"):
        stores[a].start()
    for a in ("sum_out", "cond") + BLOCKS_OUT:
        loads[a].wait()
    stores["cond"].start()
    for k in range(8):
        folded = r["sum_out"][32 * k : 32 * k + 32, :]
        grad = jnp.concatenate([folded[:, :64], folded[:, 64:]], axis=0)
        r["grad_out"][k] = grad
        r["left_out"][k], r["right_out"][k], r["w_out"][k] = shampoo_block(
            grad, r["left_out"][k], r["right_out"][k], r["root_left_out"][k], r["root_right_out"][k],
            r["w_out"][k], rate_out,
        )
        if k % 2 == 0:
            widen(k // 2, "low")
    for a in ("grad_out", "w_out", "left_out", "right_out"):
        stores[a].start()
    for copy in stores.values():
        copy.wait()


def rows_first(blocks):
    return blocks.transpose(1, 0, 2)


def fused_local(
    signal, condition, lengths, owner, grad_out, grad_skip, w_in, w_out,
    left_in, right_in, root_left_in, root_right_in,
    left_out, right_out, root_left_out, root_right_out,
):
    samples, width, mels = signal.shape[1], signal.shape[2], condition.shape[2]
    block = lambda *shape: jax.ShapeDtypeStruct(shape, f32)
    low = [jax.ShapeDtypeStruct((samples, lanes), bf16) for lanes in (2 * width, width)]
    large = [block(samples, width)] * 3 + [block(mels, samples)]
    rows_in = rows_first(w_in).reshape(552, 128)
    both, grad_x, grad_cond_t, sum_in, sum_out = pl.pallas_call(
        network_kernel,
        out_shape=low + [block(mels, samples), block(ROWS_IN, 128), block(ROWS_OUT, 128)],
        in_specs=[SMEM, SMEM, ANY, ANY, ANY, VMEM, VMEM, VMEM],
        out_specs=[ANY] * 5,
        scratch_shapes=list(SCRATCH.values()) + GATHER_SEMS * 2 + REDUCE_SEMS * 2,
        name="network",
        compiler_params=pltpu.CompilerParams(
            collective_id=0, has_side_effects=True, vmem_limit_bytes=64 << 20
        ),
    )(
        owner, lengths, signal[0], grad_out[0], grad_skip[0], condition[0].T, rows_in, w_out,
    )
    taken = (
        sum_in, sum_out,
        rows_in, rows_first(left_in).reshape(552, 69), rows_first(root_left_in).reshape(552, 69),
        right_in, root_right_in,
        w_out, left_out, root_left_out, right_out, root_right_out,
    )
    new_in = [block(552, 128), block(552, 69), block(8, 128, 128)]
    new_out = [block(8, 64, 64)] * 3
    held = [pltpu.VMEM((584 if a.shape[0] == 552 else a.shape[0], *a.shape[1:]), f32) for a in taken]
    outs = pl.pallas_call(
        finish_kernel,
        out_shape=large + [new_in[0], new_out[0]] + new_in + new_out,
        in_specs=[ANY] * (len(taken) + 3),
        out_specs=[ANY] * 12,
        scratch_shapes=held
        + [pltpu.VMEM((584, 128), f32), pltpu.VMEM((8, 64, 64), f32)]
        + [pltpu.VMEM((3, samples, width), f32)]
        + [pltpu.VMEM(a.shape, a.dtype) for a in low + [block(mels, samples)]]
        + [pltpu.SemaphoreType.DMA((32,))] * 2,
        name="finish",
        compiler_params=pltpu.CompilerParams(vmem_limit_bytes=63 << 20),
    )(*taken, both, grad_x, grad_cond_t)
    out_x, skip_sum, grad_x, grad_cond_t, g_in, g_out, nw_in, nl_in, nr_in, nw_out, nl_out, nr_out = outs

    def blocks_first(rows):
        return rows.reshape(69, 8, rows.shape[1]).transpose(1, 0, 2)

    return (
        out_x[None], skip_sum[None], grad_x[None], grad_cond_t.T[None],
        blocks_first(g_in), g_out, blocks_first(nl_in), nr_in, nl_out, nr_out, blocks_first(nw_in), nw_out,
    )


def local(
    signal,
    condition,
    lengths,
    owner,
    grad_out,
    grad_skip,
    w_in,
    w_out,
    left_in,
    right_in,
    root_left_in,
    root_right_in,
    left_out,
    right_out,
    root_left_out,
    root_right_out,
):
    fused = (lax.axis_size("row"), lax.axis_size("seq"), signal.shape[1]) == (4, 8, 4 * TILE)
    audio_samples = signal.shape[1]
    width = signal.shape[2]
    if fused:
        return fused_local(
            signal, condition, lengths, owner, grad_out, grad_skip, w_in, w_out,
            left_in, right_in, root_left_in, root_right_in,
            left_out, right_out, root_left_out, root_right_out,
        )
    stack_in = lax.all_gather(w_in.astype(bf16), ("row", "seq"), axis=0, tiled=True)
    stack_out = lax.all_gather(w_out.astype(bf16), ("row", "seq"), axis=0, tiled=True)
    inverse = jnp.argsort(owner)
    input_weight = from_blocks(jnp.take(stack_in, inverse, axis=0), 16, 8)
    output_weight = from_blocks(jnp.take(stack_out, inverse, axis=0), 8, 16)
    sample_positions = lax.axis_index("seq") * audio_samples + jnp.arange(
        audio_samples, dtype=jnp.int32
    )
    longer_mask = receptive_mask(lengths, sample_positions, FIRST_DILATION)[:, :, None]
    mask_short = receptive_mask(lengths, sample_positions, 1)[:, :, None]
    preceding_longer = shifted(signal[:, audio_samples - FIRST_DILATION :, :], "seq", 1)
    delayed_one = jnp.concatenate([preceding_longer, signal], axis=1)[:, :audio_samples, :]
    delayed_one = jnp.where(longer_mask, delayed_one, jnp.zeros_like(delayed_one))
    units_one = jnp.concatenate([delayed_one, signal, condition], axis=2)
    tanh_one, sigm_one, hidden_one, proj_one = gate_forward(
        units_one, input_weight[0], output_weight[0]
    )
    first_layer_state = signal.astype(jnp.float32) + proj_one[..., :width]
    rounded_one = first_layer_state.astype(jnp.bfloat16)
    before_short = shifted(rounded_one[:, audio_samples - 1 :, :], "seq", 1)
    delayed_two = jnp.concatenate([before_short, rounded_one[:, : audio_samples - 1, :]], axis=1)
    delayed_two = jnp.where(mask_short, delayed_two, jnp.zeros_like(delayed_two))
    units_two = jnp.concatenate([delayed_two, rounded_one, condition], axis=2)
    tanh_two, sigm_two, hidden_two, proj_two = gate_forward(
        units_two, input_weight[1], output_weight[1]
    )
    out_x = first_layer_state + proj_two[..., :width]
    skip_sum = proj_one[..., width:] + proj_two[..., width:]
    grad_next = grad_out.astype(jnp.float32)
    gin_two, gout_two, units_grad_two = gate_backward(
        units_two,
        tanh_two,
        sigm_two,
        hidden_two,
        input_weight[1],
        output_weight[1],
        grad_next,
        grad_skip,
    )
    early_two = jnp.where(mask_short, units_grad_two[..., :width], 0.0)
    from_short = shifted(early_two[:, :1, :], "seq", -1)
    grad_state = (
        grad_next
        + units_grad_two[..., width : 2 * width]
        + jnp.concatenate([early_two[:, 1:, :], from_short], axis=1)
    )
    gin_one, gout_one, units_grad_one = gate_backward(
        units_one,
        tanh_one,
        sigm_one,
        hidden_one,
        input_weight[0],
        output_weight[0],
        grad_state,
        grad_skip,
    )
    earlier_first = jnp.where(longer_mask, units_grad_one[..., :width], 0.0)
    taken_longer = shifted(earlier_first[:, :FIRST_DILATION, :], "seq", -1)
    grad_x = (
        grad_state
        + units_grad_one[..., width : 2 * width]
        + jnp.concatenate([earlier_first[:, FIRST_DILATION:, :], taken_longer], axis=1)
    )
    grad_cond = units_grad_one[..., 2 * width :] + units_grad_two[..., 2 * width :]
    local_in = jnp.take(to_blocks(jnp.stack([gin_one, gin_two]), 16, 8), owner, axis=0)
    local_out = jnp.take(to_blocks(jnp.stack([gout_one, gout_two]), 8, 16), owner, axis=0)
    grad_in_blocks, grad_out_blocks = (
        lax.psum_scatter(local_in, ("row", "seq"), scatter_dimension=0, tiled=True),
        lax.psum_scatter(local_out, ("row", "seq"), scatter_dimension=0, tiled=True),
    )
    new_left_in, new_right_in, new_w_in = shampoo(
        grad_in_blocks, left_in, right_in, root_left_in, root_right_in, w_in, rate_in
    )
    new_left_out, new_right_out, new_w_out = shampoo(
        grad_out_blocks, left_out, right_out, root_left_out, root_right_out, w_out, rate_out
    )
    return (
        out_x,
        skip_sum,
        grad_x,
        grad_cond,
        grad_in_blocks,
        grad_out_blocks,
        new_left_in,
        new_right_in,
        new_left_out,
        new_right_out,
        new_w_in,
        new_w_out,
    )


def solution(mesh):
    tokens, blocks = P("row", "seq", None), P(("row", "seq"), None, None)
    in_specs = (tokens, tokens, P("row", None), P(), tokens, tokens) + (blocks,) * 10
    out_specs = (tokens,) * 4 + (blocks,) * 8
    return jax.shard_map(local, mesh=mesh, in_specs=in_specs, out_specs=out_specs, check_vma=False)
```

```python
import jax
import jax.numpy as jnp
from jax import lax
from jax.experimental import pallas as pl
from jax.experimental.pallas import tpu as pltpu
from jax.sharding import PartitionSpec as P

FIRST_DILATION = 512
MESH = pl.DeviceIdType.MESH
bf16, f32, i32 = jnp.bfloat16, jnp.float32, jnp.int32

highest = lax.Precision.HIGHEST
rate_in = 0.3
rate_out = 1.0

TILE = 512
ROWS_IN = 576
ROWS_OUT = 256


def shifted(block, axis, distance):
    devices = range(lax.axis_size(axis))
    route = [(i - distance, i) for i in devices if i - distance in devices]
    return lax.ppermute(block, axis, route)


def to_blocks(full, row_parts, col_parts):
    layers, rows, cols = full.shape
    shaped = full.reshape(layers, row_parts, rows // row_parts, col_parts, cols // col_parts)
    return shaped.transpose(0, 1, 3, 2, 4).reshape(
        layers * row_parts * col_parts, rows // row_parts, cols // col_parts
    )


def from_blocks(blocks, row_parts, col_parts):
    count, block_rows, block_cols = blocks.shape
    layers = count // (row_parts * col_parts)
    shaped = blocks.reshape(layers, row_parts, col_parts, block_rows, block_cols)
    return shaped.transpose(0, 1, 3, 2, 4).reshape(
        layers, row_parts * block_rows, col_parts * block_cols
    )


def receptive_mask(lengths, sample_positions, dilation):
    ends = jnp.cumsum(lengths, axis=1)
    starts = jnp.sum(
        jnp.where(ends[:, None, :] <= sample_positions[None, :, None], lengths[:, None, :], 0),
        axis=2,
    )
    return sample_positions[None, :] - dilation >= starts


def gate_forward(units, input_weight, output_weight):
    pre = jnp.einsum("ptk,kg->ptg", units, input_weight, preferred_element_type=jnp.float32)
    half = pre.shape[2] // 2
    tanh_part = jnp.tanh(pre[..., :half])
    sigm_part = jax.nn.sigmoid(pre[..., half:])
    hidden = (tanh_part * sigm_part).astype(jnp.bfloat16)
    projected = jnp.einsum("ptg,gk->ptk", hidden, output_weight, preferred_element_type=jnp.float32)
    return (tanh_part, sigm_part, hidden, projected)


def gate_backward(
    units, tanh_part, sigm_part, hidden, input_weight, output_weight, grad_state, grad_skip
):
    grad_proj = jnp.concatenate([grad_state, grad_skip.astype(jnp.float32)], axis=2).astype(
        jnp.bfloat16
    )
    grad_wout = jnp.einsum("ptg,ptk->gk", hidden, grad_proj, preferred_element_type=jnp.float32)
    grad_hidden = jnp.einsum(
        "ptk,gk->ptg", grad_proj, output_weight, preferred_element_type=jnp.float32
    )
    grad_tanh = grad_hidden * sigm_part * (1.0 - tanh_part * tanh_part)
    grad_sigm = grad_hidden * tanh_part * sigm_part * (1.0 - sigm_part)
    grad_pre = jnp.concatenate([grad_tanh, grad_sigm], axis=2).astype(jnp.bfloat16)
    grad_win = jnp.einsum("ptk,ptg->kg", units, grad_pre, preferred_element_type=jnp.float32)
    grad_units = jnp.einsum(
        "ptg,kg->ptk", grad_pre, input_weight, preferred_element_type=jnp.float32
    )
    return (grad_win, grad_wout, grad_units)


def shampoo(grad, left, right, root_left, root_right, weight, rate):
    new_left = 0.5 * left + 0.5 * jnp.einsum("bij,bkj->bik", grad, grad, precision=highest)
    new_right = 0.5 * right + 0.5 * jnp.einsum("bji,bjk->bik", grad, grad, precision=highest)
    step = jnp.einsum("bij,bjk->bik", root_left, grad, precision=highest)
    step = jnp.einsum("bij,bjk->bik", step, root_right, precision=highest)
    return (new_left, new_right, weight - rate * step)


class Place:
    def __init__(self):
        self.row, self.seq = lax.axis_index("row"), lax.axis_index("seq")
        self.z, self.core = self.seq // 2, self.seq % 2
        x, y = self.row % 2, self.row // 2
        self.rows = (
            self.row,
            self.row + 1 - 2 * x,
            self.row + 2 - 4 * y,
            self.row + 3 - 2 * x - 4 * y,
        )
        self.x_peer = (self.rows[1], self.seq)
        self.y_peer = (self.rows[2], self.seq)
        self.sibling = (self.row, self.seq + 1 - 2 * self.core)
        self.near = self.mirrored(self.z)
        self.others = [self.mirrored(t) for t in (1 - self.near, 2, 3)]

    def mirrored(self, z):
        return z + self.z // 2 * (3 - 2 * z)

    def z_peer(self, z):
        return (self.row, 2 * z + self.core)

    def owner(self, rel, z, core=None):
        core = self.core if core is None else core
        return self.rows[rel] * 8 + 2 * z + core

    def announce(self):
        peers = [self.x_peer, self.y_peer, self.sibling] + [self.z_peer(z) for z in self.others]
        for peer in peers:
            pl.semaphore_signal(
                pltpu.get_barrier_semaphore(), inc=1, device_id=peer, device_id_type=MESH
            )

    def all_here(self):
        pl.semaphore_wait(pltpu.get_barrier_semaphore(), 6)


class Gather:
    def __init__(self, place, stack, count, sems):
        self.p, self.stack, self.count = place, stack, count
        self.send_sem, self.z_sems, self.x_sems, self.y_sems, self.s_sem = sems
        self.sent = 0

    def at(self, rel, z, half=None, core=None):
        start = self.p.owner(rel, z, core) * self.count
        if half is None:
            return self.stack.at[pl.ds(start, self.count)]
        part = self.count // 2
        return self.stack.at[pl.ds(start + half * part, part)]

    def copy(self, ref, sem, peer):
        return pltpu.make_async_remote_copy(
            src_ref=ref, dst_ref=ref, send_sem=self.send_sem.at[0], recv_sem=sem, device_id=peer, device_id_type=MESH
        )

    def send(self, ref, sem, peer):
        self.copy(ref, sem, peer).start()
        self.sent += 1

    def arrived(self, ref, sem, peer):
        self.copy(ref, sem, peer).wait_recv()

    def to_x(self, kind, rel, z, half):
        self.send(self.at(rel, z, half), self.x_sems.at[kind * 4 + z], self.p.x_peer)

    def to_y(self, kind, rel, z, half):
        self.send(self.at(rel, z, half), self.y_sems.at[kind * 4 + z], self.p.y_peer)

    def to_sibling(self, rel, z, half):
        self.send(self.at(rel, z, half), self.s_sem.at[0], self.p.sibling)

    def sides(self, z, half):
        if half == 0:
            self.to_x(0, 0, z, 0)
            self.to_y(1, 0, z, 0)
        else:
            self.to_y(0, 0, z, 1)
            self.to_x(1, 0, z, 1)
        self.to_sibling(0, z, half)

    def z_copy(self, src, half, z):
        return self.copy(self.at(0, src, half), self.z_sems.at[2 * src + half], self.p.z_peer(z))

    def z_passed(self, n, half):
        p = self.p
        outer, inner = p.mirrored(0), p.mirrored(2)
        near, far, farthest = p.others
        src, z = ((p.z, inner), (near, inner), (far, outer), (farthest, outer))[n]
        return self.z_copy(src, half, z)

    def pass_on(self, n, half):
        pl.when(self.p.near == 1)(lambda: self.z_passed(n, half).start())

    def start(self):
        p = self.p
        for half in range(2):
            self.z_copy(p.z, half, p.mirrored(1 - p.near)).start()
            self.sent += 1
            self.pass_on(0, half)

    def start_sides(self):
        for half in range(2):
            self.sides(self.p.z, half)

    def relay(self, n, half):
        z = self.p.others[n]
        self.arrived(self.at(0, z, half), self.z_sems.at[2 * z + half], self.p.z_peer(z))
        self.pass_on(n + 1, half)

    def spread(self, n, half):
        self.sides(self.p.others[n], half)

    def along_z(self, n):
        for half in range(2):
            self.relay(n, half)
            self.spread(n, half)

    def first(self, z):
        p = self.p
        self.arrived(self.at(1, z, 0), self.x_sems.at[z], p.x_peer)
        self.to_y(2, 1, z, 0)
        self.to_sibling(1, z, 0)
        self.arrived(self.at(2, z, 1), self.y_sems.at[z], p.y_peer)
        self.to_x(2, 2, z, 1)
        self.to_sibling(2, z, 1)

    def second(self, z):
        p = self.p
        self.arrived(self.at(1, z, 1), self.x_sems.at[4 + z], p.x_peer)
        self.to_sibling(1, z, 1)
        self.arrived(self.at(2, z, 0), self.y_sems.at[4 + z], p.y_peer)
        self.to_sibling(2, z, 0)

    def third(self, z):
        p = self.p
        self.arrived(self.at(3, z, 1), self.x_sems.at[8 + z], p.x_peer)
        self.to_sibling(3, z, 1)
        self.arrived(self.at(3, z, 0), self.y_sems.at[8 + z], p.y_peer)
        self.to_sibling(3, z, 0)

    def rest(self, z):
        self.second(z)
        self.third(z)

    def bytes_of(self, halves):
        return self.stack.at[pl.ds(0, halves * self.count // 2)]

    def finish(self):
        self.arrived(self.bytes_of(32), self.s_sem.at[0], self.p.sibling)
        self.copy(self.bytes_of(self.sent), self.s_sem.at[0], self.p.sibling).wait_send()

        @pl.when(self.p.near == 1)
        def _():
            self.copy(self.bytes_of(8), self.s_sem.at[0], self.p.sibling).wait_send()


GATHER_SEMS = [pltpu.SemaphoreType.DMA((n,)) for n in (1, 8, 12, 12, 1)]


def pick(which, zero, one):
    return jnp.where(jnp.full(zero.shape, which, i32) == 0, zero, one)


def assemble_in(inverse, stack, spread, weight, layer):
    def column(j, _):
        for i in range(16):
            q = inverse[layer, i * 8 + j]
            pair = stack[lax.div(q, 2)].astype(f32)
            spread[j, pl.ds(69 * i, 72), :] = pick(lax.rem(q, 2), pair[:72], pair[72:])
        weight[layer, :1104, pl.ds(pl.multiple_of(j * 128, 128), 128)] = spread[j, :1104, :].astype(bf16)
        return 0

    lax.fori_loop(0, 8, column, 0)


def across(top, bottom):
    left = lax.broadcasted_iota(i32, top.shape, 1) < 64
    return (
        jnp.where(left, top, pltpu.roll(bottom, 64, 1)),
        jnp.where(left, pltpu.roll(top, 64, 1), bottom),
    )


def assemble_out(inverse, stack, weight, layer):
    def line(i, _):
        for m in range(8):
            two = [stack[inverse[layer, i * 16 + 2 * m + h]].astype(f32) for h in range(2)]
            for k, rows in enumerate(across(*two)):
                first = pl.multiple_of(layer * 512 + i * 64 + 32 * k, 32)
                weight[pl.ds(first, 32), 128 * m : 128 * m + 128] = rows.astype(bf16)
        return 0

    lax.fori_loop(0, 8, line, 0)


VMEM = pl.BlockSpec(memory_space=pltpu.VMEM)
SMEM = pl.BlockSpec(memory_space=pltpu.SMEM)


class Reduce:
    def __init__(self, place, pack, rows, bufs, sems):
        self.p, self.pack, self.rows, self.half, self.pair = place, pack, rows, rows // 2, rows // 4
        (self.s_out, self.s_in, self.x1_out, self.x1_in, self.y1_out, self.y1_in,
         self.x2_out, self.x2_in, self.y2_out, self.y2_in, self.z_out, self.z_in) = bufs
        self.send_sem, self.s_sems, self.x1_sems, self.y1_sems, self.x2_sems, self.y2_sems, self.z_sems = sems
        self.sent = 0

    def rows_at(self, start, count):
        return pl.ds(pl.multiple_of(start, 16), count)

    def at(self, buf, start, count):
        ref, first = buf
        return ref.at[self.rows_at(first + start, count)]

    def put(self, buf, start, value):
        ref, first = buf
        ref[self.rows_at(first + start, self.pair), :] = value.astype(bf16)

    def read(self, buf, start):
        ref, first = buf
        return ref[self.rows_at(first + start, self.pair), :].astype(f32)

    def move(self, out, into, sems, index, count, peer):
        start = index * count
        return self.copy(self.at(out, start, count), self.at(into, start, count), sems.at[index], peer)

    def copy(self, src, dst, sem, peer):
        return pltpu.make_async_remote_copy(
            src_ref=src, dst_ref=dst, send_sem=self.send_sem.at[0], recv_sem=sem, device_id=peer, device_id_type=MESH
        )

    def sibling_copy(self, z):
        return self.move(self.s_out, self.s_in, self.s_sems, z, 4 * self.rows, self.p.sibling)

    def first_copies(self, z):
        return (
            self.move(self.x1_out, self.x1_in, self.x1_sems, z, 2 * self.half, self.p.x_peer),
            self.move(self.y1_out, self.y1_in, self.y1_sems, z, 2 * self.half, self.p.y_peer),
        )

    def second_copies(self, z):
        return (
            self.move(self.x2_out, self.x2_in, self.x2_sems, z, self.half, self.p.x_peer),
            self.move(self.y2_out, self.y2_in, self.y2_sems, z, self.half, self.p.y_peer),
        )

    def z_copy(self, src, dst, peer_z):
        return self.copy(
            self.at(self.z_out, dst * self.rows, self.rows), self.at(self.z_in, src * self.rows, self.rows),
            self.z_sems.at[src], self.p.z_peer(peer_z),
        )

    def to_sibling(self, z):
        p = self.p
        for rel in range(4):
            owner = p.owner(rel, z, 1 - p.core)

            def put(m, _, rel=rel, owner=owner):
                start = (z * 4 + rel) * self.rows + m * self.pair
                self.put(self.s_out, start, self.pack(owner, m))
                return 0

            lax.fori_loop(0, 4, put, 0)
        self.sibling_copy(z).start()

    def term(self, rel, z, half, m):
        start = (z * 4 + rel) * self.rows + half * self.half + m * self.pair
        return self.pack(self.p.owner(rel, z), half * 2 + m).astype(f32) + self.read(self.s_in, start)

    def first(self, z):
        self.sibling_copy(z).wait_recv()
        for out, half, rels in ((self.x1_out, 0, (1, 3)), (self.y1_out, 1, (2, 3))):
            for n, rel in enumerate(rels):

                def put(m, _, out=out, half=half, rel=rel, n=n):
                    start = (z * 2 + n) * self.half + m * self.pair
                    self.put(out, start, self.term(rel, z, half, m))
                    return 0

                lax.fori_loop(0, 2, put, 0)
        for copy in self.first_copies(z):
            copy.start()

    def second(self, z):
        for copy in self.first_copies(z):
            copy.wait_recv()
        for out, into, half, rel in ((self.y2_out, self.x1_in, 0, 2), (self.x2_out, self.y1_in, 1, 1)):

            def put(m, _, out=out, into=into, half=half, rel=rel):
                there = (z * 2 + 1) * self.half + m * self.pair
                total = self.term(rel, z, half, m) + self.read(into, there)
                self.put(out, z * self.half + m * self.pair, total)
                return 0

            lax.fori_loop(0, 2, put, 0)
        for copy in self.second_copies(z):
            copy.start()

    def column(self, z, half, m):
        first, second = ((self.x1_in, self.y2_in), (self.y1_in, self.x2_in))[half]
        return (
            self.term(0, z, half, m)
            + self.read(first, z * 2 * self.half + m * self.pair)
            + self.read(second, z * self.half + m * self.pair)
        )

    def third(self, z):
        for copy in self.second_copies(z):
            copy.wait_recv()
        for half in range(2):

            def put(m, _, half=half):
                start = z * self.rows + half * self.half + m * self.pair
                self.put(self.z_out, start, self.column(z, half, m))
                return 0

            lax.fori_loop(0, 2, put, 0)
        self.z_copy(self.p.z, z, z).start()

    def last(self, out):
        p = self.p
        for copy in self.second_copies(p.z):
            copy.wait_recv()
        for z in p.others:
            self.z_copy(z, p.z, z).wait_recv()
        for half in range(2):

            def put(m, _, half=half):
                total = self.column(p.z, half, m)
                start = half * self.half + m * self.pair
                for z in p.others:
                    total = total + self.read(self.z_in, z * self.rows + start)
                out[pl.ds(pl.multiple_of(start, 8), self.pair), :] = total
                return 0

            lax.fori_loop(0, 2, put, 0)

    def finish(self):
        whole = self.at((self.s_out[0], 0), 0, 31 * self.rows)
        self.copy(whole, whole, self.z_sems.at[0], self.p.sibling).wait_send()

    def events(self, out, steps):
        order = self.p.others[::-1] + [self.p.z]

        def event(step):
            kind, k = step
            if kind == "last":
                return lambda: self.last(out)
            return lambda: getattr(self, kind)(order[k])

        return [event(step) for step in steps]


def steps_of(*kinds):
    seen = {}
    for kind in kinds:
        seen[kind] = seen.get(kind, -1) + 1
        yield kind, seen[kind]


TO, ONE, TWO, THREE, LAST = "to_sibling", "first", "second", "third", "last"
REDUCE_ORDER = tuple(
    steps_of(TO, TO, ONE, TO, ONE, TO, TWO, ONE, TWO, THREE, TWO, ONE, THREE, THREE, TWO, LAST)
)
REDUCE_ORDER_OUT = tuple(
    steps_of(TO, TO, ONE, TO, ONE, TO, ONE, ONE, TWO, TWO, TWO, THREE, TWO, THREE, THREE, LAST)
)


REDUCE_COUNTS = (16, 4, 4, 2, 2, 4)
REDUCE_SEMS = [pltpu.SemaphoreType.DMA((n,)) for n in (1, 4, 4, 4, 4, 4, 4)]


def reduce_bufs(out, into, rows):
    bufs, first = [], 0
    for count in REDUCE_COUNTS:
        bufs += [(out, first), (into, first)]
        first += count * rows
    return bufs


def pack_in(owner, grad):
    def pack(device, m):
        halves = []
        for h in range(2):
            b = owner[device * 8 + m * 2 + h]
            layer, i, j = lax.div(b, 128), lax.div(lax.rem(b, 128), 8), lax.rem(b, 8)
            halves.append(grad[layer * 8 + j, pl.ds(69 * i, 72), :])
        return jnp.concatenate(halves, axis=0)

    return pack


def pack_out(owner, grad):
    def pack(device, m):
        return jnp.concatenate([grad[owner[device * 8 + m * 2 + h]] for h in range(2)], axis=0)

    return pack


def dot(a, b, ca, cb, precision=None):
    return lax.dot_general(
        a, b, (((ca,), (cb,)), ((), ())), precision=precision, preferred_element_type=f32
    )


def shampoo_block(grad, left, right, root_left, root_right, weight, rate):
    new_left = 0.5 * left + 0.5 * dot(grad, grad, 1, 1, highest)
    new_right = 0.5 * right + 0.5 * dot(grad, grad, 0, 0, highest)
    step = dot(dot(root_left, grad, 1, 0, highest), root_right, 1, 0, highest)
    return new_left, new_right, weight - rate * step


def dot(a, b, ca, cb, precision=None):
    return lax.dot_general(
        a, b, (((ca,), (cb,)), ((), ())), precision=precision, preferred_element_type=f32
    )


def tile(t, size=TILE):
    return pl.ds(pl.multiple_of(t * size, size), size)


def wide(mask):
    return jnp.concatenate([mask, mask], axis=1)


def gate_of(left, right):
    tau = jnp.tanh(left)
    sigma = 0.5 * jnp.tanh(0.5 * right) + 0.5
    hidden = tau * sigma
    return hidden, sigma - hidden * tau, hidden * (1.0 - sigma)


class Planes:
    def __init__(self, ref, samples, count):
        self.ref, self.samples, self.count = ref, samples, count

    def rows(self, plane, start, size):
        return pl.ds(pl.multiple_of(plane * self.samples + start, size), size)

    def get(self, t, planes, size=TILE):
        return jnp.concatenate([self.ref[self.rows(c, t * size, size), :] for c in planes], axis=1)

    def put(self, t, planes, value, size=TILE):
        for n, c in enumerate(planes):
            self.ref[self.rows(c, t * size, size), :] = value[:, 128 * n : 128 * n + 128]


class Layers:
    def __init__(self, refs, place):
        self.__dict__.update(refs)
        self.place = place
        self.samples = self.hidden.shape[0]
        self.tiles = self.samples // TILE
        self.gate = Planes(self.stack_in, self.samples, 8)
        self.early_at = 8 * self.samples


    def make_masks(self):
        def step(t, _):
            pos = self.place.seq * self.samples + t * TILE + lax.broadcasted_iota(i32, (TILE, 128), 0)
            end, start = 0, jnp.zeros((TILE, 128), i32)
            for k in range(self.lengths.shape[1]):
                end = end + self.lengths[0, k]
                start = start + jnp.where(end <= pos, self.lengths[0, k], 0)
            for ref, dilation in ((self.mask_long, FIRST_DILATION), (self.mask_short, 1)):
                ref[tile(t), :] = jnp.where(pos - dilation >= start, 1.0, 0.0).astype(bf16)
            return 0

        lax.fori_loop(0, self.tiles, step, 0)

    def make_inverse(self):
        block = lax.broadcasted_iota(i32, (2, 128), 0) * 128 + lax.broadcasted_iota(i32, (2, 128), 1)

        def step(q, found):
            return jnp.maximum(found, jnp.where(block == self.owner[q], q, 0))

        found = lax.fori_loop(0, 256, step, jnp.zeros((2, 128), i32), unroll=8)
        self.inverse_vmem[pl.ds(0, 2), :] = found
        copy = pltpu.make_async_copy(self.inverse_vmem, self.inverse, self.inverse_sem)
        copy.start()
        copy.wait()

    def make_condition(self):
        def step(t, _):
            lanes = tile(t)
            part = self.cond_t[:, lanes].astype(f32)
            padded = jnp.concatenate([part, jnp.zeros((128 - part.shape[0], TILE), f32)], axis=0)
            turned = padded.T.astype(bf16)
            self.units1[tile(t), 1024:] = turned
            self.units2[tile(t), 1024:] = turned
            return 0

        lax.fori_loop(0, self.tiles, step, 0)

    def make_delayed(self):
        def step(t, _):
            mask = self.mask_long[tile(t), :]
            for c in range(4):
                before = self.units1[tile(t - 1), 512 + 128 * c : 640 + 128 * c]
                self.units1[tile(t), 128 * c : 128 * c + 128] = before * mask
            return 0

        lax.fori_loop(1, self.tiles, step, 0)

    def make_first_delayed(self):
        mask = self.mask_long[pl.ds(0, TILE), :]
        for c in range(4):
            lanes = slice(128 * c, 128 * c + 128)
            self.units1[pl.ds(0, TILE), lanes] = self.halo_signal[:, lanes] * mask


    def forward_one(self, t):
        for c in range(2):
            left, right = self.halves(self.units1[tile(t), :], self.full_in[0], c)
            hidden, by_tanh, by_sigmoid = gate_of(left, right)
            self.hidden[tile(t), 256 * c : 256 * c + 256] = hidden.astype(bf16)
            self.gate.put(t, range(2 * c, 2 * c + 2), by_tanh.astype(bf16))
            self.gate.put(t, range(4 + 2 * c, 6 + 2 * c), by_sigmoid.astype(bf16))

    def halves(self, units, weight, c):
        return [dot(units, weight[:, first : first + 256], 1, 0) for first in (256 * c, 512 + 256 * c)]

    def state_one(self, t):
        mask = self.mask_short[tile(t), :].astype(f32)
        for c in range(2):
            lanes = slice(256 * c, 256 * c + 256)
            out = dot(self.hidden[tile(t), :512], self.full_out[:512, lanes], 1, 0)
            state = self.units1[tile(t), 512 + 256 * c : 768 + 256 * c].astype(f32) + out
            rounded = state.astype(bf16)
            self.units2[tile(t), 512 + 256 * c : 768 + 256 * c] = rounded
            delayed = pltpu.roll(rounded.astype(f32), 1, 0)
            self.last_rows[t, :, lanes] = delayed[:8]
            self.units2[tile(t), lanes] = (delayed * wide(mask)).astype(bf16)

    def mend_delayed(self, t):
        source = self.halo_state if t == 0 else self.last_rows.at[t - 1]
        first = lax.broadcasted_iota(i32, (16, 128), 0) == 0
        mask = self.mask_short[pl.ds(t * TILE, 16), :].astype(f32)
        rows = pl.ds(t * TILE, 16)
        for c in range(4):
            lanes = slice(128 * c, 128 * c + 128)
            row = jnp.broadcast_to(source[0:1, lanes], (16, 128)) * mask
            self.units2[rows, lanes] = jnp.where(first, row, self.units2[rows, lanes].astype(f32)).astype(bf16)

    def layer_two(self, t):
        for c in range(2):
            left, right = self.halves(self.units2[tile(t), :], self.full_in[1], c)
            hidden, by_tanh, by_sigmoid = gate_of(left, right)
            self.hidden[tile(t), 512 + 256 * c : 768 + 256 * c] = hidden.astype(bf16)
            gh = dot(self.go[tile(t), :], self.full_out[512 + 256 * c : 768 + 256 * c, :], 1, 1)
            self.gz[tile(t), 256 * c : 256 * c + 256] = (gh * by_tanh).astype(bf16)
            self.gz[tile(t), 512 + 256 * c : 768 + 256 * c] = (gh * by_sigmoid).astype(bf16)

    def units_two(self, t):
        mask = wide(self.mask_short[tile(t), :].astype(f32))
        last = lax.broadcasted_iota(i32, (TILE, 256), 0) == TILE - 1
        gz = self.gz[tile(t), :]
        for c in range(2):
            lanes = slice(256 * c, 256 * c + 256)
            early = dot(gz, self.full_in[1, lanes, :], 1, 1) * mask
            self.first_rows[t, :, lanes] = early[:8]
            moved = jnp.where(last, 0.0, pltpu.roll(early, TILE - 1, 0))
            here = dot(gz, self.full_in[1, 512 + 256 * c : 768 + 256 * c, :], 1, 1)
            self.gx[tile(t), lanes] = self.go[tile(t), lanes].astype(f32) + here + moved
        self.cond_grad[:, tile(t)] = self.condition_part(gz, 1)

    def condition_part(self, gz, layer):
        part = dot(gz, self.full_in[layer, 1024:, :], 1, 1).T
        return part[: self.cond_grad.shape[0], :]

    def mend_gx(self, t):
        source = self.halo_grad if t == self.tiles - 1 else self.first_rows.at[t + 1]
        last = lax.broadcasted_iota(i32, (8, 512), 0) == 7
        rows = pl.ds((t + 1) * TILE - 8, 8)
        row = jnp.broadcast_to(source[0:1, :], (8, 512))
        self.gx[rows, :] = self.gx[rows, :] + jnp.where(last, row, 0.0)

    def round_gx(self, t):
        self.go[tile(t), :512] = self.gx[tile(t), :].astype(bf16)

    def layer_one_back(self, t):
        for c in range(2):
            gh = dot(self.go[tile(t), :], self.full_out[256 * c : 256 * c + 256, :], 1, 1)
            for part in range(2):
                gate = self.gate.get(t, range(4 * part + 2 * c, 4 * part + 2 * c + 2)).astype(f32)
                first = 512 * part + 256 * c
                self.gz[tile(t), first : first + 256] = (gh * gate).astype(bf16)


    def weight_out(self, layer):
        def step(m, _):
            lanes = pl.ds(pl.multiple_of(layer * 512 + m * 256, 256), 256)
            grad = dot(self.hidden[:, lanes], self.go[...], 0, 0)
            for i in range(4):
                for j in range(8):
                    pair = grad[64 * i : 64 * i + 64, 128 * j : 128 * j + 128]
                    first = layer * 128 + (m * 4 + i) * 16 + 2 * j
                    for k, block in enumerate(across(pair[:32], pair[32:])):
                        self.grad_out[first + k] = block.astype(bf16)
            return 0

        lax.fori_loop(0, 2, step, 0)

    def weight_in(self, layer, units, m):
        rows = pl.ds(pl.multiple_of(384 * m, 384), 384)
        grad = dot(units[:, rows], self.gz[...], 0, 0)
        for j in range(8):
            self.grad_in[layer * 8 + j, rows, :] = grad[:, 128 * j : 128 * j + 128]


    def early_units_one(self):
        mask = wide(self.mask_long[pl.ds(0, TILE), :].astype(f32))
        for c in range(2):
            lanes = slice(256 * c, 256 * c + 256)
            early = dot(self.gz[pl.ds(0, TILE), :], self.full_in[0, lanes, :], 1, 1) * mask
            for k in range(2):
                rows = pl.ds(self.early_at + TILE * (2 * c + k), TILE)
                self.stack_in[rows, :] = early[:, 128 * k : 128 * k + 128].astype(bf16)

    def units_one(self, t):
        gz = self.gz[tile(t), :]
        mask = wide(self.mask_long[tile(t), :].astype(f32))
        for c in range(2):
            lanes = slice(256 * c, 256 * c + 256)
            if t > 0:
                early = dot(gz, self.full_in[0, lanes, :], 1, 1)
                self.gx[tile(t - 1), lanes] = self.gx[tile(t - 1), lanes] + early * mask
            here = dot(gz, self.full_in[0, 512 + 256 * c : 768 + 256 * c, :], 1, 1)
            self.gx[tile(t), lanes] = self.gx[tile(t), lanes] + here
        self.cond_grad[:, tile(t)] = self.cond_grad[:, tile(t)] + self.condition_part(gz, 0)

    def put_out(self, src, dst, sem):
        copy = pltpu.make_async_copy(src, dst, sem)
        copy.start()
        self.pending.append(copy)

    def send_gx(self, t):
        self.units2[tile(t), :512] = self.gx[tile(t), :].astype(bf16)
        self.put_out(self.units2.at[tile(t), pl.ds(0, 512)], self.grad_x.at[tile(t)], self.gx_sems.at[t])

    def outputs(self, n):
        rows = tile(n, 256)
        for c in range(4):
            lanes = slice(256 * c, 256 * c + 256)
            out = dot(self.hidden[rows, :], self.full_out[:, lanes], 1, 0)
            if c < 2:
                out = out + self.units1[rows, 512 + 256 * c : 768 + 256 * c].astype(f32)
            self.go[rows, lanes] = out.astype(bf16)
        self.output_copy(n).start()

    def output_copy(self, n):
        rows = tile(n, 256)
        return pltpu.make_async_copy(self.go.at[rows], self.both.at[rows], self.stage_sems.at[n])

    def drain(self, copies):
        for copy in copies:
            copy.wait()

    def end_gx(self, near, early_halo):
        t = self.tiles - 1
        near.arrived(*early_halo)
        for c in range(4):
            lanes = slice(128 * c, 128 * c + 128)
            late = self.halo_early[pl.ds(TILE * c, TILE), :].astype(f32)
            self.gx[tile(t), lanes] = self.gx[tile(t), lanes] + late
        self.send_gx(t)

    def tail(self, near, early_halo, small, rest_out):
        work = {}
        work[TO, 3] = [self.early_units_one, lambda: near.start(*early_halo), lambda: self.units_one(0)]
        work[ONE, 2] = [lambda: self.units_one(1), lambda: self.send_gx(0)]
        work[TWO, 1] = [lambda: near.sent(*early_halo)]
        work[THREE, 0] = [lambda: self.units_one(2), lambda: self.send_gx(1), lambda: self.outputs(0)]
        work[ONE, 3] = [lambda: self.outputs(1)]
        work[THREE, 1] = [lambda: self.outputs(2), *rest_out, lambda: small[1].start()]
        work[THREE, 2] = [
            lambda: self.units_one(3),
            lambda: self.send_gx(2),
            lambda: self.end_gx(near, early_halo),
            lambda: small[0].start(),
        ]
        work[TWO, 3] = [lambda: loop(3, self.samples // 256, self.outputs)]
        return [work.get(step, []) for step in REDUCE_ORDER]


def loop(first, last, body):
    lax.fori_loop(first, last, lambda t, _: (body(t), 0)[1], 0)


class Neighbours:
    def __init__(self, place):
        self.p = place
        self.has = {1: place.seq < 7, -1: place.seq > 0}

    def copy(self, src, dst, sems, way):
        return pltpu.make_async_remote_copy(
            src_ref=src, dst_ref=dst, send_sem=sems[0], recv_sem=sems[1],
            device_id=(self.p.row, self.p.seq + way), device_id_type=MESH)

    def start(self, src, dst, sems, way):
        pl.when(self.has[way])(lambda: self.copy(src, dst, sems, way).start())

    def sent(self, src, dst, sems, way):
        pl.when(self.has[way])(lambda: self.copy(src, dst, sems, way).wait_send())

    def arrived(self, src, dst, sems, way):
        pl.when(self.has[-way])(lambda: self.copy(src, dst, sems, way).wait_recv())


INPUTS = ("owner", "lengths", "signal", "cot_x", "cot_skip", "from_cond", "from_w_in", "from_w_out")
OUTPUTS = ("both", "grad_x", "grad_cond_t", "sum_in", "sum_out")
SCRATCH = dict(
    stack_in=pltpu.VMEM((32 * ROWS_IN, 128), bf16),
    stack_out=pltpu.VMEM((32 * ROWS_OUT, 128), bf16),
    full_in=pltpu.VMEM((2, 1152, 1024), bf16),
    full_out=pltpu.VMEM((1024, 1024), bf16),
    units1=pltpu.VMEM((2048, 1152), bf16),
    units2=pltpu.VMEM((2048, 1152), bf16),
    hidden=pltpu.VMEM((2048, 1024), bf16),
    gz=pltpu.VMEM((2048, 1024), bf16),
    go=pltpu.VMEM((2048, 1024), bf16),
    gx=pltpu.VMEM((2048, 512), f32),
    grad_in=pltpu.VMEM((16, 1152, 128), f32),
    grad_out=pltpu.VMEM((256, 32, 128), bf16),
    mask_long=pltpu.VMEM((2048, 128), bf16),
    mask_short=pltpu.VMEM((2048, 128), bf16),
    halo_signal=pltpu.VMEM((TILE, 512), bf16),
    halo_early=pltpu.VMEM((4 * TILE, 128), bf16),
    last_rows=pltpu.VMEM((4, 8, 512), f32),
    first_rows=pltpu.VMEM((4, 8, 512), f32),
    halo_state=pltpu.VMEM((8, 512), f32),
    halo_grad=pltpu.VMEM((8, 512), f32),
    reduce_in=pltpu.VMEM((32 * ROWS_IN, 128), bf16),
    reduce_out=pltpu.VMEM((32 * ROWS_OUT, 128), bf16),
    cond_t=pltpu.VMEM((80, 2048), bf16),
    w_in=pltpu.VMEM((552, 128), f32),
    w_out=pltpu.VMEM((8, 64, 64), f32),
    cond_grad=pltpu.VMEM((80, 2048), f32),
    share_in=pltpu.VMEM((ROWS_IN, 128), f32),
    share_out=pltpu.VMEM((ROWS_OUT, 128), f32),
    small_sems=pltpu.SemaphoreType.DMA((3,)),
    inverse_vmem=pltpu.VMEM((8, 128), i32),
    inverse=pltpu.SMEM((8, 128), i32),
    inverse_sem=pltpu.SemaphoreType.DMA,
    load_sems=pltpu.SemaphoreType.DMA((6,)),
    gx_sems=pltpu.SemaphoreType.DMA((4,)),
    stage_sems=pltpu.SemaphoreType.DMA((8,)),
    halo_sems=pltpu.SemaphoreType.DMA((8,)),
)


def network_kernel(*refs):
    names = INPUTS + OUTPUTS + tuple(SCRATCH)
    sems = refs[len(names) :]
    gather_sems, reduce_sems = len(GATHER_SEMS), len(REDUCE_SEMS)
    sems_in, sems = sems[:gather_sems], sems[gather_sems:]
    sems_out, sems = sems[:gather_sems], sems[gather_sems:]
    sum_sems_out, sum_sems_in = sems[:reduce_sems], sems[reduce_sems:]
    place = Place()
    n = Layers(dict(zip(names, refs)), place)
    n.pending = []
    near = Neighbours(place)
    samples, tiles = n.samples, n.tiles

    place.announce()
    targets = ((n.signal, n.units1, 512), (n.cot_x, n.go, 0), (n.cot_skip, n.go, 512))
    early = [
        pltpu.make_async_copy(src, dst, n.load_sems.at[k])
        for k, (src, dst) in enumerate(
            ((n.from_w_in, n.w_in), (n.from_w_out, n.w_out), (n.from_cond, n.cond_t))
        )
    ]
    loads = [
        pltpu.make_async_copy(src, dst.at[:, pl.ds(lane, 512)], n.load_sems.at[3 + k])
        for k, (src, dst, lane) in enumerate(targets)
    ]
    for copy in early + loads:
        copy.start()
    me = place.row * 8 + place.seq
    pairs_in, blocks_out = n.stack_in.reshape(128, 144, 128), n.stack_out.reshape(256, 32, 128)
    spread = n.grad_in
    early[0].wait()
    spread[0, :ROWS_IN, :] = jnp.zeros((ROWS_IN, 128), f32)
    spread[1, : 8 * 69, :] = n.w_in[...]
    for k in range(8):
        spread[0, pl.ds(72 * k, 69), :] = spread[1, pl.ds(k, 72, 8), :][:69]
    for m in range(4):
        pairs_in[me * 4 + m] = spread[0, 144 * m : 144 * m + 144, :].astype(bf16)

    early[1].wait()
    for k in range(8):
        block = n.w_out[k]
        blocks_out[me * 8 + k] = jnp.concatenate([block[:32], block[32:]], axis=1).astype(bf16)

    def cleared(refs, when):
        @pl.when(when)
        def _():
            for ref in refs:
                ref[...] = jnp.zeros_like(ref)

    cleared([n.halo_signal, n.halo_state], place.seq == 0)
    cleared([n.halo_early, n.halo_grad], place.seq == 7)
    place.all_here()

    halo = [(n.halo_sems.at[2 * k], n.halo_sems.at[2 * k + 1]) for k in range(4)]
    signal_halo = (n.signal.at[pl.ds(samples - TILE, TILE)], n.halo_signal, halo[0], 1)
    state_halo = (n.last_rows.at[tiles - 1], n.halo_state, halo[1], 1)
    grad_halo = (n.first_rows.at[0], n.halo_grad, halo[2], -1)
    early_halo = (n.stack_in.at[pl.ds(n.early_at, 4 * TILE)], n.halo_early, halo[3], -1)
    into = Gather(place, pairs_in, 4, sems_in)
    out = Gather(place, blocks_out, 8, sems_out)
    order = [place.z] + place.others
    into.start()
    into.start_sides()
    out.start()

    def make_rest():
        early[2].wait()
        n.make_condition()
        n.full_in[0, 1104:, :] = jnp.zeros((48, 1024), bf16)
        n.full_in[1, 1104:, :] = jnp.zeros((48, 1024), bf16)

    n.make_masks()
    n.make_inverse()
    for k, work in enumerate((make_rest, lambda: None, lambda: None)):
        into.along_z(k)
        work()
        out.relay(k, 0)
        out.relay(k, 1)
        into.first(order[k])
    into.rest(order[0])
    into.first(order[3])
    near.start(*signal_halo)
    out.start_sides()
    for k in range(3):
        out.spread(k, 0)
        out.spread(k, 1)
    for copy in loads:
        copy.wait()
    n.make_delayed()
    for k in range(1, tiles):
        into.rest(order[k])
    into.finish()
    assemble_in(n.inverse, pairs_in, spread, n.full_in, 0)
    assemble_in(n.inverse, pairs_in, spread, n.full_in, 1)

    near.arrived(*signal_halo)
    n.make_first_delayed()
    out.first(order[0])
    out.first(order[1])
    loop(0, 2, n.forward_one)
    out.first(order[2])
    out.first(order[3])
    out.rest(order[0])
    out.rest(order[1])
    loop(2, tiles, n.forward_one)
    out.rest(order[2])
    out.rest(order[3])
    out.finish()
    assemble_out(n.inverse, blocks_out, n.full_out, 0)
    assemble_out(n.inverse, blocks_out, n.full_out, 1)
    n.state_one(tiles - 1)
    near.start(*state_halo)
    loop(0, tiles - 1, n.state_one)
    for t in range(1, tiles):
        n.mend_delayed(t)
    near.arrived(*state_halo)
    n.mend_delayed(0)

    loop(0, tiles, n.layer_two)
    n.units_two(0)
    near.start(*grad_halo)
    loop(1, tiles, n.units_two)
    n.weight_out(1)
    for t in range(tiles - 1):
        n.mend_gx(t)
    near.arrived(*grad_halo)
    n.mend_gx(tiles - 1)
    loop(0, tiles, n.round_gx)
    n.weight_out(0)

    reduce_out = Reduce(
        place, pack_out(n.owner, n.grad_out), ROWS_OUT,
        reduce_bufs(n.stack_out, n.reduce_out, ROWS_OUT), sum_sems_out,
    )
    reduce_in = Reduce(
        place, pack_in(n.owner, n.grad_in), ROWS_IN,
        reduce_bufs(n.stack_in, n.reduce_in, ROWS_IN), sum_sems_in,
    )
    sum_out = reduce_out.events(n.share_out, REDUCE_ORDER_OUT)
    sum_in = reduce_in.events(n.share_in, REDUCE_ORDER)

    def run(*events):
        for event in events:
            event()

    small = [
        pltpu.make_async_copy(a, b, n.small_sems.at[k])
        for k, (a, b) in enumerate(
            ((n.cond_grad, n.grad_cond_t), (n.share_out, n.sum_out), (n.share_in, n.sum_in))
        )
    ]
    run(*sum_out[:2])
    n.weight_in(1, n.units2, 0)
    run(*sum_out[2:6])
    n.weight_in(1, n.units2, 1)
    run(*sum_out[6:8])
    n.weight_in(1, n.units2, 2)
    run(*sum_out[8:10])
    loop(0, 2, n.layer_one_back)
    run(sum_out[10])
    loop(2, tiles, n.layer_one_back)
    run(*sum_out[11:13])
    n.weight_in(0, n.units1, 0)
    run(*sum_out[13:15])
    n.weight_in(0, n.units1, 1)
    n.weight_in(0, n.units1, 2)
    for event, work in zip(sum_in, n.tail(near, early_halo, small, [sum_out[15], reduce_out.finish])):
        event()
        for part in work:
            part()
    reduce_in.finish()
    small[2].start()
    for halo in (signal_halo, state_halo, grad_halo):
        near.sent(*halo)
    n.drain(n.pending)
    loop(0, samples // 256, lambda k: n.output_copy(k).wait())
    n.drain(small)


ANY = pl.BlockSpec(memory_space=pl.ANY)


def shampoo_block(grad, left, right, root_left, root_right, weight, rate):
    low = grad.astype(bf16)
    new_left = 0.5 * left + 0.5 * dot(low, low, 1, 1)
    new_right = 0.5 * right + 0.5 * dot(low, low, 0, 0)
    step = dot(dot(root_left.astype(bf16), low, 1, 0).astype(bf16), root_right.astype(bf16), 1, 0)
    return new_left, new_right, weight - rate * step


BLOCKS_IN = ("w_in", "left_in", "root_left_in", "right_in", "root_right_in")
BLOCKS_OUT = ("w_out", "left_out", "root_left_out", "right_out", "root_right_out")
SUMS = ("sum_in", "sum_out")
LARGE = ("out_x", "skip_sum", "grad_x")
LOW = ("both", "grad_x")


def finish_kernel(*refs):
    taken = SUMS + BLOCKS_IN + BLOCKS_OUT
    names = ["from_" + a for a in taken + LOW + ("cond",)]
    names += ["to_" + a for a in LARGE + ("cond", "grad_in", "grad_out")]
    names += ["to_" + a for kind in ("in", "out") for a in ("w_" + kind, "left_" + kind, "right_" + kind)]
    names += list(taken) + ["grad_in", "grad_out", "large", "both", "low", "cond", "load_sems", "store_sems"]
    r = dict(zip(names, refs))
    loads, stores, sems = {}, {}, iter(range(64))

    def move(table, key, src, dst, sem):
        table[key] = pltpu.make_async_copy(src, dst, r[sem].at[next(sems)])

    for a in taken:
        there = r[a].at[pl.ds(0, 552)] if a in BLOCKS_IN[:3] else r[a]
        move(loads, a, r["from_" + a], there, "load_sems")
    for m in range(4):
        move(loads, ("both", m), r["from_both"].at[tile(m)], r["both"].at[tile(m)], "load_sems")
        move(loads, ("low", m), r["from_grad_x"].at[tile(m)], r["low"].at[tile(m)], "load_sems")
    move(loads, "cond", r["from_cond"], r["cond"], "load_sems")
    sems = iter(range(64))
    for m in range(4):
        for k in range(3):
            move(stores, (k, m), r["large"].at[k, tile(m)], r["to_" + LARGE[k]].at[tile(m)], "store_sems")
    for a in ("cond", "grad_in", "w_in", "left_in", "right_in", "grad_out", "w_out", "left_out", "right_out"):
        here = r[a].at[pl.ds(0, 552)] if a in ("grad_in", "w_in", "left_in") else r[a]
        move(stores, a, here, r["to_" + a], "store_sems")
    for copy in loads.values():
        copy.start()

    def widen(m, name):
        loads[name, m].wait()
        for k in (0, 1) if name == "both" else (2,):
            lanes = slice(512 * (k % 2), 512 * (k % 2) + 512)
            r["large"][k, tile(m), :] = r[name][tile(m), lanes].astype(f32)
            stores[k, m].start()

    for a in taken:
        loads[a].wait()
    for k in range(8):
        at, put = pl.ds(k, 72, 8), pl.ds(k, 69, 8)
        grad = r["sum_in"][72 * k : 72 * k + 72, :]
        r["grad_in"][at, :] = grad
        r["left_in"][put, :], r["right_in"][k], r["w_in"][put, :] = shampoo_block(
            grad[:69], r["left_in"][at, :][:69], r["right_in"][k], r["root_left_in"][at, :][:69],
            r["root_right_in"][k], r["w_in"][at, :][:69], rate_in,
        )
        folded = r["sum_out"][32 * k : 32 * k + 32, :]
        grad = jnp.concatenate([folded[:, :64], folded[:, 64:]], axis=0)
        r["grad_out"][k] = grad
        r["left_out"][k], r["right_out"][k], r["w_out"][k] = shampoo_block(
            grad, r["left_out"][k], r["right_out"][k], r["root_left_out"][k], r["root_right_out"][k],
            r["w_out"][k], rate_out,
        )
        if k % 2:
            widen(k // 2, "both")
            widen(k // 2, "low")
    loads["cond"].wait()
    for a in ("cond", "grad_in", "w_in", "left_in", "right_in"):
        stores[a].start()
    for a in ("grad_out", "w_out", "left_out", "right_out"):
        stores[a].start()
    for copy in stores.values():
        copy.wait()


def rows_first(blocks):
    return blocks.transpose(1, 0, 2)


def fused_local(
    signal, condition, lengths, owner, grad_out, grad_skip, w_in, w_out,
    left_in, right_in, root_left_in, root_right_in,
    left_out, right_out, root_left_out, root_right_out,
):
    samples, width, mels = signal.shape[1], signal.shape[2], condition.shape[2]
    block = lambda *shape: jax.ShapeDtypeStruct(shape, f32)
    low = [jax.ShapeDtypeStruct((samples, lanes), bf16) for lanes in (2 * width, width)]
    large = [block(samples, width)] * 3 + [block(mels, samples)]
    rows_in = rows_first(w_in).reshape(552, 128)
    both, grad_x, grad_cond_t, sum_in, sum_out = pl.pallas_call(
        network_kernel,
        out_shape=low + [block(mels, samples), block(ROWS_IN, 128), block(ROWS_OUT, 128)],
        in_specs=[SMEM, SMEM] + [ANY] * 6,
        out_specs=[ANY] * 5,
        scratch_shapes=list(SCRATCH.values()) + GATHER_SEMS * 2 + REDUCE_SEMS * 2,
        name="network",
        compiler_params=pltpu.CompilerParams(
            collective_id=0, has_side_effects=True, vmem_limit_bytes=64 << 20
        ),
    )(
        owner, lengths, signal[0], grad_out[0], grad_skip[0], condition[0].T, rows_in, w_out,
    )
    taken = (
        sum_in, sum_out,
        rows_in, rows_first(left_in).reshape(552, 69), rows_first(root_left_in).reshape(552, 69),
        right_in, root_right_in,
        w_out, left_out, root_left_out, right_out, root_right_out,
    )
    new_in = [block(552, 128), block(552, 69), block(8, 128, 128)]
    new_out = [block(8, 64, 64)] * 3
    held = [pltpu.VMEM((584 if a.shape[0] == 552 else a.shape[0], *a.shape[1:]), f32) for a in taken]
    outs = pl.pallas_call(
        finish_kernel,
        out_shape=large + [new_in[0], new_out[0]] + new_in + new_out,
        in_specs=[ANY] * (len(taken) + 3),
        out_specs=[ANY] * 12,
        scratch_shapes=held
        + [pltpu.VMEM((584, 128), f32), pltpu.VMEM((8, 64, 64), f32)]
        + [pltpu.VMEM((3, samples, width), f32)]
        + [pltpu.VMEM(a.shape, a.dtype) for a in low + [block(mels, samples)]]
        + [pltpu.SemaphoreType.DMA((32,))] * 2,
        name="finish",
        compiler_params=pltpu.CompilerParams(vmem_limit_bytes=63 << 20),
    )(*taken, both, grad_x, grad_cond_t)
    out_x, skip_sum, grad_x, grad_cond_t, g_in, g_out, nw_in, nl_in, nr_in, nw_out, nl_out, nr_out = outs

    def blocks_first(rows):
        return rows.reshape(69, 8, rows.shape[1]).transpose(1, 0, 2)

    return (
        out_x[None], skip_sum[None], grad_x[None], grad_cond_t.T[None],
        blocks_first(g_in), g_out, blocks_first(nl_in), nr_in, nl_out, nr_out, blocks_first(nw_in), nw_out,
    )


def local(
    signal,
    condition,
    lengths,
    owner,
    grad_out,
    grad_skip,
    w_in,
    w_out,
    left_in,
    right_in,
    root_left_in,
    root_right_in,
    left_out,
    right_out,
    root_left_out,
    root_right_out,
):
    fused = (lax.axis_size("row"), lax.axis_size("seq"), signal.shape[1]) == (4, 8, 4 * TILE)
    audio_samples = signal.shape[1]
    width = signal.shape[2]
    if fused:
        return fused_local(
            signal, condition, lengths, owner, grad_out, grad_skip, w_in, w_out,
            left_in, right_in, root_left_in, root_right_in,
            left_out, right_out, root_left_out, root_right_out,
        )
    stack_in = lax.all_gather(w_in.astype(bf16), ("row", "seq"), axis=0, tiled=True)
    stack_out = lax.all_gather(w_out.astype(bf16), ("row", "seq"), axis=0, tiled=True)
    inverse = jnp.argsort(owner)
    input_weight = from_blocks(jnp.take(stack_in, inverse, axis=0), 16, 8)
    output_weight = from_blocks(jnp.take(stack_out, inverse, axis=0), 8, 16)
    sample_positions = lax.axis_index("seq") * audio_samples + jnp.arange(
        audio_samples, dtype=jnp.int32
    )
    longer_mask = receptive_mask(lengths, sample_positions, FIRST_DILATION)[:, :, None]
    mask_short = receptive_mask(lengths, sample_positions, 1)[:, :, None]
    preceding_longer = shifted(signal[:, audio_samples - FIRST_DILATION :, :], "seq", 1)
    delayed_one = jnp.concatenate([preceding_longer, signal], axis=1)[:, :audio_samples, :]
    delayed_one = jnp.where(longer_mask, delayed_one, jnp.zeros_like(delayed_one))
    units_one = jnp.concatenate([delayed_one, signal, condition], axis=2)
    tanh_one, sigm_one, hidden_one, proj_one = gate_forward(
        units_one, input_weight[0], output_weight[0]
    )
    first_layer_state = signal.astype(jnp.float32) + proj_one[..., :width]
    rounded_one = first_layer_state.astype(jnp.bfloat16)
    before_short = shifted(rounded_one[:, audio_samples - 1 :, :], "seq", 1)
    delayed_two = jnp.concatenate([before_short, rounded_one[:, : audio_samples - 1, :]], axis=1)
    delayed_two = jnp.where(mask_short, delayed_two, jnp.zeros_like(delayed_two))
    units_two = jnp.concatenate([delayed_two, rounded_one, condition], axis=2)
    tanh_two, sigm_two, hidden_two, proj_two = gate_forward(
        units_two, input_weight[1], output_weight[1]
    )
    out_x = first_layer_state + proj_two[..., :width]
    skip_sum = proj_one[..., width:] + proj_two[..., width:]
    grad_next = grad_out.astype(jnp.float32)
    gin_two, gout_two, units_grad_two = gate_backward(
        units_two,
        tanh_two,
        sigm_two,
        hidden_two,
        input_weight[1],
        output_weight[1],
        grad_next,
        grad_skip,
    )
    early_two = jnp.where(mask_short, units_grad_two[..., :width], 0.0)
    from_short = shifted(early_two[:, :1, :], "seq", -1)
    grad_state = (
        grad_next
        + units_grad_two[..., width : 2 * width]
        + jnp.concatenate([early_two[:, 1:, :], from_short], axis=1)
    )
    gin_one, gout_one, units_grad_one = gate_backward(
        units_one,
        tanh_one,
        sigm_one,
        hidden_one,
        input_weight[0],
        output_weight[0],
        grad_state,
        grad_skip,
    )
    earlier_first = jnp.where(longer_mask, units_grad_one[..., :width], 0.0)
    taken_longer = shifted(earlier_first[:, :FIRST_DILATION, :], "seq", -1)
    grad_x = (
        grad_state
        + units_grad_one[..., width : 2 * width]
        + jnp.concatenate([earlier_first[:, FIRST_DILATION:, :], taken_longer], axis=1)
    )
    grad_cond = units_grad_one[..., 2 * width :] + units_grad_two[..., 2 * width :]
    local_in = jnp.take(to_blocks(jnp.stack([gin_one, gin_two]), 16, 8), owner, axis=0)
    local_out = jnp.take(to_blocks(jnp.stack([gout_one, gout_two]), 8, 16), owner, axis=0)
    grad_in_blocks, grad_out_blocks = (
        lax.psum_scatter(local_in, ("row", "seq"), scatter_dimension=0, tiled=True),
        lax.psum_scatter(local_out, ("row", "seq"), scatter_dimension=0, tiled=True),
    )
    new_left_in, new_right_in, new_w_in = shampoo(
        grad_in_blocks, left_in, right_in, root_left_in, root_right_in, w_in, rate_in
    )
    new_left_out, new_right_out, new_w_out = shampoo(
        grad_out_blocks, left_out, right_out, root_left_out, root_right_out, w_out, rate_out
    )
    return (
        out_x,
        skip_sum,
        grad_x,
        grad_cond,
        grad_in_blocks,
        grad_out_blocks,
        new_left_in,
        new_right_in,
        new_left_out,
        new_right_out,
        new_w_in,
        new_w_out,
    )


def solution(mesh):
    tokens, blocks = P("row", "seq", None), P(("row", "seq"), None, None)
    in_specs = (tokens, tokens, P("row", None), P(), tokens, tokens) + (blocks,) * 10
    out_specs = (tokens,) * 4 + (blocks,) * 8
    return jax.shard_map(local, mesh=mesh, in_specs=in_specs, out_specs=out_specs, check_vma=False)
```

```python
import jax
import jax.numpy as jnp
from jax import lax
from jax.experimental import pallas as pl
from jax.experimental.pallas import tpu as pltpu
from jax.sharding import PartitionSpec as P

FIRST_DILATION = 512
MESH = pl.DeviceIdType.MESH
bf16, f32, i32 = jnp.bfloat16, jnp.float32, jnp.int32

highest = lax.Precision.HIGHEST
rate_in = 0.3
rate_out = 1.0

TILE = 512
ROWS_IN = 576
ROWS_OUT = 256


def shifted(block, axis, distance):
    devices = range(lax.axis_size(axis))
    route = [(i - distance, i) for i in devices if i - distance in devices]
    return lax.ppermute(block, axis, route)


def to_blocks(full, row_parts, col_parts):
    layers, rows, cols = full.shape
    shaped = full.reshape(layers, row_parts, rows // row_parts, col_parts, cols // col_parts)
    return shaped.transpose(0, 1, 3, 2, 4).reshape(
        layers * row_parts * col_parts, rows // row_parts, cols // col_parts
    )


def from_blocks(blocks, row_parts, col_parts):
    count, block_rows, block_cols = blocks.shape
    layers = count // (row_parts * col_parts)
    shaped = blocks.reshape(layers, row_parts, col_parts, block_rows, block_cols)
    return shaped.transpose(0, 1, 3, 2, 4).reshape(
        layers, row_parts * block_rows, col_parts * block_cols
    )


def receptive_mask(lengths, sample_positions, dilation):
    ends = jnp.cumsum(lengths, axis=1)
    starts = jnp.sum(
        jnp.where(ends[:, None, :] <= sample_positions[None, :, None], lengths[:, None, :], 0),
        axis=2,
    )
    return sample_positions[None, :] - dilation >= starts


def gate_forward(units, input_weight, output_weight):
    pre = jnp.einsum("ptk,kg->ptg", units, input_weight, preferred_element_type=jnp.float32)
    half = pre.shape[2] // 2
    tanh_part = jnp.tanh(pre[..., :half])
    sigm_part = jax.nn.sigmoid(pre[..., half:])
    hidden = (tanh_part * sigm_part).astype(jnp.bfloat16)
    projected = jnp.einsum("ptg,gk->ptk", hidden, output_weight, preferred_element_type=jnp.float32)
    return (tanh_part, sigm_part, hidden, projected)


def gate_backward(
    units, tanh_part, sigm_part, hidden, input_weight, output_weight, grad_state, grad_skip
):
    grad_proj = jnp.concatenate([grad_state, grad_skip.astype(jnp.float32)], axis=2).astype(
        jnp.bfloat16
    )
    grad_wout = jnp.einsum("ptg,ptk->gk", hidden, grad_proj, preferred_element_type=jnp.float32)
    grad_hidden = jnp.einsum(
        "ptk,gk->ptg", grad_proj, output_weight, preferred_element_type=jnp.float32
    )
    grad_tanh = grad_hidden * sigm_part * (1.0 - tanh_part * tanh_part)
    grad_sigm = grad_hidden * tanh_part * sigm_part * (1.0 - sigm_part)
    grad_pre = jnp.concatenate([grad_tanh, grad_sigm], axis=2).astype(jnp.bfloat16)
    grad_win = jnp.einsum("ptk,ptg->kg", units, grad_pre, preferred_element_type=jnp.float32)
    grad_units = jnp.einsum(
        "ptg,kg->ptk", grad_pre, input_weight, preferred_element_type=jnp.float32
    )
    return (grad_win, grad_wout, grad_units)


def shampoo(grad, left, right, root_left, root_right, weight, rate):
    new_left = 0.5 * left + 0.5 * jnp.einsum("bij,bkj->bik", grad, grad, precision=highest)
    new_right = 0.5 * right + 0.5 * jnp.einsum("bji,bjk->bik", grad, grad, precision=highest)
    step = jnp.einsum("bij,bjk->bik", root_left, grad, precision=highest)
    step = jnp.einsum("bij,bjk->bik", step, root_right, precision=highest)
    return (new_left, new_right, weight - rate * step)


class Place:
    def __init__(self):
        self.row, self.seq = lax.axis_index("row"), lax.axis_index("seq")
        self.z, self.core = self.seq // 2, self.seq % 2
        x, y = self.row % 2, self.row // 2
        self.rows = (
            self.row,
            self.row + 1 - 2 * x,
            self.row + 2 - 4 * y,
            self.row + 3 - 2 * x - 4 * y,
        )
        self.x_peer = (self.rows[1], self.seq)
        self.y_peer = (self.rows[2], self.seq)
        self.sibling = (self.row, self.seq + 1 - 2 * self.core)
        self.near = self.mirrored(self.z)
        self.others = [self.mirrored(t) for t in (1 - self.near, 2, 3)]

    def mirrored(self, z):
        return z + self.z // 2 * (3 - 2 * z)

    def z_peer(self, z):
        return (self.row, 2 * z + self.core)

    def owner(self, rel, z, core=None):
        core = self.core if core is None else core
        return self.rows[rel] * 8 + 2 * z + core

    def announce(self):
        peers = [self.x_peer, self.y_peer, self.sibling] + [self.z_peer(z) for z in self.others]
        for peer in peers:
            pl.semaphore_signal(
                pltpu.get_barrier_semaphore(), inc=1, device_id=peer, device_id_type=MESH
            )

    def all_here(self):
        pl.semaphore_wait(pltpu.get_barrier_semaphore(), 6)


class Gather:
    def __init__(self, place, stack, count, sems):
        self.p, self.stack, self.count = place, stack, count
        self.send_sem, self.z_sems, self.x_sems, self.y_sems, self.s_sem = sems
        self.sent = 0

    def at(self, rel, z, half=None, core=None):
        start = self.p.owner(rel, z, core) * self.count
        if half is None:
            return self.stack.at[pl.ds(start, self.count)]
        part = self.count // 2
        return self.stack.at[pl.ds(start + half * part, part)]

    def copy(self, ref, sem, peer):
        return pltpu.make_async_remote_copy(
            src_ref=ref, dst_ref=ref, send_sem=self.send_sem.at[0], recv_sem=sem, device_id=peer, device_id_type=MESH
        )

    def send(self, ref, sem, peer):
        self.copy(ref, sem, peer).start()
        self.sent += 1

    def arrived(self, ref, sem, peer):
        self.copy(ref, sem, peer).wait_recv()

    def to_x(self, kind, rel, z, half):
        self.send(self.at(rel, z, half), self.x_sems.at[kind * 4 + z], self.p.x_peer)

    def to_y(self, kind, rel, z, half):
        self.send(self.at(rel, z, half), self.y_sems.at[kind * 4 + z], self.p.y_peer)

    def to_sibling(self, rel, z, half):
        self.send(self.at(rel, z, half), self.s_sem.at[0], self.p.sibling)

    def sides(self, z, half):
        if half == 0:
            self.to_x(0, 0, z, 0)
            self.to_y(1, 0, z, 0)
        else:
            self.to_y(0, 0, z, 1)
            self.to_x(1, 0, z, 1)
        self.to_sibling(0, z, half)

    def z_copy(self, src, quarter, z):
        part = self.count // 4
        ref = self.stack.at[pl.ds(self.p.owner(0, src) * self.count + quarter * part, part)]
        return self.copy(ref, self.z_sems.at[4 * src + quarter], self.p.z_peer(z))

    def z_passed(self, n, quarter):
        p = self.p
        outer, inner = p.mirrored(0), p.mirrored(2)
        near, far, farthest = p.others
        src, z = ((p.z, inner), (near, inner), (far, outer), (farthest, outer))[n]
        return self.z_copy(src, quarter, z)

    def pass_on(self, n, quarter):
        pl.when(self.p.near == 1)(lambda: self.z_passed(n, quarter).start())

    def start(self):
        p = self.p
        for quarter in range(4):
            self.z_copy(p.z, quarter, p.mirrored(1 - p.near)).start()
            self.pass_on(0, quarter)
        self.sent += 2

    def start_sides(self):
        for half in range(2):
            self.sides(self.p.z, half)

    def relay(self, n, half):
        z = self.p.others[n]
        for quarter in (2 * half, 2 * half + 1):
            self.z_copy(z, quarter, z).wait_recv()
            self.pass_on(n + 1, quarter)

    def spread(self, n, half):
        self.sides(self.p.others[n], half)

    def along_z(self, n):
        for half in range(2):
            self.relay(n, half)
            self.spread(n, half)

    def first(self, z):
        p = self.p
        self.arrived(self.at(1, z, 0), self.x_sems.at[z], p.x_peer)
        self.to_y(2, 1, z, 0)
        self.to_sibling(1, z, 0)
        self.arrived(self.at(2, z, 1), self.y_sems.at[z], p.y_peer)
        self.to_x(2, 2, z, 1)
        self.to_sibling(2, z, 1)

    def second(self, z):
        p = self.p
        self.arrived(self.at(1, z, 1), self.x_sems.at[4 + z], p.x_peer)
        self.to_sibling(1, z, 1)
        self.arrived(self.at(2, z, 0), self.y_sems.at[4 + z], p.y_peer)
        self.to_sibling(2, z, 0)

    def third(self, z):
        p = self.p
        self.arrived(self.at(3, z, 1), self.x_sems.at[8 + z], p.x_peer)
        self.to_sibling(3, z, 1)
        self.arrived(self.at(3, z, 0), self.y_sems.at[8 + z], p.y_peer)
        self.to_sibling(3, z, 0)

    def rest(self, z):
        self.second(z)
        self.third(z)

    def bytes_of(self, halves):
        return self.stack.at[pl.ds(0, halves * self.count // 2)]

    def finish(self):
        self.arrived(self.bytes_of(32), self.s_sem.at[0], self.p.sibling)
        self.copy(self.bytes_of(self.sent), self.s_sem.at[0], self.p.sibling).wait_send()

        @pl.when(self.p.near == 1)
        def _():
            self.copy(self.bytes_of(8), self.s_sem.at[0], self.p.sibling).wait_send()


GATHER_SEMS = [pltpu.SemaphoreType.DMA((n,)) for n in (1, 16, 12, 12, 1)]


def pick(which, zero, one):
    return jnp.where(jnp.full(zero.shape, which, i32) == 0, zero, one)


def assemble_in(inverse, stack, spread, weight, layer):
    def column(j, _):
        for i in range(16):
            q = inverse[layer, i * 8 + j]
            pair = stack[lax.div(q, 2)].astype(f32)
            spread[j, pl.ds(69 * i, 72), :] = pick(lax.rem(q, 2), pair[:72], pair[72:])
        weight[layer, :1104, pl.ds(pl.multiple_of(j * 128, 128), 128)] = spread[j, :1104, :].astype(bf16)
        return 0

    lax.fori_loop(0, 8, column, 0)


def across(top, bottom):
    left = lax.broadcasted_iota(i32, top.shape, 1) < 64
    return (
        jnp.where(left, top, pltpu.roll(bottom, 64, 1)),
        jnp.where(left, pltpu.roll(top, 64, 1), bottom),
    )


def assemble_out(inverse, stack, weight, layer):
    def line(i, _):
        for m in range(8):
            two = [stack[inverse[layer, i * 16 + 2 * m + h]].astype(f32) for h in range(2)]
            for k, rows in enumerate(across(*two)):
                first = pl.multiple_of(layer * 512 + i * 64 + 32 * k, 32)
                weight[pl.ds(first, 32), 128 * m : 128 * m + 128] = rows.astype(bf16)
        return 0

    lax.fori_loop(0, 8, line, 0)


VMEM = pl.BlockSpec(memory_space=pltpu.VMEM)
SMEM = pl.BlockSpec(memory_space=pltpu.SMEM)


class Reduce:
    def __init__(self, place, pack, rows, bufs, sems):
        self.p, self.pack, self.rows, self.half, self.pair = place, pack, rows, rows // 2, rows // 4
        (self.s_out, self.s_in, self.x1_out, self.x1_in, self.y1_out, self.y1_in,
         self.x2_out, self.x2_in, self.y2_out, self.y2_in, self.z_out, self.z_in) = bufs
        self.send_sem, self.s_sems, self.x1_sems, self.y1_sems, self.x2_sems, self.y2_sems, self.z_sems = sems
        self.sent = 0

    def rows_at(self, start, count):
        return pl.ds(pl.multiple_of(start, 16), count)

    def at(self, buf, start, count):
        ref, first = buf
        return ref.at[self.rows_at(first + start, count)]

    def put(self, buf, start, value):
        ref, first = buf
        ref[self.rows_at(first + start, self.pair), :] = value.astype(bf16)

    def read(self, buf, start):
        ref, first = buf
        return ref[self.rows_at(first + start, self.pair), :].astype(f32)

    def move(self, out, into, sems, index, count, peer):
        start = index * count
        return self.copy(self.at(out, start, count), self.at(into, start, count), sems.at[index], peer)

    def copy(self, src, dst, sem, peer):
        return pltpu.make_async_remote_copy(
            src_ref=src, dst_ref=dst, send_sem=self.send_sem.at[0], recv_sem=sem, device_id=peer, device_id_type=MESH
        )

    def sibling_copy(self, z):
        return self.move(self.s_out, self.s_in, self.s_sems, z, 4 * self.rows, self.p.sibling)

    def first_copies(self, z):
        return (
            self.move(self.x1_out, self.x1_in, self.x1_sems, z, 2 * self.half, self.p.x_peer),
            self.move(self.y1_out, self.y1_in, self.y1_sems, z, 2 * self.half, self.p.y_peer),
        )

    def second_copies(self, z):
        return (
            self.move(self.x2_out, self.x2_in, self.x2_sems, z, self.half, self.p.x_peer),
            self.move(self.y2_out, self.y2_in, self.y2_sems, z, self.half, self.p.y_peer),
        )

    def z_copy(self, src, dst, peer_z):
        return self.copy(
            self.at(self.z_out, dst * self.rows, self.rows), self.at(self.z_in, src * self.rows, self.rows),
            self.z_sems.at[src], self.p.z_peer(peer_z),
        )

    def to_sibling(self, z):
        p = self.p
        for rel in range(4):
            owner = p.owner(rel, z, 1 - p.core)

            def put(m, _, rel=rel, owner=owner):
                start = (z * 4 + rel) * self.rows + m * self.pair
                self.put(self.s_out, start, self.pack(owner, m))
                return 0

            lax.fori_loop(0, 4, put, 0)
        self.sibling_copy(z).start()

    def term(self, rel, z, half, m):
        start = (z * 4 + rel) * self.rows + half * self.half + m * self.pair
        return self.pack(self.p.owner(rel, z), half * 2 + m).astype(f32) + self.read(self.s_in, start)

    def first(self, z):
        self.sibling_copy(z).wait_recv()
        for out, half, rels in ((self.x1_out, 0, (1, 3)), (self.y1_out, 1, (2, 3))):
            for n, rel in enumerate(rels):

                def put(m, _, out=out, half=half, rel=rel, n=n):
                    start = (z * 2 + n) * self.half + m * self.pair
                    self.put(out, start, self.term(rel, z, half, m))
                    return 0

                lax.fori_loop(0, 2, put, 0)
        for copy in self.first_copies(z):
            copy.start()

    def second(self, z):
        for copy in self.first_copies(z):
            copy.wait_recv()
        for out, into, half, rel in ((self.y2_out, self.x1_in, 0, 2), (self.x2_out, self.y1_in, 1, 1)):

            def put(m, _, out=out, into=into, half=half, rel=rel):
                there = (z * 2 + 1) * self.half + m * self.pair
                total = self.term(rel, z, half, m) + self.read(into, there)
                self.put(out, z * self.half + m * self.pair, total)
                return 0

            lax.fori_loop(0, 2, put, 0)
        for copy in self.second_copies(z):
            copy.start()

    def column(self, z, half, m):
        first, second = ((self.x1_in, self.y2_in), (self.y1_in, self.x2_in))[half]
        return (
            self.term(0, z, half, m)
            + self.read(first, z * 2 * self.half + m * self.pair)
            + self.read(second, z * self.half + m * self.pair)
        )

    def third(self, z):
        for copy in self.second_copies(z):
            copy.wait_recv()
        for half in range(2):

            def put(m, _, half=half):
                start = z * self.rows + half * self.half + m * self.pair
                self.put(self.z_out, start, self.column(z, half, m))
                return 0

            lax.fori_loop(0, 2, put, 0)
        self.z_copy(self.p.z, z, z).start()

    def last(self, out):
        p = self.p
        for copy in self.second_copies(p.z):
            copy.wait_recv()
        for z in p.others:
            self.z_copy(z, p.z, z).wait_recv()
        for half in range(2):

            def put(m, _, half=half):
                total = self.column(p.z, half, m)
                start = half * self.half + m * self.pair
                for z in p.others:
                    total = total + self.read(self.z_in, z * self.rows + start)
                out[pl.ds(pl.multiple_of(start, 8), self.pair), :] = total
                return 0

            lax.fori_loop(0, 2, put, 0)

    def finish(self):
        whole = self.at((self.s_out[0], 0), 0, 31 * self.rows)
        self.copy(whole, whole, self.z_sems.at[0], self.p.sibling).wait_send()

    def events(self, out, steps):
        order = self.p.others[::-1] + [self.p.z]

        def event(step):
            kind, k = step
            if kind == "last":
                return lambda: self.last(out)
            return lambda: getattr(self, kind)(order[k])

        return [event(step) for step in steps]


def steps_of(*kinds):
    seen = {}
    for kind in kinds:
        seen[kind] = seen.get(kind, -1) + 1
        yield kind, seen[kind]


TO, ONE, TWO, THREE, LAST = "to_sibling", "first", "second", "third", "last"
REDUCE_ORDER = tuple(
    steps_of(TO, TO, ONE, TO, ONE, TO, TWO, ONE, TWO, THREE, TWO, ONE, THREE, THREE, TWO, LAST)
)
REDUCE_ORDER_OUT = tuple(
    steps_of(TO, TO, ONE, TO, ONE, TO, ONE, ONE, TWO, TWO, TWO, THREE, TWO, THREE, THREE, LAST)
)


REDUCE_COUNTS = (16, 4, 4, 2, 2, 4)
REDUCE_SEMS = [pltpu.SemaphoreType.DMA((n,)) for n in (1, 4, 4, 4, 4, 4, 4)]


def reduce_bufs(out, into, rows):
    bufs, first = [], 0
    for count in REDUCE_COUNTS:
        bufs += [(out, first), (into, first)]
        first += count * rows
    return bufs


def pack_in(owner, grad):
    def pack(device, m):
        halves = []
        for h in range(2):
            b = owner[device * 8 + m * 2 + h]
            layer, i, j = lax.div(b, 128), lax.div(lax.rem(b, 128), 8), lax.rem(b, 8)
            halves.append(grad[layer * 8 + j, pl.ds(69 * i, 72), :])
        return jnp.concatenate(halves, axis=0)

    return pack


def pack_out(owner, grad):
    def pack(device, m):
        return jnp.concatenate([grad[owner[device * 8 + m * 2 + h]] for h in range(2)], axis=0)

    return pack


def dot(a, b, ca, cb, precision=None):
    return lax.dot_general(
        a, b, (((ca,), (cb,)), ((), ())), precision=precision, preferred_element_type=f32
    )


def shampoo_block(grad, left, right, root_left, root_right, weight, rate):
    new_left = 0.5 * left + 0.5 * dot(grad, grad, 1, 1, highest)
    new_right = 0.5 * right + 0.5 * dot(grad, grad, 0, 0, highest)
    step = dot(dot(root_left, grad, 1, 0, highest), root_right, 1, 0, highest)
    return new_left, new_right, weight - rate * step


def dot(a, b, ca, cb, precision=None):
    return lax.dot_general(
        a, b, (((ca,), (cb,)), ((), ())), precision=precision, preferred_element_type=f32
    )


def tile(t, size=TILE):
    return pl.ds(pl.multiple_of(t * size, size), size)


def wide(mask):
    return jnp.concatenate([mask, mask], axis=1)


def gate_of(left, right):
    tau = jnp.tanh(left)
    sigma = 0.5 * jnp.tanh(0.5 * right) + 0.5
    hidden = tau * sigma
    return hidden, sigma - hidden * tau, hidden * (1.0 - sigma)


class Planes:
    def __init__(self, ref, samples, count):
        self.ref, self.samples, self.count = ref, samples, count

    def rows(self, plane, start, size):
        return pl.ds(pl.multiple_of(plane * self.samples + start, size), size)

    def get(self, t, planes, size=TILE):
        return jnp.concatenate([self.ref[self.rows(c, t * size, size), :] for c in planes], axis=1)

    def put(self, t, planes, value, size=TILE):
        for n, c in enumerate(planes):
            self.ref[self.rows(c, t * size, size), :] = value[:, 128 * n : 128 * n + 128]


class Layers:
    def __init__(self, refs, place):
        self.__dict__.update(refs)
        self.place = place
        self.samples = self.hidden.shape[0]
        self.tiles = self.samples // TILE
        self.gate = Planes(self.stack_in, self.samples, 8)
        self.early_at = 8 * self.samples


    def make_masks(self):
        def step(t, _):
            pos = self.place.seq * self.samples + t * TILE + lax.broadcasted_iota(i32, (TILE, 128), 0)
            end, start = 0, jnp.zeros((TILE, 128), i32)
            for k in range(self.lengths.shape[1]):
                end = end + self.lengths[0, k]
                start = start + jnp.where(end <= pos, self.lengths[0, k], 0)
            for ref, dilation in ((self.mask_long, FIRST_DILATION), (self.mask_short, 1)):
                ref[tile(t), :] = jnp.where(pos - dilation >= start, 1.0, 0.0).astype(bf16)
            return 0

        lax.fori_loop(0, self.tiles, step, 0)

    def make_inverse(self):
        block = lax.broadcasted_iota(i32, (2, 128), 0) * 128 + lax.broadcasted_iota(i32, (2, 128), 1)

        def step(q, found):
            return jnp.maximum(found, jnp.where(block == self.owner[q], q, 0))

        found = lax.fori_loop(0, 256, step, jnp.zeros((2, 128), i32), unroll=8)
        self.inverse_vmem[pl.ds(0, 2), :] = found
        copy = pltpu.make_async_copy(self.inverse_vmem, self.inverse, self.inverse_sem)
        copy.start()
        copy.wait()

    def make_condition(self):
        def step(t, _):
            lanes = tile(t)
            part = self.cond_t[:, lanes].astype(f32)
            padded = jnp.concatenate([part, jnp.zeros((128 - part.shape[0], TILE), f32)], axis=0)
            turned = padded.T.astype(bf16)
            self.units1[tile(t), 1024:] = turned
            self.units2[tile(t), 1024:] = turned
            return 0

        lax.fori_loop(0, self.tiles, step, 0)

    def make_delayed(self):
        def step(t, _):
            mask = self.mask_long[tile(t), :]
            for c in range(4):
                before = self.units1[tile(t - 1), 512 + 128 * c : 640 + 128 * c]
                self.units1[tile(t), 128 * c : 128 * c + 128] = before * mask
            return 0

        lax.fori_loop(1, self.tiles, step, 0)

    def make_first_delayed(self):
        mask = self.mask_long[pl.ds(0, TILE), :]
        for c in range(4):
            lanes = slice(128 * c, 128 * c + 128)
            self.units1[pl.ds(0, TILE), lanes] = self.halo_signal[:, lanes] * mask


    def forward_one(self, t):
        for c in range(2):
            left, right = self.halves(self.units1[tile(t), :], self.full_in[0], c)
            hidden, by_tanh, by_sigmoid = gate_of(left, right)
            self.hidden[tile(t), 256 * c : 256 * c + 256] = hidden.astype(bf16)
            self.gate.put(t, range(2 * c, 2 * c + 2), by_tanh.astype(bf16))
            self.gate.put(t, range(4 + 2 * c, 6 + 2 * c), by_sigmoid.astype(bf16))

    def halves(self, units, weight, c):
        return [dot(units, weight[:, first : first + 256], 1, 0) for first in (256 * c, 512 + 256 * c)]

    def state_one(self, t):
        mask = self.mask_short[tile(t), :].astype(f32)
        for c in range(2):
            lanes = slice(256 * c, 256 * c + 256)
            out = dot(self.hidden[tile(t), :512], self.full_out[:512, lanes], 1, 0)
            state = self.units1[tile(t), 512 + 256 * c : 768 + 256 * c].astype(f32) + out
            rounded = state.astype(bf16)
            self.units2[tile(t), 512 + 256 * c : 768 + 256 * c] = rounded
            delayed = pltpu.roll(rounded.astype(f32), 1, 0)
            self.last_rows[t, :, lanes] = delayed[:8]
            self.units2[tile(t), lanes] = (delayed * wide(mask)).astype(bf16)

    def mend_delayed(self, t):
        source = self.halo_state if t == 0 else self.last_rows.at[t - 1]
        first = lax.broadcasted_iota(i32, (16, 128), 0) == 0
        mask = self.mask_short[pl.ds(t * TILE, 16), :].astype(f32)
        rows = pl.ds(t * TILE, 16)
        for c in range(4):
            lanes = slice(128 * c, 128 * c + 128)
            row = jnp.broadcast_to(source[0:1, lanes], (16, 128)) * mask
            self.units2[rows, lanes] = jnp.where(first, row, self.units2[rows, lanes].astype(f32)).astype(bf16)

    def layer_two(self, t):
        for c in range(2):
            left, right = self.halves(self.units2[tile(t), :], self.full_in[1], c)
            hidden, by_tanh, by_sigmoid = gate_of(left, right)
            self.hidden[tile(t), 512 + 256 * c : 768 + 256 * c] = hidden.astype(bf16)
            gh = dot(self.go[tile(t), :], self.full_out[512 + 256 * c : 768 + 256 * c, :], 1, 1)
            self.gz[tile(t), 256 * c : 256 * c + 256] = (gh * by_tanh).astype(bf16)
            self.gz[tile(t), 512 + 256 * c : 768 + 256 * c] = (gh * by_sigmoid).astype(bf16)

    def units_two(self, t):
        mask = wide(self.mask_short[tile(t), :].astype(f32))
        last = lax.broadcasted_iota(i32, (TILE, 256), 0) == TILE - 1
        gz = self.gz[tile(t), :]
        for c in range(2):
            lanes = slice(256 * c, 256 * c + 256)
            early = dot(gz, self.full_in[1, lanes, :], 1, 1) * mask
            self.first_rows[t, :, lanes] = early[:8]
            moved = jnp.where(last, 0.0, pltpu.roll(early, TILE - 1, 0))
            here = dot(gz, self.full_in[1, 512 + 256 * c : 768 + 256 * c, :], 1, 1)
            self.gx[tile(t), lanes] = self.go[tile(t), lanes].astype(f32) + here + moved
        self.cond_grad[:, tile(t)] = self.condition_part(gz, 1)

    def condition_part(self, gz, layer):
        part = dot(gz, self.full_in[layer, 1024:, :], 1, 1).T
        return part[: self.cond_grad.shape[0], :]

    def mend_gx(self, t):
        source = self.halo_grad if t == self.tiles - 1 else self.first_rows.at[t + 1]
        last = lax.broadcasted_iota(i32, (8, 512), 0) == 7
        rows = pl.ds((t + 1) * TILE - 8, 8)
        row = jnp.broadcast_to(source[0:1, :], (8, 512))
        self.gx[rows, :] = self.gx[rows, :] + jnp.where(last, row, 0.0)

    def round_gx(self, t):
        self.go[tile(t), :512] = self.gx[tile(t), :].astype(bf16)

    def layer_one_back(self, t):
        for c in range(2):
            gh = dot(self.go[tile(t), :], self.full_out[256 * c : 256 * c + 256, :], 1, 1)
            for part in range(2):
                gate = self.gate.get(t, range(4 * part + 2 * c, 4 * part + 2 * c + 2)).astype(f32)
                first = 512 * part + 256 * c
                self.gz[tile(t), first : first + 256] = (gh * gate).astype(bf16)


    def weight_out(self, layer):
        def step(m, _):
            lanes = pl.ds(pl.multiple_of(layer * 512 + m * 256, 256), 256)
            grad = dot(self.hidden[:, lanes], self.go[...], 0, 0)
            for i in range(4):
                for j in range(8):
                    pair = grad[64 * i : 64 * i + 64, 128 * j : 128 * j + 128]
                    first = layer * 128 + (m * 4 + i) * 16 + 2 * j
                    for k, block in enumerate(across(pair[:32], pair[32:])):
                        self.grad_out[first + k] = block.astype(bf16)
            return 0

        lax.fori_loop(0, 2, step, 0)

    def weight_in(self, layer, units, m):
        rows = pl.ds(pl.multiple_of(384 * m, 384), 384)
        grad = dot(units[:, rows], self.gz[...], 0, 0)
        for j in range(8):
            self.grad_in[layer * 8 + j, rows, :] = grad[:, 128 * j : 128 * j + 128]


    def early_units_one(self):
        mask = wide(self.mask_long[pl.ds(0, TILE), :].astype(f32))
        for c in range(2):
            lanes = slice(256 * c, 256 * c + 256)
            early = dot(self.gz[pl.ds(0, TILE), :], self.full_in[0, lanes, :], 1, 1) * mask
            for k in range(2):
                rows = pl.ds(self.early_at + TILE * (2 * c + k), TILE)
                self.stack_in[rows, :] = early[:, 128 * k : 128 * k + 128].astype(bf16)

    def units_one(self, t):
        gz = self.gz[tile(t), :]
        mask = wide(self.mask_long[tile(t), :].astype(f32))
        for c in range(2):
            lanes = slice(256 * c, 256 * c + 256)
            if t > 0:
                early = dot(gz, self.full_in[0, lanes, :], 1, 1)
                self.gx[tile(t - 1), lanes] = self.gx[tile(t - 1), lanes] + early * mask
            here = dot(gz, self.full_in[0, 512 + 256 * c : 768 + 256 * c, :], 1, 1)
            self.gx[tile(t), lanes] = self.gx[tile(t), lanes] + here
        self.cond_grad[:, tile(t)] = self.cond_grad[:, tile(t)] + self.condition_part(gz, 0)

    def put_out(self, src, dst, sem):
        copy = pltpu.make_async_copy(src, dst, sem)
        copy.start()
        self.pending.append(copy)

    def send_gx(self, t):
        self.units2[tile(t), :512] = self.gx[tile(t), :].astype(bf16)
        self.put_out(self.units2.at[tile(t), pl.ds(0, 512)], self.grad_x.at[tile(t)], self.gx_sems.at[t])

    def outputs(self, n):
        rows = tile(n, 256)
        for c in range(4):
            lanes = slice(256 * c, 256 * c + 256)
            out = dot(self.hidden[rows, :], self.full_out[:, lanes], 1, 0)
            if c < 2:
                out = out + self.units1[rows, 512 + 256 * c : 768 + 256 * c].astype(f32)
            self.go[rows, lanes] = out.astype(bf16)
        self.output_copy(n).start()

    def output_copy(self, n):
        rows = tile(n, 256)
        return pltpu.make_async_copy(self.go.at[rows], self.both.at[rows], self.stage_sems.at[n])

    def drain(self, copies):
        for copy in copies:
            copy.wait()

    def end_gx(self, near, early_halo):
        t = self.tiles - 1
        near.arrived(*early_halo)
        for c in range(4):
            lanes = slice(128 * c, 128 * c + 128)
            late = self.halo_early[pl.ds(TILE * c, TILE), :].astype(f32)
            self.gx[tile(t), lanes] = self.gx[tile(t), lanes] + late
        self.send_gx(t)

    def tail(self, near, early_halo, small, rest_out):
        work = {}
        work[TO, 3] = [self.early_units_one, lambda: near.start(*early_halo), lambda: self.units_one(0)]
        work[ONE, 2] = [lambda: self.units_one(1), lambda: self.send_gx(0)]
        work[TWO, 1] = [lambda: near.sent(*early_halo)]
        work[THREE, 0] = [lambda: self.units_one(2), lambda: self.send_gx(1), lambda: self.outputs(0)]
        work[ONE, 3] = [lambda: self.outputs(1)]
        work[THREE, 1] = [lambda: self.outputs(2), *rest_out, lambda: small[1].start()]
        work[THREE, 2] = [
            lambda: self.units_one(3),
            lambda: self.send_gx(2),
            lambda: self.end_gx(near, early_halo),
            lambda: small[0].start(),
        ]
        work[TWO, 3] = [lambda: loop(3, self.samples // 256, self.outputs)]
        return [work.get(step, []) for step in REDUCE_ORDER]


def loop(first, last, body, unroll=1):
    lax.fori_loop(first, last, lambda t, _: (body(t), 0)[1], 0, unroll=unroll)


class Neighbours:
    def __init__(self, place):
        self.p = place
        self.has = {1: place.seq < 7, -1: place.seq > 0}

    def copy(self, src, dst, sems, way):
        return pltpu.make_async_remote_copy(
            src_ref=src, dst_ref=dst, send_sem=sems[0], recv_sem=sems[1],
            device_id=(self.p.row, self.p.seq + way), device_id_type=MESH)

    def start(self, src, dst, sems, way):
        pl.when(self.has[way])(lambda: self.copy(src, dst, sems, way).start())

    def sent(self, src, dst, sems, way):
        pl.when(self.has[way])(lambda: self.copy(src, dst, sems, way).wait_send())

    def arrived(self, src, dst, sems, way):
        pl.when(self.has[-way])(lambda: self.copy(src, dst, sems, way).wait_recv())


INPUTS = ("owner", "lengths", "signal", "cot_x", "cot_skip", "from_cond", "from_w_in", "from_w_out")
OUTPUTS = ("both", "grad_x", "grad_cond_t", "sum_in", "sum_out")
SCRATCH = dict(
    stack_in=pltpu.VMEM((32 * ROWS_IN, 128), bf16),
    stack_out=pltpu.VMEM((32 * ROWS_OUT, 128), bf16),
    full_in=pltpu.VMEM((2, 1152, 1024), bf16),
    full_out=pltpu.VMEM((1024, 1024), bf16),
    units1=pltpu.VMEM((2048, 1152), bf16),
    units2=pltpu.VMEM((2048, 1152), bf16),
    hidden=pltpu.VMEM((2048, 1024), bf16),
    gz=pltpu.VMEM((2048, 1024), bf16),
    go=pltpu.VMEM((2048, 1024), bf16),
    gx=pltpu.VMEM((2048, 512), f32),
    grad_in=pltpu.VMEM((16, 1152, 128), f32),
    grad_out=pltpu.VMEM((256, 32, 128), bf16),
    mask_long=pltpu.VMEM((2048, 128), bf16),
    mask_short=pltpu.VMEM((2048, 128), bf16),
    halo_signal=pltpu.VMEM((TILE, 512), bf16),
    halo_early=pltpu.VMEM((4 * TILE, 128), bf16),
    last_rows=pltpu.VMEM((4, 8, 512), f32),
    first_rows=pltpu.VMEM((4, 8, 512), f32),
    halo_state=pltpu.VMEM((8, 512), f32),
    halo_grad=pltpu.VMEM((8, 512), f32),
    reduce_in=pltpu.VMEM((32 * ROWS_IN, 128), bf16),
    reduce_out=pltpu.VMEM((32 * ROWS_OUT, 128), bf16),
    cond_t=pltpu.VMEM((80, 2048), bf16),
    w_in=pltpu.VMEM((552, 128), f32),
    w_out=pltpu.VMEM((8, 64, 64), f32),
    cond_grad=pltpu.VMEM((80, 2048), f32),
    share_in=pltpu.VMEM((ROWS_IN, 128), f32),
    share_out=pltpu.VMEM((ROWS_OUT, 128), f32),
    small_sems=pltpu.SemaphoreType.DMA((3,)),
    inverse_vmem=pltpu.VMEM((8, 128), i32),
    inverse=pltpu.SMEM((8, 128), i32),
    inverse_sem=pltpu.SemaphoreType.DMA,
    load_sems=pltpu.SemaphoreType.DMA((6,)),
    gx_sems=pltpu.SemaphoreType.DMA((4,)),
    stage_sems=pltpu.SemaphoreType.DMA((8,)),
    halo_sems=pltpu.SemaphoreType.DMA((8,)),
)


def network_kernel(*refs):
    names = INPUTS + OUTPUTS + tuple(SCRATCH)
    sems = refs[len(names) :]
    gather_sems, reduce_sems = len(GATHER_SEMS), len(REDUCE_SEMS)
    sems_in, sems = sems[:gather_sems], sems[gather_sems:]
    sems_out, sems = sems[:gather_sems], sems[gather_sems:]
    sum_sems_out, sum_sems_in = sems[:reduce_sems], sems[reduce_sems:]
    place = Place()
    n = Layers(dict(zip(names, refs)), place)
    n.pending = []
    near = Neighbours(place)
    samples, tiles = n.samples, n.tiles

    place.announce()
    targets = ((n.signal, n.units1, 512), (n.cot_x, n.go, 0), (n.cot_skip, n.go, 512))
    early = [
        pltpu.make_async_copy(src, dst, n.load_sems.at[k])
        for k, (src, dst) in enumerate(
            ((n.from_w_in, n.w_in), (n.from_w_out, n.w_out), (n.from_cond, n.cond_t))
        )
    ]
    loads = [
        pltpu.make_async_copy(src, dst.at[:, pl.ds(lane, 512)], n.load_sems.at[3 + k])
        for k, (src, dst, lane) in enumerate(targets)
    ]
    for copy in early + loads:
        copy.start()
    me = place.row * 8 + place.seq
    pairs_in, blocks_out = n.stack_in.reshape(128, 144, 128), n.stack_out.reshape(256, 32, 128)
    spread = n.grad_in
    early[0].wait()
    spread[0, :ROWS_IN, :] = jnp.zeros((ROWS_IN, 128), f32)
    spread[1, : 8 * 69, :] = n.w_in[...]
    for k in range(8):
        spread[0, pl.ds(72 * k, 69), :] = spread[1, pl.ds(k, 72, 8), :][:69]
    for m in range(4):
        pairs_in[me * 4 + m] = spread[0, 144 * m : 144 * m + 144, :].astype(bf16)

    early[1].wait()
    for k in range(8):
        block = n.w_out[k]
        blocks_out[me * 8 + k] = jnp.concatenate([block[:32], block[32:]], axis=1).astype(bf16)

    def cleared(refs, when):
        @pl.when(when)
        def _():
            for ref in refs:
                ref[...] = jnp.zeros_like(ref)

    cleared([n.halo_signal, n.halo_state], place.seq == 0)
    cleared([n.halo_early, n.halo_grad], place.seq == 7)
    place.all_here()

    halo = [(n.halo_sems.at[2 * k], n.halo_sems.at[2 * k + 1]) for k in range(4)]
    signal_halo = (n.signal.at[pl.ds(samples - TILE, TILE)], n.halo_signal, halo[0], 1)
    state_halo = (n.last_rows.at[tiles - 1], n.halo_state, halo[1], 1)
    grad_halo = (n.first_rows.at[0], n.halo_grad, halo[2], -1)
    early_halo = (n.stack_in.at[pl.ds(n.early_at, 4 * TILE)], n.halo_early, halo[3], -1)
    into = Gather(place, pairs_in, 4, sems_in)
    out = Gather(place, blocks_out, 8, sems_out)
    order = [place.z] + place.others
    into.start()
    into.start_sides()
    out.start()

    def make_rest():
        early[2].wait()
        n.make_condition()
        n.full_in[0, 1104:, :] = jnp.zeros((48, 1024), bf16)
        n.full_in[1, 1104:, :] = jnp.zeros((48, 1024), bf16)

    n.make_masks()
    n.make_inverse()
    into.along_z(0)
    into.along_z(1)
    make_rest()
    into.first(order[0])
    into.along_z(2)
    into.first(order[1])
    for k in range(3):
        out.relay(k, 0)
        out.relay(k, 1)
    into.first(order[2])
    into.rest(order[0])
    into.first(order[3])
    near.start(*signal_halo)
    for copy in loads:
        copy.wait()
    n.make_delayed()
    for k in range(1, tiles):
        into.rest(order[k])
    out.start_sides()
    for k in range(3):
        out.spread(k, 0)
        out.spread(k, 1)
    into.finish()
    assemble_in(n.inverse, pairs_in, spread, n.full_in, 0)
    assemble_in(n.inverse, pairs_in, spread, n.full_in, 1)

    near.arrived(*signal_halo)
    n.make_first_delayed()
    out.first(order[0])
    out.first(order[1])
    loop(0, 2, n.forward_one)
    out.first(order[2])
    out.first(order[3])
    out.rest(order[0])
    out.rest(order[1])
    loop(2, tiles, n.forward_one)
    out.rest(order[2])
    out.rest(order[3])
    out.finish()
    assemble_out(n.inverse, blocks_out, n.full_out, 0)
    assemble_out(n.inverse, blocks_out, n.full_out, 1)
    n.state_one(tiles - 1)
    near.start(*state_halo)
    loop(0, tiles - 1, n.state_one, 3)
    for t in range(1, tiles):
        n.mend_delayed(t)
    near.arrived(*state_halo)
    n.mend_delayed(0)

    loop(0, tiles, n.layer_two, 2)
    n.units_two(0)
    near.start(*grad_halo)
    loop(1, tiles, n.units_two)
    n.weight_out(1)
    for t in range(tiles - 1):
        n.mend_gx(t)
    near.arrived(*grad_halo)
    n.mend_gx(tiles - 1)
    loop(0, tiles, n.round_gx)
    n.weight_out(0)

    reduce_out = Reduce(
        place, pack_out(n.owner, n.grad_out), ROWS_OUT,
        reduce_bufs(n.stack_out, n.reduce_out, ROWS_OUT), sum_sems_out,
    )
    reduce_in = Reduce(
        place, pack_in(n.owner, n.grad_in), ROWS_IN,
        reduce_bufs(n.stack_in, n.reduce_in, ROWS_IN), sum_sems_in,
    )
    sum_out = reduce_out.events(n.share_out, REDUCE_ORDER_OUT)
    sum_in = reduce_in.events(n.share_in, REDUCE_ORDER)

    def run(*events):
        for event in events:
            event()

    small = [
        pltpu.make_async_copy(a, b, n.small_sems.at[k])
        for k, (a, b) in enumerate(
            ((n.cond_grad, n.grad_cond_t), (n.share_out, n.sum_out), (n.share_in, n.sum_in))
        )
    ]
    run(*sum_out[:2])
    n.weight_in(1, n.units2, 0)
    run(*sum_out[2:6])
    n.weight_in(1, n.units2, 1)
    run(*sum_out[6:8])
    n.weight_in(1, n.units2, 2)
    run(*sum_out[8:10])
    loop(0, 2, n.layer_one_back, 2)
    run(sum_out[10])
    loop(2, tiles, n.layer_one_back, 2)
    run(*sum_out[11:13])
    n.weight_in(0, n.units1, 0)
    run(*sum_out[13:15])
    n.weight_in(0, n.units1, 1)
    n.weight_in(0, n.units1, 2)
    for event, work in zip(sum_in, n.tail(near, early_halo, small, [sum_out[15], reduce_out.finish])):
        event()
        for part in work:
            part()
    reduce_in.finish()
    small[2].start()
    for halo in (signal_halo, state_halo, grad_halo):
        near.sent(*halo)
    n.drain(n.pending)
    loop(0, samples // 256, lambda k: n.output_copy(k).wait())
    n.drain(small)


ANY = pl.BlockSpec(memory_space=pl.ANY)


def shampoo_block(grad, left, right, root_left, root_right, weight, rate):
    low = grad.astype(bf16)
    new_left = 0.5 * left + 0.5 * dot(low, low, 1, 1)
    new_right = 0.5 * right + 0.5 * dot(low, low, 0, 0)
    step = dot(dot(root_left.astype(bf16), low, 1, 0).astype(bf16), root_right.astype(bf16), 1, 0)
    return new_left, new_right, weight - rate * step


BLOCKS_IN = ("w_in", "left_in", "root_left_in", "right_in", "root_right_in")
BLOCKS_OUT = ("w_out", "left_out", "root_left_out", "right_out", "root_right_out")
SUMS = ("sum_in", "sum_out")
LARGE = ("out_x", "skip_sum", "grad_x")
LOW = ("both", "grad_x")


def finish_kernel(*refs):
    taken = SUMS + BLOCKS_IN + BLOCKS_OUT
    names = ["from_" + a for a in taken + LOW + ("cond",)]
    names += ["to_" + a for a in LARGE + ("cond", "grad_in", "grad_out")]
    names += ["to_" + a for kind in ("in", "out") for a in ("w_" + kind, "left_" + kind, "right_" + kind)]
    names += list(taken) + ["grad_in", "grad_out", "large", "both", "low", "cond", "load_sems", "store_sems"]
    r = dict(zip(names, refs))
    loads, stores, sems = {}, {}, iter(range(64))

    def move(table, key, src, dst, sem):
        table[key] = pltpu.make_async_copy(src, dst, r[sem].at[next(sems)])

    for a in taken:
        there = r[a].at[pl.ds(0, 552)] if a in BLOCKS_IN[:3] else r[a]
        move(loads, a, r["from_" + a], there, "load_sems")
    for m in range(4):
        move(loads, ("both", m), r["from_both"].at[tile(m)], r["both"].at[tile(m)], "load_sems")
        move(loads, ("low", m), r["from_grad_x"].at[tile(m)], r["low"].at[tile(m)], "load_sems")
    move(loads, "cond", r["from_cond"], r["cond"], "load_sems")
    sems = iter(range(64))
    for m in range(4):
        for k in range(3):
            move(stores, (k, m), r["large"].at[k, tile(m)], r["to_" + LARGE[k]].at[tile(m)], "store_sems")
    for a in ("cond", "grad_in", "w_in", "left_in", "right_in", "grad_out", "w_out", "left_out", "right_out"):
        here = r[a].at[pl.ds(0, 552)] if a in ("grad_in", "w_in", "left_in") else r[a]
        move(stores, a, here, r["to_" + a], "store_sems")
    for copy in loads.values():
        copy.start()

    def widen(m, name):
        loads[name, m].wait()
        for k in (0, 1) if name == "both" else (2,):
            lanes = slice(512 * (k % 2), 512 * (k % 2) + 512)
            r["large"][k, tile(m), :] = r[name][tile(m), lanes].astype(f32)
            stores[k, m].start()

    for a in taken:
        loads[a].wait()
    for k in range(8):
        at, put = pl.ds(k, 72, 8), pl.ds(k, 69, 8)
        grad = r["sum_in"][72 * k : 72 * k + 72, :]
        r["grad_in"][at, :] = grad
        r["left_in"][put, :], r["right_in"][k], r["w_in"][put, :] = shampoo_block(
            grad[:69], r["left_in"][at, :][:69], r["right_in"][k], r["root_left_in"][at, :][:69],
            r["root_right_in"][k], r["w_in"][at, :][:69], rate_in,
        )
        folded = r["sum_out"][32 * k : 32 * k + 32, :]
        grad = jnp.concatenate([folded[:, :64], folded[:, 64:]], axis=0)
        r["grad_out"][k] = grad
        r["left_out"][k], r["right_out"][k], r["w_out"][k] = shampoo_block(
            grad, r["left_out"][k], r["right_out"][k], r["root_left_out"][k], r["root_right_out"][k],
            r["w_out"][k], rate_out,
        )
        if k % 2:
            widen(k // 2, "both")
            widen(k // 2, "low")
    loads["cond"].wait()
    for a in ("cond", "grad_in", "w_in", "left_in", "right_in"):
        stores[a].start()
    for a in ("grad_out", "w_out", "left_out", "right_out"):
        stores[a].start()
    for copy in stores.values():
        copy.wait()


def rows_first(blocks):
    return blocks.transpose(1, 0, 2)


def fused_local(
    signal, condition, lengths, owner, grad_out, grad_skip, w_in, w_out,
    left_in, right_in, root_left_in, root_right_in,
    left_out, right_out, root_left_out, root_right_out,
):
    samples, width, mels = signal.shape[1], signal.shape[2], condition.shape[2]
    block = lambda *shape: jax.ShapeDtypeStruct(shape, f32)
    low = [jax.ShapeDtypeStruct((samples, lanes), bf16) for lanes in (2 * width, width)]
    large = [block(samples, width)] * 3 + [block(mels, samples)]
    rows_in = rows_first(w_in).reshape(552, 128)
    both, grad_x, grad_cond_t, sum_in, sum_out = pl.pallas_call(
        network_kernel,
        out_shape=low + [block(mels, samples), block(ROWS_IN, 128), block(ROWS_OUT, 128)],
        in_specs=[SMEM, SMEM] + [ANY] * 6,
        out_specs=[ANY] * 5,
        scratch_shapes=list(SCRATCH.values()) + GATHER_SEMS * 2 + REDUCE_SEMS * 2,
        name="network",
        compiler_params=pltpu.CompilerParams(
            collective_id=0, has_side_effects=True, vmem_limit_bytes=64 << 20
        ),
    )(
        owner, lengths, signal[0], grad_out[0], grad_skip[0], condition[0].T, rows_in, w_out,
    )
    taken = (
        sum_in, sum_out,
        rows_in, rows_first(left_in).reshape(552, 69), rows_first(root_left_in).reshape(552, 69),
        right_in, root_right_in,
        w_out, left_out, root_left_out, right_out, root_right_out,
    )
    new_in = [block(552, 128), block(552, 69), block(8, 128, 128)]
    new_out = [block(8, 64, 64)] * 3
    held = [pltpu.VMEM((584 if a.shape[0] == 552 else a.shape[0], *a.shape[1:]), f32) for a in taken]
    outs = pl.pallas_call(
        finish_kernel,
        out_shape=large + [new_in[0], new_out[0]] + new_in + new_out,
        in_specs=[ANY] * (len(taken) + 3),
        out_specs=[ANY] * 12,
        scratch_shapes=held
        + [pltpu.VMEM((584, 128), f32), pltpu.VMEM((8, 64, 64), f32)]
        + [pltpu.VMEM((3, samples, width), f32)]
        + [pltpu.VMEM(a.shape, a.dtype) for a in low + [block(mels, samples)]]
        + [pltpu.SemaphoreType.DMA((32,))] * 2,
        name="finish",
        compiler_params=pltpu.CompilerParams(vmem_limit_bytes=63 << 20),
    )(*taken, both, grad_x, grad_cond_t)
    out_x, skip_sum, grad_x, grad_cond_t, g_in, g_out, nw_in, nl_in, nr_in, nw_out, nl_out, nr_out = outs

    def blocks_first(rows):
        return rows.reshape(69, 8, rows.shape[1]).transpose(1, 0, 2)

    return (
        out_x[None], skip_sum[None], grad_x[None], grad_cond_t.T[None],
        blocks_first(g_in), g_out, blocks_first(nl_in), nr_in, nl_out, nr_out, blocks_first(nw_in), nw_out,
    )


def local(
    signal,
    condition,
    lengths,
    owner,
    grad_out,
    grad_skip,
    w_in,
    w_out,
    left_in,
    right_in,
    root_left_in,
    root_right_in,
    left_out,
    right_out,
    root_left_out,
    root_right_out,
):
    fused = (lax.axis_size("row"), lax.axis_size("seq"), signal.shape[1]) == (4, 8, 4 * TILE)
    audio_samples = signal.shape[1]
    width = signal.shape[2]
    if fused:
        return fused_local(
            signal, condition, lengths, owner, grad_out, grad_skip, w_in, w_out,
            left_in, right_in, root_left_in, root_right_in,
            left_out, right_out, root_left_out, root_right_out,
        )
    stack_in = lax.all_gather(w_in.astype(bf16), ("row", "seq"), axis=0, tiled=True)
    stack_out = lax.all_gather(w_out.astype(bf16), ("row", "seq"), axis=0, tiled=True)
    inverse = jnp.argsort(owner)
    input_weight = from_blocks(jnp.take(stack_in, inverse, axis=0), 16, 8)
    output_weight = from_blocks(jnp.take(stack_out, inverse, axis=0), 8, 16)
    sample_positions = lax.axis_index("seq") * audio_samples + jnp.arange(
        audio_samples, dtype=jnp.int32
    )
    longer_mask = receptive_mask(lengths, sample_positions, FIRST_DILATION)[:, :, None]
    mask_short = receptive_mask(lengths, sample_positions, 1)[:, :, None]
    preceding_longer = shifted(signal[:, audio_samples - FIRST_DILATION :, :], "seq", 1)
    delayed_one = jnp.concatenate([preceding_longer, signal], axis=1)[:, :audio_samples, :]
    delayed_one = jnp.where(longer_mask, delayed_one, jnp.zeros_like(delayed_one))
    units_one = jnp.concatenate([delayed_one, signal, condition], axis=2)
    tanh_one, sigm_one, hidden_one, proj_one = gate_forward(
        units_one, input_weight[0], output_weight[0]
    )
    first_layer_state = signal.astype(jnp.float32) + proj_one[..., :width]
    rounded_one = first_layer_state.astype(jnp.bfloat16)
    before_short = shifted(rounded_one[:, audio_samples - 1 :, :], "seq", 1)
    delayed_two = jnp.concatenate([before_short, rounded_one[:, : audio_samples - 1, :]], axis=1)
    delayed_two = jnp.where(mask_short, delayed_two, jnp.zeros_like(delayed_two))
    units_two = jnp.concatenate([delayed_two, rounded_one, condition], axis=2)
    tanh_two, sigm_two, hidden_two, proj_two = gate_forward(
        units_two, input_weight[1], output_weight[1]
    )
    out_x = first_layer_state + proj_two[..., :width]
    skip_sum = proj_one[..., width:] + proj_two[..., width:]
    grad_next = grad_out.astype(jnp.float32)
    gin_two, gout_two, units_grad_two = gate_backward(
        units_two,
        tanh_two,
        sigm_two,
        hidden_two,
        input_weight[1],
        output_weight[1],
        grad_next,
        grad_skip,
    )
    early_two = jnp.where(mask_short, units_grad_two[..., :width], 0.0)
    from_short = shifted(early_two[:, :1, :], "seq", -1)
    grad_state = (
        grad_next
        + units_grad_two[..., width : 2 * width]
        + jnp.concatenate([early_two[:, 1:, :], from_short], axis=1)
    )
    gin_one, gout_one, units_grad_one = gate_backward(
        units_one,
        tanh_one,
        sigm_one,
        hidden_one,
        input_weight[0],
        output_weight[0],
        grad_state,
        grad_skip,
    )
    earlier_first = jnp.where(longer_mask, units_grad_one[..., :width], 0.0)
    taken_longer = shifted(earlier_first[:, :FIRST_DILATION, :], "seq", -1)
    grad_x = (
        grad_state
        + units_grad_one[..., width : 2 * width]
        + jnp.concatenate([earlier_first[:, FIRST_DILATION:, :], taken_longer], axis=1)
    )
    grad_cond = units_grad_one[..., 2 * width :] + units_grad_two[..., 2 * width :]
    local_in = jnp.take(to_blocks(jnp.stack([gin_one, gin_two]), 16, 8), owner, axis=0)
    local_out = jnp.take(to_blocks(jnp.stack([gout_one, gout_two]), 8, 16), owner, axis=0)
    grad_in_blocks, grad_out_blocks = (
        lax.psum_scatter(local_in, ("row", "seq"), scatter_dimension=0, tiled=True),
        lax.psum_scatter(local_out, ("row", "seq"), scatter_dimension=0, tiled=True),
    )
    new_left_in, new_right_in, new_w_in = shampoo(
        grad_in_blocks, left_in, right_in, root_left_in, root_right_in, w_in, rate_in
    )
    new_left_out, new_right_out, new_w_out = shampoo(
        grad_out_blocks, left_out, right_out, root_left_out, root_right_out, w_out, rate_out
    )
    return (
        out_x,
        skip_sum,
        grad_x,
        grad_cond,
        grad_in_blocks,
        grad_out_blocks,
        new_left_in,
        new_right_in,
        new_left_out,
        new_right_out,
        new_w_in,
        new_w_out,
    )


def solution(mesh):
    tokens, blocks = P("row", "seq", None), P(("row", "seq"), None, None)
    in_specs = (tokens, tokens, P("row", None), P(), tokens, tokens) + (blocks,) * 10
    out_specs = (tokens,) * 4 + (blocks,) * 8
    return jax.shard_map(local, mesh=mesh, in_specs=in_specs, out_specs=out_specs, check_vma=False)
```
